32 devices in a mesh: dp: 16 (over z, y, x), chan: 2 (over core).
Axes of the slice: x: 2, y: 2, z: 4, core: 2. Of those that a mesh axis runs over, the one named last changes fastest.
Arguments:
- crops_in: bfloat16 [3, 256, 49, 2048], P(None, 'dp', None, 'chan'), may hold values from -6 to 6
- stem_weight: bfloat16 [2048, 512], P(None, 'chan'), may hold values from -0.125 to 0.125
- middle_weight: bfloat16 [9, 512, 512], P(None, None, 'chan'), may hold values from -0.09375 to 0.09375
- expand_weight: bfloat16 [512, 2048], P('chan'), may hold values from -0.25 to 0.25
- stem_gain: float32 [512], P('chan'), may hold values from 0.5 to 1.5
- stem_bias: float32 [512], P('chan'), may hold values from -1.5 to 1.5
- middle_gain: float32 [512], P('chan'), may hold values from 0.5 to 1.5
- middle_bias: float32 [512], P('chan'), may hold values from -1.5 to 1.5
- expand_gain: float32 [2048], P('chan'), may hold values from 0.5 to 1.5
- expand_bias: float32 [2048], P('chan'), may hold values from -1.5 to 1.5
- hidden_weight: bfloat16 [2048, 1024], P(None, 'chan'), may hold values from -0.125 to 0.125
- hidden_gain: float32 [1024], P('chan'), may hold values from 0.5 to 1.5
- hidden_bias: float32 [1024], P('chan'), may hold values from -1.5 to 1.5
- embed_weight: bfloat16 [1024, 128], P('chan'), may hold values from -0.375 to 0.375
- sub_sizes: int32 [3, 4], replicated, may hold values from 32 to 96, as said below
- crop_order: int32 [3, 256], replicated, may hold values from 0 to 255, each once within a row
- pair_index: int32 [3, 128, 2], replicated, may hold values from 0 to 255
Outputs:
- loss_mean: float32 [], replicated
- grad_crops: float32 [3, 256, 49, 2048], P(None, 'dp', None, 'chan')
- grad_stem_weight: float32 [2048, 512], P(None, 'chan')
- grad_middle_weight: float32 [9, 512, 512], P(None, None, 'chan')
- grad_expand_weight: float32 [512, 2048], P('chan')
- grad_stem_gain: float32 [512], P('chan')
- grad_stem_bias: float32 [512], P('chan')
- grad_middle_gain: float32 [512], P('chan')
- grad_middle_bias: float32 [512], P('chan')
- grad_expand_gain: float32 [2048], P('chan')
- grad_expand_bias: float32 [2048], P('chan')
- grad_hidden_weight: float32 [2048, 1024], P(None, 'chan')
- grad_hidden_gain: float32 [1024], P('chan')
- grad_hidden_bias: float32 [1024], P('chan')
- grad_embed_weight: float32 [1024, 128], P('chan')
The draws below stay inside these ranges and needn't reach their ends.
Inputs may be any that keep to these rules, and one draw needn't show every extreme that they name: `sub_sizes`: each row sums to 256. `crop_order`: each row is a permutation of the crops of one micro-batch. `pair_index`: crop indices within one micro-batch.
All inputs are finite; a program needn't handle non-finite values.
Results may differ from the reference program's by a relative error of at most 0.025.
Values may be sent and summed in bfloat16 or wider, within the bound.
A program may use at most 256 MiB of HBM per device.

```python
import jax
import jax.numpy as jnp
from jax import lax

CIN = 2048
MID = 512
PH = 1024
PO = 128
SIDE = 7
MB = 3
SUBS = 4
CROPS_MB = 256
SUB_AVG = 64
PAIRS = 128


def draw_crops_in(key, part):
    key = jax.random.fold_in(key, 23)
    crop_key, pixel_key = jax.random.split(key)
    crop_term = jax.random.normal(crop_key, (MB, CROPS_MB, 1, CIN), jnp.float32)
    pixel_term = jax.random.normal(pixel_key, (MB, CROPS_MB, SIDE * SIDE, CIN), jnp.float32)
    values = jnp.clip(0.8 * crop_term + 0.6 * pixel_term, -6.0, 6.0)
    return values.astype(jnp.bfloat16)


def draw_sub_sizes(key, part):
    key = jax.random.fold_in(key, 17)
    first_key, second_key = jax.random.split(key)
    half = SUB_AVG // 2
    pair_count = (SUBS - 2) // 2
    extra = jax.random.randint(first_key, (MB, pair_count), 0, half + 1)
    columns = [jnp.full((MB, 1), half, jnp.int32), jnp.full((MB, 1), -half, jnp.int32), extra, -extra]
    if SUBS % 2 == 1:
        columns.append(jnp.zeros((MB, 1), jnp.int32))
    offsets = jnp.concatenate(columns, axis=1).astype(jnp.int32)
    scores = jax.random.randint(second_key, (MB, SUBS), 0, 1 << 20) * SUBS + jnp.arange(SUBS, dtype=jnp.int32)[None, :]
    order = jnp.argsort(scores, axis=1)
    shuffled = jnp.take_along_axis(offsets, order, axis=1)
    return (SUB_AVG + shuffled).astype(jnp.int32)


def place_ends(drawn, own_key, low, high):
    longest = drawn.shape.index(max(drawn.shape))
    spots = []
    for shift in (0, 1):
        where = [jax.random.randint(jax.random.fold_in(own_key, axis), (), 0, length) for axis, length in enumerate(drawn.shape)]
        where[longest] = (where[longest] + shift) % drawn.shape[longest]
        spots.append(tuple(where))
    return drawn.at[spots[0]].set(low).at[spots[1]].set(high)


def steps_of(rng, shape, cuts, low, top_value):
    factor_of = 1.0
    for dim, blocks in cuts:
        draws = jax.random.uniform(jax.random.fold_in(jax.random.fold_in(rng, 6), dim), (blocks,), jnp.float32, low / len(cuts), top_value / len(cuts))
        factor_of = factor_of * jnp.repeat(jnp.exp(draws), shape[dim] // blocks).reshape((-1,) + (1,) * (len(shape) - 1 - dim))
    return factor_of


def bell_draw(own_key, shape, deviation, limit, shards=(), held_as=jnp.bfloat16):
    values = deviation * jax.random.normal(own_key, shape, jnp.float32)
    if shards:
        values = values * steps_of(own_key, shape, shards, -0.22, 0.18)
    return jnp.clip(values, -limit, limit).astype(held_as)


def setup_inputs(seed: int = 0) -> dict:
    key_of = jax.random.split(jax.random.key(seed), 18)
    return {
        "crops_in": draw_crops_in(jax.random.fold_in(key_of[17], 71), 0),
        "stem_weight": bell_draw(key_of[1], (CIN, MID), CIN ** -0.5, 0.125, ((1, 2),)),
        "middle_weight": bell_draw(key_of[2], (9, MID, MID), (9 * MID) ** -0.5, 0.09375, ((2, 2),)),
        "expand_weight": bell_draw(key_of[3], (MID, CIN), MID ** -0.5, 0.25, ((0, 2),)),
        "stem_gain": jnp.clip(1.0 + 0.1 * jax.random.normal(key_of[4], (MID,), jnp.float32), 0.5, 1.5),
        "stem_bias": bell_draw(key_of[5], (MID,), 0.3, 1.5, ((0, 2),), jnp.float32),
        "middle_gain": jnp.clip(1.0 + 0.1 * jax.random.normal(key_of[6], (MID,), jnp.float32), 0.5, 1.5),
        "middle_bias": bell_draw(key_of[7], (MID,), 0.3, 1.5, ((0, 2),), jnp.float32),
        "expand_gain": jnp.clip(1.0 + 0.1 * jax.random.normal(key_of[8], (CIN,), jnp.float32), 0.5, 1.5),
        "expand_bias": bell_draw(key_of[9], (CIN,), 0.3, 1.5, ((0, 2),), jnp.float32),
        "hidden_weight": bell_draw(key_of[10], (CIN, PH), CIN ** -0.5, 0.125, ((1, 2),)),
        "hidden_gain": jnp.clip(1.0 + 0.1 * jax.random.normal(key_of[11], (PH,), jnp.float32), 0.5, 1.5),
        "hidden_bias": bell_draw(key_of[12], (PH,), 0.3, 1.5, ((0, 2),), jnp.float32),
        "embed_weight": bell_draw(key_of[13], (PH, PO), (PH // 4) ** -0.5, 0.375, ((0, 2),)),
        "sub_sizes": draw_sub_sizes(jax.random.fold_in(key_of[17], 71), 0),
        "crop_order": jax.vmap(lambda own: jax.random.permutation(own, CROPS_MB))(jax.random.split(key_of[15], MB)).reshape((MB, CROPS_MB)).astype(jnp.int32),
        "pair_index": place_ends(jax.random.randint(key_of[16], (MB, PAIRS, 2), 0, CROPS_MB), jax.random.fold_in(key_of[16], 1), 0, CROPS_MB - 1).astype(jnp.int32),
    }


@jax.custom_vjp
def low(v):
    return lax.optimization_barrier(v.astype(jnp.bfloat16)).astype(jnp.float32)

@jax.custom_vjp
def low_back(v):
    return v

def low_keep(v):
    return (low(v), None)

def low_pass(kept, grad):
    return (grad,)

def back_keep(v):
    return (v, None)

def back_low(kept, grad):
    return (low(grad),)
low.defvjp(low_keep, low_pass)
low_back.defvjp(back_keep, back_low)
EPS_NORM = 1e-05
RIDGE = 0.5
LOSS_SCALE = 8192.0
HIGH = lax.Precision.HIGHEST

def matmul(left, right):
    return jnp.dot(left.astype(jnp.float32), right.astype(jnp.float32), precision=HIGH, preferred_element_type=jnp.float32)

def batch_norm(values, gain, bias):
    centre = lax.optimization_barrier(jnp.mean(values, axis=0))
    centred = values - centre
    spread = lax.optimization_barrier(jnp.mean(centred * centred, axis=0))
    return centred * lax.rsqrt(spread + EPS_NORM) * gain + bias

def conv_taps(field, weight):
    crops = field.shape[0]
    padded = jnp.pad(field, ((0, 0), (1, 1), (1, 1), (0, 0)))
    total = jnp.zeros((crops * SIDE * SIDE, weight.shape[2]), jnp.float32)
    for tap in range(9):
        row_off, col_off = (tap // 3, tap % 3)
        window = padded[:, row_off:row_off + SIDE, col_off:col_off + SIDE, :].reshape(crops * SIDE * SIDE, -1)
        total = total + matmul(window, weight[tap])
    return total

def whiten_stats(first, second, counts):
    centre = first / counts[:, None]
    eye = jnp.eye(first.shape[1], dtype=first.dtype)
    cov = second / counts[:, None, None] - centre[:, :, None] * centre[:, None, :] + RIDGE * eye
    return (centre, jnp.linalg.cholesky(cov))

def whiten_rows(embed, onehot, centre, factor):
    eye = jnp.broadcast_to(jnp.eye(factor.shape[1], dtype=factor.dtype), factor.shape)
    inverse = lax.linalg.triangular_solve(factor, eye, left_side=True, lower=True)
    centred = embed - jnp.dot(onehot.astype(jnp.float32), centre.astype(jnp.float32), precision=HIGH, preferred_element_type=jnp.float32)
    white = jnp.einsum('cs,sij,cj->ci', onehot, inverse, centred, precision=HIGH)
    return white * lax.rsqrt(lax.optimization_barrier(jnp.sum(white * white, axis=1, keepdims=True)) + EPS_NORM)

def pair_loss(normed, pairs):
    differ = normed[pairs[:, 0]] - normed[pairs[:, 1]]
    return jnp.mean(lax.optimization_barrier(jnp.sum(differ * differ, axis=1)))

def membership(order, sizes):
    count = order.shape[0]
    ends = jnp.cumsum(sizes)
    position = jnp.arange(count, dtype=jnp.int32)
    segment = lax.optimization_barrier(jnp.sum((position[:, None] >= ends[None, :-1]).astype(jnp.int32), axis=1)).astype(jnp.int32)
    return jnp.zeros((count,), jnp.int32).at[order].set(segment)

def micro_loss(field, weights, member, counts, pairs):
    stem_weight, middle_weight, expand_weight, stem_gain, stem_bias, middle_gain, middle_bias, expand_gain, expand_bias, hidden_weight, hidden_gain, hidden_bias, embed_weight = weights
    crops = field.shape[0]
    rows = field.reshape(crops * SIDE * SIDE, CIN)
    stem_pre = low_back(matmul(rows, stem_weight))
    stem_act = low(jax.nn.silu(batch_norm(stem_pre, stem_gain, stem_bias)))
    middle_pre = low_back(conv_taps(stem_act.reshape(crops, SIDE, SIDE, MID), middle_weight))
    middle_act = low(jax.nn.silu(batch_norm(middle_pre, middle_gain, middle_bias)))
    expand_pre = low_back(matmul(middle_act, expand_weight))
    summed = batch_norm(expand_pre, expand_gain, expand_bias) + rows
    pooled = low(lax.optimization_barrier(jnp.mean(jax.nn.silu(summed).reshape(crops, SIDE * SIDE, CIN), axis=1)))
    hidden_pre = low_back(matmul(pooled, hidden_weight))
    hidden_act = low(jax.nn.silu(batch_norm(hidden_pre, hidden_gain, hidden_bias)))
    embed = low_back(matmul(hidden_act, embed_weight))
    onehot = (member[:, None] == jnp.arange(SUBS, dtype=jnp.int32)[None, :]).astype(jnp.float32)
    first = matmul(onehot.T, embed)
    second = jnp.einsum('cs,ci,cj->sij', onehot, embed, embed, precision=HIGH)
    centre, factor = whiten_stats(first, second, counts)
    normed = whiten_rows(embed, onehot, centre, factor)
    return pair_loss(normed, pairs)

def reference(crops_in, stem_weight, middle_weight, expand_weight, stem_gain, stem_bias, middle_gain, middle_bias, expand_gain, expand_bias, hidden_weight, hidden_gain, hidden_bias, embed_weight, sub_sizes, crop_order, pair_index):
    params = tuple((value.astype(jnp.float32) for value in (stem_weight, middle_weight, expand_weight, stem_gain, stem_bias, middle_gain, middle_bias, expand_gain, expand_bias, hidden_weight, hidden_gain, hidden_bias, embed_weight)))
    loss_cotangent = jnp.asarray(LOSS_SCALE / MB, jnp.float32)
    loss_total = jnp.zeros((), jnp.float32)
    crop_grads = []
    totals = params
    for batch in range(MB):
        member = membership(crop_order[batch], sub_sizes[batch])
        counts = sub_sizes[batch].astype(jnp.float32)
        pairs = pair_index[batch]

        def objective(field, *weights):
            return micro_loss(field, weights, member, counts, pairs)
        value, pull = jax.vjp(objective, crops_in[batch].astype(jnp.float32), *params)
        pulled = pull(loss_cotangent)
        loss_total = loss_total + value / MB
        crop_grads.append(pulled[0])
        if batch == 0:
            totals = pulled[1:]
        else:
            totals = tuple((left + right for left, right in zip(totals, pulled[1:])))
    return (loss_total, jnp.stack(crop_grads, axis=0), totals[0], totals[1], totals[2], totals[3], totals[4], totals[5], totals[6], totals[7], totals[8], totals[9], totals[10], totals[11], totals[12])
```

```python
import types

import jax
import jax.numpy as jnp
from jax import lax
from jax.experimental import pallas as pl
from jax.experimental.pallas import tpu as pltpu
from jax.sharding import PartitionSpec as P

SIDE = 7
AREA = SIDE * SIDE
WIDE = SIDE + 1
EPS_NORM = 1e-05
RIDGE = 0.5
LOSS_SCALE = 8192.0
HIGH = lax.Precision.HIGHEST
MESH = pl.DeviceIdType.MESH
F32 = jnp.float32
BF16 = jnp.bfloat16
DMA = pltpu.SemaphoreType.DMA


def nn(left, right):
    return jnp.dot(left, right, preferred_element_type=F32)


def nt(left, right, precision=None):
    return lax.dot_general(
        left, right, (((1,), (1,)), ((), ())), precision=precision, preferred_element_type=F32
    )


def tn(left, right, precision=None):
    return lax.dot_general(
        left, right, (((0,), (0,)), ((), ())), precision=precision, preferred_element_type=F32
    )


def sigmoid(values):
    return 0.5 * jnp.tanh(0.5 * values) + 0.5


def silu(values):
    return values * sigmoid(values)


def slope(values):
    part = sigmoid(values)
    return part * (1.0 + values * (1.0 - part))


def rows_at(start, size):
    return pl.ds(pl.multiple_of(start, size if size % 16 else 16), size)


class Ctx:
    def __init__(self, devices, partner, peers):
        self.n = devices
        self.p = lax.axis_index("dp")
        self.h = lax.axis_index("chan")
        self.o = 1 - self.h
        self.waits = 0
        if partner or peers:
            barrier = pltpu.get_barrier_semaphore()
            if partner:
                pl.semaphore_signal(barrier, inc=1, device_id=(self.p, self.o), device_id_type=MESH)
                self.waits += 1
            if peers:

                def greet(d, carry):
                    pl.semaphore_signal(
                        barrier,
                        inc=1,
                        device_id=(lax.rem(self.p + d, self.n), self.h),
                        device_id_type=MESH,
                    )
                    return carry

                lax.fori_loop(1, self.n, greet, 0)
                self.waits += self.n - 1

    def ready(self):
        if self.waits:
            pl.semaphore_wait(pltpu.get_barrier_semaphore(), self.waits)
            self.waits = 0

    def half(self, which, size):
        return pl.ds(pl.multiple_of(which * size, size), size)

    def partner(self, src, dst, sems):
        return pltpu.make_async_remote_copy(
            src_ref=src,
            dst_ref=dst,
            send_sem=sems.at[0],
            recv_sem=sems.at[1],
            device_id=(self.p, self.o),
            device_id_type=MESH,
        )

    def spread(self, src, dst, sems):
        def one(d, carry):
            pltpu.make_async_remote_copy(
                src_ref=src,
                dst_ref=dst,
                send_sem=sems.at[0],
                recv_sem=sems.at[1],
                device_id=(lax.rem(self.p + d, self.n), self.h),
                device_id_type=MESH,
            ).start()
            return carry

        lax.fori_loop(1, self.n, one, 0)

    def take(self, blocks, sems, which):
        pltpu.make_async_copy(blocks, blocks, sems.at[which]).wait()


class Phase:
    def __init__(self, pre, post, begin=None, arrive=None, end=None, **more):
        nothing = lambda *_: None
        self.pre, self.post = pre, post
        self.begin, self.arrive, self.end = begin or nothing, arrive or nothing, end or nothing
        self.__dict__.update(more)

    def alone(self, nb):
        self.begin()
        for step in (self.pre, self.post, self.arrive):
            for mb in range(nb):
                step(mb)
        self.end()


def each(count, body):
    lax.fori_loop(0, count, lambda i, c: (body(i), c)[1], 0)


def local_moments(ref, mb, rows, chunk, cols, out):
    lanes = 256
    for lo in range(0, cols, lanes):
        at = pl.ds(lo, lanes)

        def add(i, total):
            part = ref[mb, rows_at(i * chunk, chunk), at]
            return total + jnp.sum(part.reshape(-1, 8, lanes), axis=0)

        total = lax.fori_loop(0, rows // chunk, add, jnp.zeros((8, lanes), F32))
        mean = jnp.sum(total, axis=0, keepdims=True) * (1.0 / rows)

        def square(i, total):
            part = ref[mb, rows_at(i * chunk, chunk), at] - mean
            return total + jnp.sum((part * part).reshape(-1, 8, lanes), axis=0)

        total = lax.fori_loop(0, rows // chunk, square, jnp.zeros((8, lanes), F32))
        out[mb, 0:1, at] = mean
        out[mb, 1:2, at] = jnp.sum(total, axis=0, keepdims=True)


def joint_moments(parts, rows):
    n = parts.shape[0]
    mean = jnp.sum(parts, axis=0)[0:1] * (1.0 / n)
    apart = parts[:, 0:1, :] - mean[None]
    squares = jnp.sum(parts, axis=0)[1:2] + rows * jnp.sum(apart * apart, axis=0)
    return mean, lax.rsqrt(squares * (1.0 / (n * rows)) + EPS_NORM)


def stem_forward(g, c):
    nb, rows, half = g.x.shape
    crops = rows // AREA
    mid = g.ws.shape[1]

    def swap():
        return c.partner(g.ws.at[c.half(c.o, half)], g.wsp, g.sem_sw)

    def give(mb):
        return c.partner(g.ss.at[mb], g.sr.at[mb], g.sem_sp.at[mb])

    def act(mb):
        return c.partner(g.ao.at[mb], g.ap.at[mb], g.sem_sa.at[mb])

    def begin():
        c.ready()
        swap().start()
        g.ao[...] = jnp.zeros(g.ao.shape, BF16)
        swap().wait_recv()
        for mb in range(nb):
            g.ss[mb] = nn(g.x[mb], g.wsp[...]).astype(BF16)
            give(mb).start()

    def pre(mb):
        own = nn(g.x[mb], g.ws[c.half(c.h, half), :])
        give(mb).wait_recv()
        g.ef[0] = own + g.sr[mb].astype(F32)
        local_moments(g.ef, 0, rows, 7 * crops, mid, g.em)
        g.spre[mb] = g.ef[0].astype(BF16)
        g.sm[mb] = g.em[0]
        g.sbuf[mb, c.p] = g.sm[mb]
        c.spread(g.sm.at[mb], g.sbuf.at[mb, c.p], g.sem_ss.at[mb])

    def post(mb):
        c.take(g.sbuf.at[mb, pl.ds(0, c.n - 1)], g.sem_ss.at[mb], 1)
        mean, scale = joint_moments(g.sbuf[mb], float(rows))
        g.sst[mb, 0:1] = mean
        g.sst[mb, 1:2] = scale
        gain = scale * g.stem_gain[...]
        bias = g.stem_bias[...] - mean * gain
        for i in range(SIDE):
            post = g.spre[mb, pl.ds(i * SIDE * crops, SIDE * crops)].astype(F32) * gain + bias
            g.ao[mb, pl.ds((WIDE + 1 + WIDE * i) * crops, SIDE * crops)] = silu(post).astype(BF16)
        act(mb).start()

    def end():
        swap().wait_send()
        for mb in range(nb):
            give(mb).wait_send()
            act(mb).wait_send()
            c.take(g.sbuf.at[mb, pl.ds(0, c.n - 1)], g.sem_ss.at[mb], 0)

    return Phase(pre, post, begin, lambda mb: act(mb).wait_recv(), end)


def conv_rows(crops):
    return SIDE * WIDE * crops


def middle_forward(g, c):
    nb, rows, mid = g.mpre.shape
    crops = rows // AREA
    long = conv_rows(crops)

    def act(mb):
        return c.partner(g.mo.at[mb], g.mp.at[mb], g.sem_ma.at[mb])

    def pre(mb):
        total = None
        for tap in range(9):
            at = pl.ds((WIDE * (tap // 3) + tap % 3) * crops, long)
            part = nn(g.ao[mb, at], g.wm[tap, c.half(c.h, mid), :])
            total = part if total is None else total + part
            total = total + nn(g.ap[mb, at], g.wm[tap, c.half(c.o, mid), :])
        for i in range(SIDE):
            g.ef[0, pl.ds(i * SIDE * crops, SIDE * crops)] = total[
                i * WIDE * crops : (i * WIDE + SIDE) * crops
            ]
        local_moments(g.ef, 0, rows, 7 * crops, mid, g.em)
        g.mpre[mb] = g.ef[0].astype(BF16)
        g.mm[mb] = g.em[0]
        g.mbuf[mb, c.p] = g.mm[mb]
        c.spread(g.mm.at[mb], g.mbuf.at[mb, c.p], g.sem_ms.at[mb])

    def post(mb):
        c.take(g.mbuf.at[mb, pl.ds(0, c.n - 1)], g.sem_ms.at[mb], 1)
        mean, scale = joint_moments(g.mbuf[mb], float(rows))
        g.mst[mb, 0:1] = mean
        g.mst[mb, 1:2] = scale
        gain = scale * g.middle_gain[...]
        bias = g.middle_bias[...] - mean * gain
        for i in range(SIDE):
            at = pl.ds(i * SIDE * crops, SIDE * crops)
            g.mo[mb, at] = silu(g.mpre[mb, at].astype(F32) * gain + bias).astype(BF16)
        act(mb).start()

    def end():
        for mb in range(nb):
            act(mb).wait_send()
            c.take(g.mbuf.at[mb, pl.ds(0, c.n - 1)], g.sem_ms.at[mb], 0)

    return Phase(pre, post, c.ready, lambda mb: act(mb).wait_recv(), end)


def expand_forward(g, c):
    nb, rows, half = g.x.shape
    crops = rows // AREA
    lanes = 256

    def swap():
        return c.partner(g.we.at[:, c.half(c.o, half)], g.wep, g.sem_ew)

    def pool(mb):
        return c.partner(g.po.at[mb], g.pp.at[mb], g.sem_ep.at[mb])

    def early():
        c.ready()
        swap().start()

    def begin():
        early()
        swap().wait_recv()

    def pre(mb):
        for k in range(half // lanes):
            cols = pl.ds(k * lanes, lanes)
            own = g.we[:, pl.ds(pl.multiple_of(c.h * half + k * lanes, lanes), lanes)]
            g.ef[0] = nn(g.mo[mb], own) + nn(g.mp[mb], g.wep[:, cols])
            local_moments(g.ef, 0, rows, 7 * crops, lanes, g.em)
            g.epre[mb, :, cols] = g.ef[0].astype(BF16)
            g.esend[mb, :, cols] = g.em[0]
        g.ebuf[mb, c.p] = g.esend[mb]
        c.spread(g.esend.at[mb], g.ebuf.at[mb, c.p], g.sem_es.at[mb])

    def post(mb):
        c.take(g.ebuf.at[mb, pl.ds(0, c.n - 1)], g.sem_es.at[mb], 1)
        mean, scale = joint_moments(g.ebuf[mb], float(rows))
        g.est[mb, 0:1] = mean
        g.est[mb, 1:2] = scale
        for lo in range(0, half, lanes):
            cols = pl.ds(lo, lanes)
            gain = g.est[mb, 1:2, cols] * g.expand_gain[:, cols]
            bias = g.expand_bias[:, cols] - g.est[mb, 0:1, cols] * gain

            def pixels(i, total):
                for j in range(SIDE):
                    at = rows_at((i * SIDE + j) * crops, crops)
                    summed = g.epre[mb, at, cols].astype(F32) * gain + bias
                    summed = summed + g.x[mb, at, cols].astype(F32)
                    total = total + silu(summed)
                return total

            total = lax.fori_loop(0, SIDE, pixels, jnp.zeros((crops, lanes), F32))
            g.po[mb, :, cols] = (total * (1.0 / AREA)).astype(BF16)
        pool(mb).start()

    def end():
        swap().wait_send()
        for mb in range(nb):
            pool(mb).wait_send()
            c.take(g.ebuf.at[mb, pl.ds(0, c.n - 1)], g.sem_es.at[mb], 0)

    return Phase(
        pre, post, begin, lambda mb: pool(mb).wait_recv(), end, early=early,
        weights=lambda: swap().wait_recv(),
    )


def hidden_forward(g, c):
    nb, crops, half = g.po.shape
    part = crops // 2

    def trade(mb):
        return c.partner(g.pe.at[mb], g.pr.at[mb], g.sem_he.at[mb])

    def swap(mb):
        where = g.gath.at[mb, :, c.h]
        return c.partner(where, where, g.sem_hx.at[mb])

    def others(mb):
        return g.gath.at[mb, pl.ds(0, c.n - 1), c.h]

    def pre(mb):
        at = slice(mb * crops, (mb + 1) * crops)
        value = nn(g.po[mb], g.wh[c.half(c.h, half), :]) + nn(g.pp[mb], g.wh[c.half(c.o, half), :])
        g.hpre[at] = value
        mean = jnp.mean(value, axis=0, keepdims=True)
        g.hm[mb, 0:1] = mean
        g.hm[mb, 1:2] = jnp.sum((value - mean) * (value - mean), axis=0, keepdims=True)
        g.hbuf[mb, c.p] = g.hm[mb]
        c.spread(g.hm.at[mb], g.hbuf.at[mb, c.p], g.sem_hs.at[mb])

    def post(mb):
        at = slice(mb * crops, (mb + 1) * crops)
        c.take(g.hbuf.at[mb, pl.ds(0, c.n - 1)], g.sem_hs.at[mb], 1)
        mean, scale = joint_moments(g.hbuf[mb], float(crops))
        g.hst[mb, 0:1] = mean
        g.hst[mb, 1:2] = scale
        gain = scale * g.hidden_gain[...]
        bias = g.hidden_bias[...] - mean * gain
        act = silu(g.hpre[at] * gain + bias).astype(BF16)
        g.hact[at] = act
        g.pe[mb] = nn(act, g.w2[...])
        trade(mb).start()

    def embed(mb):
        trade(mb).wait_recv()
        g.em2[mb] = (g.pe[mb] + g.pr[mb]).reshape(2, part, -1)
        g.gath[mb, c.p, c.h] = g.em2[mb, c.h]
        c.spread(g.em2.at[mb, c.h], g.gath.at[mb, c.p, c.h], g.sem_hg.at[mb])

    def mirror(mb):
        c.take(others(mb), g.sem_hg.at[mb], 1)
        swap(mb).start()

    def arrive(mb):
        swap(mb).wait_recv()

    def end():
        for mb in range(nb):
            trade(mb).wait_send()
            swap(mb).wait_send()
            c.take(g.hbuf.at[mb, pl.ds(0, c.n - 1)], g.sem_hs.at[mb], 0)
            c.take(others(mb), g.sem_hg.at[mb], 0)

    def all_arrive(mb):
        if mb == 0:
            for step in (embed, mirror, arrive):
                for k in range(nb):
                    step(k)

    return Phase(
        pre, post, c.ready, all_arrive, end, embed=embed, mirror=mirror, landed=arrive
    )


def eliminate(cov):
    total, width = cov.shape[0], cov.shape[1]
    pack = 8 * total
    side = -(-pack // width) * width
    lane = lax.broadcasted_iota(jnp.int32, (1, 1, width), 2)
    level = lax.broadcasted_iota(jnp.int32, (1, 8, width), 1)
    wide = lax.broadcasted_iota(jnp.int32, (1, side), 1)
    for start in range(0, width, 8):
        panel = cov[:, start : start + 8, :]
        inverses = []
        for i in range(8):
            here = lane == start + i
            column = panel[:, :, start + i : start + i + 1]
            pivot = panel[:, i : i + 1, :]
            inverse = 1.0 / column[:, i : i + 1, :]
            row = jnp.where(here, 1.0, pivot) * inverse
            inverses.append(inverse)
            cleared = jnp.where(here, 0.0, panel)
            panel = jnp.where(level > i, cleared - column * row, panel)
        cov[:, start : start + 8, :] = panel
        if start + 8 == width:
            break
        inside = lane - start
        unit = jnp.where(inside == level, 1.0, 0.0)
        rows = jnp.where(jnp.logical_and(inside >= level, inside < 8), unit, panel)
        scaled = panel * jnp.concatenate(inverses, axis=1)
        rows = rows.reshape(pack, width)
        scaled = scaled.reshape(pack, width)
        if side > pack:
            blank = jnp.zeros((side - pack, width), F32)
            rows = jnp.concatenate([rows, blank], axis=0)
            scaled = jnp.concatenate([scaled, blank], axis=0)
        factors = scaled.T[start + 8 :]
        kept = jnp.logical_or(lane[0] < start, lane[0] >= start + 8)
        for k in range(total):
            own = jnp.where(wide // 8 == k, factors, 0.0)
            change = jnp.dot(own, rows, precision=HIGH, preferred_element_type=F32)
            cov[k, start + 8 :, :] = jnp.where(kept, cov[k, start + 8 :, :], 0.0) - change


def whiten(g, c):
    nb, count = g.order.shape[0], g.order.shape[2]
    crops = g.ed.shape[0] // nb
    subs = g.sizes.shape[1]
    width = g.gath.shape[-1]
    pairs = g.pairs.shape[2]
    lane = lax.broadcasted_iota(jnp.int32, (1, width), 1)
    eye = (
        lax.broadcasted_iota(jnp.int32, (width, width), 0)
        == lax.broadcasted_iota(jnp.int32, (width, width), 1)
    ).astype(F32)
    lower = (
        lax.broadcasted_iota(jnp.int32, (width, width), 0)
        >= lax.broadcasted_iota(jnp.int32, (width, width), 1)
    ).astype(F32)
    strict = lower - eye
    crop_id = lax.broadcasted_iota(jnp.int32, (count, 1), 0)
    place = lax.broadcasted_iota(jnp.int32, (1, count), 1)

    def prepare(mb):
        end = jnp.int32(0)
        segment = jnp.zeros((1, count), F32)
        for k in range(subs - 1):
            end = end + g.sizes[mb, k]
            segment = segment + (place >= end).astype(F32)
        member = jnp.sum(
            jnp.where(g.order[mb] == crop_id, segment, 0.0), axis=1, keepdims=True
        )
        g.member[mb] = jnp.broadcast_to(member, (count, width))
        embed = g.gath[mb].reshape(count, width)
        centred = jnp.zeros((count, width), F32)
        for k in range(subs):
            mask = (member == float(k)).astype(F32)
            size = g.sizes[mb, k].astype(F32)
            centre = jnp.sum(embed * mask, axis=0, keepdims=True) / size
            rows = (embed - centre) * mask
            centred = centred + rows
            g.cov[mb * subs + k] = tn(rows, rows, HIGH) / size + RIDGE * eye
        g.cent[mb] = centred

    def factor_all():
        eliminate(g.cov)
        for k in range(nb * subs):
            inverse = g.cov[k]
            power = jnp.sum(inverse * eye, axis=1, keepdims=True)
            g.cov[k] = lax.rsqrt(power) * (inverse * strict + eye)
        g.loss[...] = jnp.zeros(g.loss.shape, F32)

    def rest(mb):
        centred = g.cent[mb]
        member = g.member[mb]
        white = jnp.zeros((count, width), F32)
        for k in range(subs):
            mask = (member == float(k)).astype(F32)
            white = white + nt(centred * mask, g.cov[mb * subs + k], HIGH)
        power = jnp.sum(white * white, axis=1, keepdims=True)
        factor = lax.rsqrt(power + EPS_NORM)
        normed = white * factor
        choose = (g.pairs[mb, 0:1] == crop_id).astype(F32) - (g.pairs[mb, 1:2] == crop_id).astype(F32)
        differ = tn(choose, normed, HIGH)
        g.loss[...] = g.loss[...] + jnp.sum(differ * differ) * (1.0 / (pairs * nb))
        grad = jnp.dot(choose, differ, precision=HIGH, preferred_element_type=F32)
        grad = grad * (2.0 * LOSS_SCALE / (nb * pairs))
        inner = jnp.sum(grad * white, axis=1, keepdims=True)
        grad = grad * factor - white * (factor * factor * factor * inner)
        own = pl.ds(pl.multiple_of(c.p * crops, crops), crops)
        g.cent[mb] = white
        g.wgrad[...] = grad
        own_white = g.cent[mb, own, :]
        own_grad = g.wgrad[own, :]
        own_member = g.member[mb, own, :]
        delta = jnp.zeros((crops, width), F32)
        for k in range(subs):
            size = g.sizes[mb, k].astype(F32)
            rows = grad * (member == float(k)).astype(F32)
            sums = jnp.sum(rows, axis=0, keepdims=True)
            low = tn(rows, white, HIGH)
            both = low * lower + (low * strict).T
            inside = (own_member == float(k)).astype(F32)
            part = jnp.dot(own_white * inside, both, precision=HIGH, preferred_element_type=F32)
            part = (own_grad - (sums + part) / size) * inside
            delta = delta + jnp.dot(
                part, g.cov[mb * subs + k], precision=HIGH, preferred_element_type=F32
            )
        g.ed[rows_at(mb * crops, crops), :] = delta.astype(BF16)

    def post(mb):
        if mb == 0:
            factor_all()
        rest(mb)

    return Phase(prepare, post)


def hidden_backward(g, c):
    nb, crops, half = g.po.shape

    def give():
        return c.partner(g.pgs, g.pgr, g.sem_hp)

    def run():
        delta = g.ed[...]
        grad = nt(delta, g.w2[...])
        normals, grads = [], []
        for mb in range(nb):
            at = slice(mb * crops, (mb + 1) * crops)
            normal = (g.hpre[at] - g.hst[mb, 0:1]) * g.hst[mb, 1:2]
            part = grad[at] * slope(normal * g.hidden_gain[...] + g.hidden_bias[...])
            g.hbm[mb, 0:1] = jnp.sum(part, axis=0, keepdims=True)
            g.hbm[mb, 1:2] = jnp.sum(part * normal, axis=0, keepdims=True)
            normals.append(normal)
            grads.append(part)
        g.hbb[c.p] = g.hbm[...]
        c.ready()
        c.spread(g.hbm, g.hbb.at[c.p], g.sem_hb)
        g.gemb[...] = tn(g.hact[...], delta).astype(BF16)
        c.take(g.hbb.at[pl.ds(0, c.n - 1)], g.sem_hb, 1)
        count = float(crops) * c.n
        totals = jnp.zeros(g.hgrad.shape, F32)
        for mb in range(nb):
            sums = jnp.sum(g.hbb[:, mb], axis=0)
            totals = totals + sums
            part = grads[mb] - sums[0:1] * (1.0 / count) - normals[mb] * (sums[1:2] * (1.0 / count))
            part = part * (g.hidden_gain[...] * g.hst[mb, 1:2])
            g.hd[mb * crops : (mb + 1) * crops] = part.astype(BF16)
        g.hgrad[...] = totals
        hd = g.hd[...]
        g.pgs[...] = nt(hd, g.wh[c.half(c.o, half), :]).astype(BF16)
        give().start()

    def weights():
        hd = g.hd[...]
        po = g.po[...].reshape(nb * crops, half)
        pp = g.pp[...].reshape(nb * crops, half)
        g.ghid[c.half(c.h, half), :] = tn(po, hd).astype(BF16)
        g.ghid[c.half(c.o, half), :] = tn(pp, hd).astype(BF16)

    def finish():
        own = nt(g.hd[...], g.wh[c.half(c.h, half), :])
        give().wait_recv()
        g.pg[...] = ((own + g.pgr[...].astype(F32)) * (1.0 / AREA)).reshape(g.pg.shape)

    def end():
        give().wait_send()
        c.take(g.hbb.at[pl.ds(0, c.n - 1)], g.sem_hb, 0)

    def pre(mb):
        if mb == 0:
            for step in (run, weights, finish):
                step()

    return Phase(pre, lambda mb: None, None, None, end, run=run, weights=weights, finish=finish)


def expand_backward(g, c):
    nb, rows, half = g.x.shape
    crops = rows // AREA
    mid = g.we.shape[0]
    lanes = 256
    total_rows = float(rows) * c.n

    def pre(mb):
        if mb == 0:
            g.egrad[...] = jnp.zeros(g.egrad.shape, F32)
        for lo in range(0, half, lanes):
            cols = pl.ds(lo, lanes)
            scale = g.est[mb, 1:2, cols]
            shift = -g.est[mb, 0:1, cols] * scale
            gain = g.expand_gain[:, cols]
            bias = g.expand_bias[:, cols]
            grad = g.pg[mb, :, cols]

            def pixels(i, carry):
                one, two = carry
                for j in range(SIDE):
                    at = rows_at((i * SIDE + j) * crops, crops)
                    normal = g.epre[mb, at, cols].astype(F32) * scale + shift
                    summed = normal * gain + bias + g.x[mb, at, cols].astype(F32)
                    part = grad * slope(summed)
                    g.sg[mb, at, cols] = part.astype(BF16)
                    one = one + part
                    two = two + part * normal
                return one, two

            zero = jnp.zeros((crops, lanes), F32)
            one, two = lax.fori_loop(0, SIDE, pixels, (zero, zero))
            g.ebm[mb, 0:1, cols] = jnp.sum(one, axis=0, keepdims=True)
            g.ebm[mb, 1:2, cols] = jnp.sum(two, axis=0, keepdims=True)
        g.ebb[mb, c.p] = g.ebm[mb]
        c.spread(g.ebm.at[mb], g.ebb.at[mb, c.p], g.sem_eb.at[mb])

    def give(mb):
        return c.partner(g.mgs.at[mb], g.mgr.at[mb], g.sem_mg.at[mb])

    def swap():
        return c.partner(g.gxs, g.gexp.at[c.half(c.h, mid)], g.sem_gx)

    def post(mb):
        c.take(g.ebb.at[mb, pl.ds(0, c.n - 1)], g.sem_eb.at[mb], 1)
        g.ebt[...] = jnp.sum(g.ebb[mb], axis=0)
        g.egrad[...] = g.egrad[...] + g.ebt[...]
        for lo in range(0, half, lanes):
            cols = pl.ds(lo, lanes)
            scale = g.est[mb, 1:2, cols]
            gain = g.expand_gain[:, cols] * scale
            slant = gain * g.ebt[1:2, cols] * (-1.0 / total_rows)
            base = gain * g.ebt[0:1, cols] * (-1.0 / total_rows)
            base = base - slant * scale * g.est[mb, 0:1, cols]
            slant = slant * scale

            def pixels(i, carry):
                for j in range(SIDE):
                    at = rows_at((i * SIDE + j) * crops, crops)
                    part = g.sg[mb, at, cols].astype(F32) * gain + base
                    part = part + g.epre[mb, at, cols].astype(F32) * slant
                    g.xd[mb, at, cols] = part.astype(BF16)
                return carry

            lax.fori_loop(0, SIDE, pixels, 0)
        g.mgs[mb] = nt(g.xd[mb], g.wep[...]).astype(BF16)
        give(mb).start()
        g.mg[mb] = nt(g.xd[mb], g.we[:, c.half(c.h, half)])

    def weights():
        xd = g.xd[...].reshape(nb * rows, half)
        g.gxs[...] = tn(g.mp[...].reshape(nb * rows, mid), xd).astype(BF16)
        swap().start()
        g.gexp[c.half(c.h, mid), :] = tn(g.mo[...].reshape(nb * rows, mid), xd).astype(BF16)

    def arrive(mb):
        give(mb).wait()
        g.mg[mb] = g.mg[mb] + g.mgr[mb].astype(F32)

    def weights_in():
        swap().wait_recv()

    def end():
        swap().wait_send()
        for mb in range(nb):
            c.take(g.ebb.at[mb, pl.ds(0, c.n - 1)], g.sem_eb.at[mb], 0)

    def end_alone():
        weights()
        weights_in()
        end()

    return Phase(
        pre, post, c.ready, arrive, end_alone, weights=weights, weights_in=weights_in, close=end
    )


def norm_slopes(c, mb, grad, pre, stats, gain, bias, sums, buf, sem, out):
    rows, mid = pre.shape[1:]
    scale = stats[mb, 1:2]
    shift = -stats[mb, 0:1] * scale
    chunk = rows // SIDE

    def image_row(i, carry):
        one, two = carry
        at = rows_at(i * chunk, chunk)
        normal = pre[mb, at].astype(F32) * scale + shift
        part = grad[mb, at] * slope(normal * gain[...] + bias[...])
        out[mb, at] = part
        one = one + jnp.sum(part.reshape(-1, 8, mid), axis=0)
        two = two + jnp.sum((part * normal).reshape(-1, 8, mid), axis=0)
        return one, two

    zero = jnp.zeros((8, mid), F32)
    one, two = lax.fori_loop(0, SIDE, image_row, (zero, zero))
    sums[mb, 0:1] = jnp.sum(one, axis=0, keepdims=True)
    sums[mb, 1:2] = jnp.sum(two, axis=0, keepdims=True)
    buf[mb, c.p] = sums[mb]
    c.spread(sums.at[mb], buf.at[mb, c.p], sem.at[mb])


def norm_terms(stats, mb, gain, sums, count):
    scale = stats[mb, 1:2]
    a = gain * scale
    slant = a * sums[1:2] * (-1.0 / count)
    k = a * sums[0:1] * (-1.0 / count) - slant * scale * stats[mb, 0:1]
    return a, slant * scale, k


def middle_backward(g, c):
    nb, rows, mid = g.mpre.shape
    crops = rows // AREA
    long = conv_rows(crops)
    count = float(rows) * c.n

    def begin():
        c.ready()
        g.mdg[...] = jnp.zeros(g.mdg.shape, BF16)
        g.mgrad[...] = jnp.zeros(g.mgrad.shape, F32)

    def pre(mb):
        norm_slopes(
            c, mb, g.mg, g.mpre, g.mst, g.middle_gain, g.middle_bias, g.mbm, g.mbb,
            g.sem_mb, g.mgf,
        )

    def give(mb):
        return c.partner(g.ags.at[mb], g.agr.at[mb], g.sem_ag.at[mb])

    def delta(mb):
        c.take(g.mbb.at[mb, pl.ds(0, c.n - 1)], g.sem_mb.at[mb], 1)
        sums = jnp.sum(g.mbb[mb], axis=0)
        g.mgrad[...] = g.mgrad[...] + sums
        a, b, k = norm_terms(g.mst, mb, g.middle_gain[...], sums, count)
        for i in range(SIDE):
            at = pl.ds(i * SIDE * crops, SIDE * crops)
            part = g.mgf[mb, at] * a + g.mpre[mb, at].astype(F32) * b + k
            g.mdg[mb, pl.ds((WIDE + 1 + WIDE * i) * crops, SIDE * crops)] = part.astype(BF16)
        g.mdt[:, mb * long : (mb + 1) * long] = g.mdg[mb, pl.ds((WIDE + 1) * crops, long)].T

    def spread(mb):
        for which, place in ((c.o, 0), (c.h, 1)):
            total = None
            for tap in range(9):
                at = pl.ds((WIDE * (2 - tap // 3) + 2 - tap % 3) * crops, long)
                part = nt(g.mdg[mb, at], g.wm[tap, c.half(which, mid), :])
                total = part if total is None else total + part
            for i in range(SIDE):
                at = pl.ds(i * SIDE * crops, SIDE * crops)
                part = total[i * WIDE * crops : (i * WIDE + SIDE) * crops]
                if place == 0:
                    g.ags[mb, at] = part.astype(BF16)
                else:
                    g.ag[mb, at] = part
            if place == 0:
                give(mb).start()

    def weights(out, first, taps):
        def one(i):
            tap = first + i
            at = pl.ds(pl.multiple_of((WIDE * (tap // 3) + tap % 3) * crops, crops), long)
            for act, which in ((g.ao, c.h), (g.ap, c.o)):
                field = jnp.concatenate([act[mb, at] for mb in range(nb)], axis=0)
                part = nn(g.mdt[...], field)
                out[c.half(2 * i + which, mid), :] = part.T.astype(BF16)

        each(taps, one)

    def arrive(mb):
        give(mb).wait()
        g.ag[mb] = g.ag[mb] + g.agr[mb].astype(F32)

    def end():
        for mb in range(nb):
            c.take(g.mbb.at[mb, pl.ds(0, c.n - 1)], g.sem_mb.at[mb], 0)

    def post(mb):
        delta(mb)
        spread(mb)

    def all_weights():
        weights(g.gmida, 0, 3)
        weights(g.gmidb, 3, 3)
        weights(g.gmidc, 6, 3)

    def end_alone():
        all_weights()
        end()

    return Phase(
        pre, post, begin, arrive, end_alone, delta=delta, spread=spread, weights=weights, close=end
    )


def stem_backward(g, c):
    nb, rows, mid = g.spre.shape
    half = g.x.shape[2]
    crops = rows // AREA
    count = float(rows) * c.n

    def begin():
        c.ready()
        g.sgrad[...] = jnp.zeros(g.sgrad.shape, F32)

    def pre(mb):
        norm_slopes(
            c, mb, g.ag, g.spre, g.sst, g.stem_gain, g.stem_bias, g.sbm, g.sbb,
            g.sem_sb, g.sgf,
        )

    def give(mb):
        return c.partner(g.sd.at[mb], g.sdp.at[mb], g.sem_sd.at[mb])

    def swap():
        return c.partner(g.gss, g.gstem.at[c.half(c.h, half)], g.sem_gs)

    def post(mb):
        c.take(g.sbb.at[mb, pl.ds(0, c.n - 1)], g.sem_sb.at[mb], 1)
        sums = jnp.sum(g.sbb[mb], axis=0)
        g.sgrad[...] = g.sgrad[...] + sums
        a, b, k = norm_terms(g.sst, mb, g.stem_gain[...], sums, count)
        for i in range(SIDE):
            at = pl.ds(i * SIDE * crops, SIDE * crops)
            g.sd[mb, at] = (g.sgf[mb, at] * a + g.spre[mb, at].astype(F32) * b + k).astype(BF16)
        give(mb).start()

    def weights():
        lanes = 256
        sd = g.sd[...].reshape(nb * rows, mid)
        sdp = g.sdp[...].reshape(nb * rows, mid)
        for lo in range(0, half, lanes):
            field = g.x[:, :, lo : lo + lanes].reshape(nb * rows, lanes)
            g.gss[lo : lo + lanes] = tn(field, sdp).astype(BF16)
            own = rows_at(c.h * half + lo, lanes)
            g.gstem[own, :] = tn(field, sd).astype(BF16)
        swap().start()

    def weights_in():
        swap().wait_recv()

    def end():
        swap().wait_send()
        for mb in range(nb):
            give(mb).wait_send()
            c.take(g.sbb.at[mb, pl.ds(0, c.n - 1)], g.sem_sb.at[mb], 0)

    def end_alone():
        weights()
        weights_in()
        end()

    return Phase(
        pre, post, begin, lambda mb: give(mb).wait_recv(), end_alone, weights=weights,
        weights_in=weights_in, close=end,
    )


def crops_backward(g, c):
    half = g.wsp.shape[0]

    def pre(mb):
        part = nt(g.sd[mb], g.ws[c.half(c.h, half), :]) + nt(g.sdp[mb], g.wsp[...])
        g.gcrops[mb] = (part + g.sg[mb].astype(F32)).astype(BF16)

    return Phase(pre, lambda mb: None)


class Total:
    def __init__(self, c, local, out, one, two, three, sems):
        self.done = 0
        self.c, self.local, self.out, self.sems = c, local, out, sems
        self.one, self.two, self.three = one, two, three
        self.long = local.shape[0] // 2
        x, y, self.z = c.p % 2, (c.p // 2) % 2, c.p // 4
        step_x, step_y = c.p + 1 - 2 * x, c.p + 2 - 4 * y
        self.ways = ((x, step_x, y, step_y), (y, step_y, x, step_x))
        self.half, self.quarter, self.piece = self.long // 2, self.long // 4, self.long // 16

    def copy(self, stream, step, src, dst, device):
        return pltpu.make_async_remote_copy(
            src_ref=src,
            dst_ref=dst,
            send_sem=self.sems.at[stream, step, 0],
            recv_sem=self.sems.at[stream, step, 1],
            device_id=(device, self.c.h),
            device_id_type=MESH,
        )

    def at(self, start, size):
        return pl.ds(pl.multiple_of(start, 16), size)

    def start(self, step):
        for stream in range(2):
            b1, d1, b2, d2 = self.ways[stream]
            base = stream * self.long
            kept = base + b1 * self.half
            core = kept + b2 * self.quarter
            if step == 0:
                src = self.local.at[self.at(base + (1 - b1) * self.half, self.half)]
                self.copy(stream, step, src, self.one.at[stream], d1).start()
            elif step == 1:
                src = self.one.at[stream, self.at((1 - b2) * self.quarter, self.quarter)]
                self.copy(stream, step, src, self.two.at[stream], d2).start()
            elif step == 4:
                self.keep(stream, core).wait()
                src = self.out.at[self.at(core, self.quarter)]
                self.copy(stream, step, src, src, d2).start()
            elif step == 5:
                src = self.out.at[self.at(kept, self.half)]
                self.copy(stream, step, src, src, d1).start()
            else:
                if step == 3:
                    self.keep(stream, core).start()
                for d in range(1, 4):
                    other = (self.z + d) % 4
                    device = self.c.p + 4 * (other - self.z)
                    if step == 2:
                        src = self.two.at[stream, self.at(other * self.piece, self.piece)]
                        dst = self.three.at[stream, 3 - d]
                    else:
                        src = self.two.at[stream, self.at(self.z * self.piece, self.piece)]
                        dst = self.out.at[self.at(core + self.z * self.piece, self.piece)]
                    self.copy(stream, step, src, dst, device).start()

    def keep(self, stream, core):
        piece = self.at(self.z * self.piece, self.piece)
        place = self.at(core + self.z * self.piece, self.piece)
        return pltpu.make_async_copy(
            self.two.at[stream, piece], self.out.at[place], self.sems.at[stream, 6, 0]
        )

    def wait(self, stream, step, which):
        blocks = {0: self.one, 1: self.two, 2: self.three, 3: self.three, 4: self.two, 5: self.one}
        self.c.take(blocks[step].at[stream], self.sems.at[stream, step], which)

    def take(self, step):
        for stream in range(2):
            self.wait(stream, step, 1)
            b1, d1, b2, d2 = self.ways[stream]
            kept = stream * self.long + b1 * self.half
            core = kept + b2 * self.quarter
            one, two, three = self.one.at[stream], self.two.at[stream], self.three.at[stream]
            if step == 0:
                self.add(one, 0, [(one, 0), (self.local, kept)], self.half)
            elif step == 1:
                self.add(two, 0, [(two, 0), (one, b2 * self.quarter)], self.quarter)
            elif step == 2:
                terms = [(two, self.z * self.piece)] + [(three.at[d], 0) for d in range(3)]
                self.add(two, self.z * self.piece, terms, self.piece)

    def add(self, out, start, terms, size):
        chunk = 16

        def one(i):
            total = None
            for ref, begin in terms:
                value = ref[rows_at(begin + i * chunk, chunk), :].astype(F32)
                total = value if total is None else total + value
            out[rows_at(start + i * chunk, chunk), :] = total.astype(BF16)

        each(size // chunk, one)

    def step(self):
        self.take(self.done)
        self.done += 1
        if self.done < 6:
            self.start(self.done)

    def close(self):
        for stream in range(2):
            for step in range(6):
                self.wait(stream, step, 0)


def whole_step(g, c):
    nb = g.x.shape[0]
    stem, middle, expand = stem_forward(g, c), middle_forward(g, c), expand_forward(g, c)
    hidden, white, hback = hidden_forward(g, c), whiten(g, c), hidden_backward(g, c)
    eback, mback, sback = expand_backward(g, c), middle_backward(g, c), stem_backward(g, c)
    field = crops_backward(g, c)

    def chain(first, second, extra=None):
        first.post(0)
        for mb in range(1, nb):
            first.post(mb)
            first.arrive(mb - 1)
            second.pre(mb - 1)
        first.arrive(nb - 1)
        second.pre(nb - 1)

    stem.begin()
    expand.early()
    for mb in range(nb):
        stem.pre(mb)
    chain(stem, middle)
    expand.weights()
    chain(middle, expand)
    chain(expand, hidden)
    for step in (hidden.post, hidden.embed, hidden.mirror):
        for mb in range(nb):
            step(mb)
    for mb in range(nb):
        hidden.landed(mb)
        white.pre(mb)
    for mb in range(nb):
        white.post(mb)
    for phase in (stem, middle, expand, hidden):
        phase.end()

    hid = Total(c, g.ghid, g.ghid_t, g.ghid_1, g.ghid_2, g.ghid_3, g.sem_ghid)
    emb = Total(c, g.gemb, g.gemb_t, g.gemb_1, g.gemb_2, g.gemb_3, g.sem_gemb)
    exp = Total(c, g.gexp, g.gexp_t, g.gexp_1, g.gexp_2, g.gexp_3, g.sem_gexp)
    one = Total(c, g.gmida, g.gmida_t, g.gmida_1, g.gmida_2, g.gmida_3, g.sem_gmida)
    two = Total(c, g.gmidb, g.gmidb_t, g.gmidb_1, g.gmidb_2, g.gmidb_3, g.sem_gmidb)
    three = Total(c, g.gmidc, g.gmidc_t, g.gmidc_1, g.gmidc_2, g.gmidc_3, g.sem_gmidc)
    last = Total(c, g.gstem, g.gstem_t, g.gstem_1, g.gstem_2, g.gstem_3, g.sem_gstem)

    hback.run()
    hback.weights()
    hid.start(0)
    emb.start(0)
    hback.finish()
    for mb in range(nb):
        eback.pre(mb)
    mback.begin()
    sback.begin()
    hid.step()
    emb.step()
    eback.post(0)
    eback.post(1)
    hid.step()
    emb.step()
    eback.arrive(0)
    mback.pre(0)
    eback.post(2)
    eback.arrive(1)
    mback.pre(1)
    hid.step()
    emb.step()
    eback.arrive(2)
    mback.pre(2)
    eback.weights()
    hid.step()
    emb.step()
    eback.weights_in()
    exp.start(0)
    for mb in range(nb):
        mback.delta(mb)
    mback.weights(g.gmida, 0, 3)
    one.start(0)
    hid.step()
    emb.step()
    exp.step()
    mback.weights(g.gmidb, 3, 3)
    two.start(0)
    exp.step()
    one.step()
    mback.weights(g.gmidc, 6, 3)
    three.start(0)
    hid.step()
    emb.step()
    exp.step()
    two.step()
    mback.spread(0)
    one.step()
    mback.spread(1)
    exp.step()
    three.step()
    mback.arrive(0)
    sback.pre(0)
    mback.spread(2)
    two.step()
    one.step()
    mback.arrive(1)
    sback.pre(1)
    exp.step()
    three.step()
    mback.arrive(2)
    sback.pre(2)
    two.step()
    one.step()
    for mb in range(nb):
        sback.post(mb)
    exp.step()
    three.step()
    for mb in range(nb):
        sback.arrive(mb)
    sback.weights()
    two.step()
    one.step()
    sback.weights_in()
    last.start(0)
    three.step()
    field.pre(0)
    two.step()
    one.step()
    field.pre(1)
    last.step()
    three.step()
    field.pre(2)
    last.step()
    two.step()
    three.step()
    last.step()
    last.step()
    last.step()
    last.step()
    for phase in (hback, white):
        phase.end()
    for phase in (eback, mback, sback):
        phase.close()
    for total in (hid, emb, exp, one, two, three, last):
        total.close()


GRADS = ("ghid", "gemb", "gexp", "gmida", "gmidb", "gmidc", "gstem")


def names_of(functions):
    found, codes = set(), [function.__code__ for function in functions]
    while codes:
        code = codes.pop()
        found |= set(code.co_names)
        codes += [value for value in code.co_consts if isinstance(value, types.CodeType)]
    return found


def body(
    crops_in, stem_weight, middle_weight, expand_weight, stem_gain, stem_bias, middle_gain,
    middle_bias, expand_gain, expand_bias, hidden_weight, hidden_gain, hidden_bias, embed_weight,
    sub_sizes, crop_order, pair_index,
):
    nb, crops, area, half = crops_in.shape
    n = lax.axis_size("dp")
    rows = crops * area
    mid = stem_weight.shape[1]
    hid = hidden_weight.shape[1]
    width = embed_weight.shape[1]
    count = crop_order.shape[1]
    subs = sub_sizes.shape[1]
    long = conv_rows(crops)
    tall = long + 2 * (WIDE + 1) * crops

    def line(v):
        return v.reshape(1, -1)

    env = dict(
        x=crops_in.transpose(0, 2, 1, 3).reshape(nb, rows, half),
        ws=stem_weight,
        wm=middle_weight,
        we=expand_weight,
        wh=hidden_weight,
        w2=embed_weight,
        stem_gain=line(stem_gain),
        stem_bias=line(stem_bias),
        middle_gain=line(middle_gain),
        middle_bias=line(middle_bias),
        expand_gain=line(expand_gain),
        expand_bias=line(expand_bias),
        hidden_gain=line(hidden_gain),
        hidden_bias=line(hidden_bias),
        sizes=sub_sizes,
        order=crop_order.reshape(nb, 1, count),
        pairs=pair_index.transpose(0, 2, 1),
    )
    table = dict(
        wsp=((half, mid), BF16),
        spre=((nb, rows, mid), BF16),
        sst=((nb, 2, mid), F32),
        ao=((nb, tall, mid), BF16),
        ap=((nb, tall, mid), BF16),
        ss=((nb, rows, mid), BF16),
        sr=((nb, rows, mid), BF16),
        sm=((nb, 2, mid), F32),
        sbuf=((nb, n, 2, mid), F32),
        mpre=((nb, rows, mid), BF16),
        mst=((nb, 2, mid), F32),
        mo=((nb, rows, mid), BF16),
        mp=((nb, rows, mid), BF16),
        mm=((nb, 2, mid), F32),
        mbuf=((nb, n, 2, mid), F32),
        wep=((mid, half), BF16),
        ef=((1, rows, 256), F32),
        em=((1, 2, 256), F32),
        esend=((nb, 2, half), F32),
        ebuf=((nb, n, 2, half), F32),
        epre=((nb, rows, half), BF16),
        est=((nb, 2, half), F32),
        po=((nb, crops, half), BF16),
        pp=((nb, crops, half), BF16),
        hpre=((nb * crops, hid), F32),
        hm=((nb, 2, hid), F32),
        hbuf=((nb, n, 2, hid), F32),
        hst=((nb, 2, hid), F32),
        hact=((nb * crops, hid), BF16),
        pe=((nb, crops, width), F32),
        pr=((nb, crops, width), F32),
        em2=((nb, 2, crops // 2, width), F32),
        gath=((nb, n, 2, crops // 2, width), F32),
        member=((nb, count, width), F32),
        cent=((nb, count, width), F32),
        wgrad=((count, width), F32),
        cov=((nb * subs, width, width), F32),
        loss=((1, width), F32),
        ed=((nb * crops, width), BF16),
        gemb=((hid, width), BF16),
        hbm=((nb, 2, hid), F32),
        hbb=((n, nb, 2, hid), F32),
        hgrad=((2, hid), F32),
        hd=((nb * crops, hid), BF16),
        pgs=((nb * crops, half), BF16),
        pgr=((nb * crops, half), BF16),
        ghid=((2 * half, hid), BF16),
        pg=((nb, crops, half), F32),
        sg=((nb, rows, half), BF16),
        ebm=((nb, 2, half), F32),
        ebt=((2, half), F32),
        ebb=((nb, n, 2, half), F32),
        egrad=((2, half), F32),
        xd=((nb, rows, half), BF16),
        mgs=((nb, rows, mid), BF16),
        mgr=((nb, rows, mid), BF16),
        mg=((nb, rows, mid), F32),
        gxs=((mid, half), BF16),
        gexp=((2 * mid, half), BF16),
        mdg=((nb, tall, mid), BF16),
        mdt=((mid, nb * long), BF16),
        mgf=((nb, rows, mid), F32),
        mbm=((nb, 2, mid), F32),
        mbb=((nb, n, 2, mid), F32),
        mgrad=((2, mid), F32),
        ags=((nb, rows, mid), BF16),
        agr=((nb, rows, mid), BF16),
        ag=((nb, rows, mid), F32),
        gmida=((6 * mid, mid), BF16),
        gmidb=((6 * mid, mid), BF16),
        gmidc=((6 * mid, mid), BF16),
        sgf=((nb, rows, mid), F32),
        sbm=((nb, 2, mid), F32),
        sbb=((nb, n, 2, mid), F32),
        sgrad=((2, mid), F32),
        sd=((nb, rows, mid), BF16),
        sdp=((nb, rows, mid), BF16),
        gss=((half, mid), BF16),
        gstem=((2 * half, mid), BF16),
        gcrops=((nb, rows, half), BF16),
    )
    pair = (2,)
    pairs = (nb, 2)
    sems = dict(
        sem_sw=pair, sem_sp=pairs, sem_ss=pairs, sem_sa=pairs, sem_ms=pairs, sem_ma=pairs,
        sem_ew=pair, sem_es=pairs, sem_ep=pairs, sem_hs=pairs, sem_he=pairs, sem_hg=pairs,
        sem_hx=pairs, sem_hb=pair, sem_hp=pair, sem_eb=pairs, sem_mg=pairs, sem_gx=pair,
        sem_mb=pairs, sem_ag=pairs, sem_sb=pairs, sem_sd=pairs, sem_gs=pair,
    )
    phases = [
        stem_forward, middle_forward, expand_forward, hidden_forward, whiten, hidden_backward,
        expand_backward, middle_backward, stem_backward, crops_backward,
    ]
    block = n == 16
    final = set(GRADS) | {"loss", "gcrops", "sgrad", "mgrad", "egrad", "hgrad"}
    shared = {}
    if block:
        shared = dict(
            xd="epre", mgs="ss", ags="ss", agr="sr", mgf="mg", ag="mg", sgf="mg", sd="mo",
            sdp="mp", gcrops="sg",
        )
        groups = [phases + [whole_step]]
        final -= set(GRADS)
        for name in GRADS:
            tall, cols = table[name][0]
            table[name + "_t"] = table[name]
            table[name + "_1"] = ((2, tall // 4, cols), BF16)
            table[name + "_2"] = ((2, tall // 8, cols), BF16)
            table[name + "_3"] = ((2, 3, tall // 32, cols), BF16)
            sems["sem_" + name] = (2, 7, 2)
            final.add(name + "_t")
    else:
        groups = [[phase] for phase in phases]

    vmem = pl.BlockSpec(memory_space=pltpu.VMEM)
    smem = pl.BlockSpec(memory_space=pltpu.SMEM)
    hbm = pl.BlockSpec(memory_space=pl.ANY)
    used = [names_of(group + [norm_slopes, norm_terms]) for group in groups]
    for number, group in enumerate(groups):
        later = final.union(*used[number + 1 :])
        here = used[number]
        reads = [name for name in env if name in here]
        made = [name for name in table if name in here and name not in env]
        sem_names = [name for name in sems if name in here]
        own = [name for name in made if name not in shared]
        bases = {shared[name] for name in made if name in shared and name in later}
        outs = [name for name in own if name in later or name in bases]
        scratch = [name for name in own if name not in outs]
        names = reads + outs + scratch + sem_names
        remote = bool(sem_names)

        def kernel(*refs, group=group, names=names, remote=remote):
            c = Ctx(n, remote, remote)
            g = types.SimpleNamespace(**dict(zip(names, refs)))
            for name, base in shared.items():
                setattr(g, name, getattr(g, base))
            if block:
                whole_step(g, c)
            else:
                group[0](g, c).alone(nb)

        params = dict(vmem_limit_bytes=62 * 2**20)
        if remote:
            params.update(collective_id=number, has_side_effects=True)
        results = pl.pallas_call(
            kernel,
            out_shape=[jax.ShapeDtypeStruct(*table[name]) for name in outs],
            in_specs=[smem if name == "sizes" else vmem for name in reads],
            out_specs=[hbm if name[-2:] == "_t" else vmem for name in outs],
            scratch_shapes=[pltpu.VMEM(*table[name]) for name in scratch]
            + [DMA(sems[name]) for name in sem_names],
            compiler_params=pltpu.CompilerParams(**params),
            name=group[-1].__name__,
        )(*[env[name] for name in reads])
        env.update(zip(outs, results))

    for name, base in shared.items():
        if name in final:
            env[name] = env[base]
    if block:
        grads = {name: env[name + "_t"].astype(F32) for name in GRADS}
    else:
        grads = dict(zip(GRADS, lax.psum([env[name] for name in GRADS], "dp")))
        grads = {name: value.astype(F32) for name, value in grads.items()}
    gexp = grads["gexp"].reshape(2, mid, half).transpose(1, 0, 2).reshape(mid, 2 * half)
    gmid = jnp.concatenate([grads[name] for name in GRADS[3:6]], axis=0)
    field = env["gcrops"].astype(F32).reshape(nb, area, crops, half).transpose(0, 2, 1, 3)
    return (
        env["loss"][0, 0],
        field,
        grads["gstem"],
        gmid.reshape(9, 2 * mid, mid),
        gexp,
        env["sgrad"][1],
        env["sgrad"][0],
        env["mgrad"][1],
        env["mgrad"][0],
        env["egrad"][1],
        env["egrad"][0],
        grads["ghid"],
        env["hgrad"][1],
        env["hgrad"][0],
        grads["gemb"],
    )


def solution(mesh):
    return jax.shard_map(
        body,
        mesh=mesh,
        in_specs=(
            P(None, "dp", None, "chan"),
            P(None, "chan"),
            P(None, None, "chan"),
            P("chan", None),
            P("chan"),
            P("chan"),
            P("chan"),
            P("chan"),
            P("chan"),
            P("chan"),
            P(None, "chan"),
            P("chan"),
            P("chan"),
            P("chan", None),
            P(),
            P(),
            P(),
        ),
        out_specs=(
            P(),
            P(None, "dp", None, "chan"),
            P(None, "chan"),
            P(None, None, "chan"),
            P("chan", None),
            P("chan"),
            P("chan"),
            P("chan"),
            P("chan"),
            P("chan"),
            P("chan"),
            P(None, "chan"),
            P("chan"),
            P("chan"),
            P("chan", None),
        ),
        check_vma=False,
    )
```

```python
import types

import jax
import jax.numpy as jnp
from jax import lax
from jax.experimental import pallas as pl
from jax.experimental.pallas import tpu as pltpu
from jax.sharding import PartitionSpec as P

SIDE = 7
AREA = SIDE * SIDE
WIDE = SIDE + 1
EPS_NORM = 1e-05
RIDGE = 0.5
LOSS_SCALE = 8192.0
HIGH = lax.Precision.HIGHEST
MESH = pl.DeviceIdType.MESH
F32 = jnp.float32
BF16 = jnp.bfloat16
DMA = pltpu.SemaphoreType.DMA


def nn(left, right):
    return jnp.dot(left, right, preferred_element_type=F32)


def nt(left, right, precision=None):
    return lax.dot_general(
        left, right, (((1,), (1,)), ((), ())), precision=precision, preferred_element_type=F32
    )


def tn(left, right, precision=None):
    return lax.dot_general(
        left, right, (((0,), (0,)), ((), ())), precision=precision, preferred_element_type=F32
    )


def sigmoid(values):
    return 0.5 * jnp.tanh(0.5 * values) + 0.5


def silu(values):
    return values * sigmoid(values)


def slope(values):
    part = sigmoid(values)
    return part * (1.0 + values * (1.0 - part))


def rows_at(start, size):
    return pl.ds(pl.multiple_of(start, size if size % 16 else 16), size)


class Ctx:
    def __init__(self, devices, partner, peers):
        self.n = devices
        self.p = lax.axis_index("dp")
        self.h = lax.axis_index("chan")
        self.o = 1 - self.h
        self.waits = 0
        self.loads = {}
        if partner or peers:
            barrier = pltpu.get_barrier_semaphore()
            if partner:
                pl.semaphore_signal(barrier, inc=1, device_id=(self.p, self.o), device_id_type=MESH)
                self.waits += 1
            if peers:

                def greet(d, carry):
                    pl.semaphore_signal(
                        barrier,
                        inc=1,
                        device_id=(lax.rem(self.p + d, self.n), self.h),
                        device_id_type=MESH,
                    )
                    return carry

                lax.fori_loop(1, self.n, greet, 0)
                self.waits += self.n - 1

    def ready(self):
        if self.waits:
            pl.semaphore_wait(pltpu.get_barrier_semaphore(), self.waits)
            self.waits = 0

    def load(self, name, index, src, dst, sem):
        self.loads[name, index] = pltpu.make_async_copy(src, dst, sem)
        self.loads[name, index].start()

    def loaded(self, name, index=0):
        copy = self.loads.pop((name, index), None)
        if copy is not None:
            copy.wait()

    def half(self, which, size):
        return pl.ds(pl.multiple_of(which * size, size), size)

    def partner(self, src, dst, sems):
        return pltpu.make_async_remote_copy(
            src_ref=src,
            dst_ref=dst,
            send_sem=sems.at[0],
            recv_sem=sems.at[1],
            device_id=(self.p, self.o),
            device_id_type=MESH,
        )

    def spread(self, src, dst, sems):
        def one(d, carry):
            pltpu.make_async_remote_copy(
                src_ref=src,
                dst_ref=dst,
                send_sem=sems.at[0],
                recv_sem=sems.at[1],
                device_id=(lax.rem(self.p + d, self.n), self.h),
                device_id_type=MESH,
            ).start()
            return carry

        lax.fori_loop(1, self.n, one, 0)

    def take(self, blocks, sems, which):
        pltpu.make_async_copy(blocks, blocks, sems.at[which]).wait()


class Phase:
    def __init__(self, pre, post, begin=None, arrive=None, end=None, **more):
        nothing = lambda *_: None
        self.pre, self.post = pre, post
        self.begin, self.arrive, self.end = begin or nothing, arrive or nothing, end or nothing
        self.__dict__.update(more)

    def alone(self, nb):
        self.begin()
        for step in (self.pre, self.post, self.arrive):
            for mb in range(nb):
                step(mb)
        self.end()


def each(count, body):
    lax.fori_loop(0, count, lambda i, c: (body(i), c)[1], 0)


def local_moments(ref, mb, rows, chunk, cols, out):
    lanes = 256
    for lo in range(0, cols, lanes):
        at = pl.ds(lo, lanes)

        def add(i, total):
            part = ref[mb, rows_at(i * chunk, chunk), at]
            return total + jnp.sum(part.reshape(-1, 8, lanes), axis=0)

        total = lax.fori_loop(0, rows // chunk, add, jnp.zeros((8, lanes), F32))
        mean = jnp.sum(total, axis=0, keepdims=True) * (1.0 / rows)

        def square(i, total):
            part = ref[mb, rows_at(i * chunk, chunk), at] - mean
            return total + jnp.sum((part * part).reshape(-1, 8, lanes), axis=0)

        total = lax.fori_loop(0, rows // chunk, square, jnp.zeros((8, lanes), F32))
        out[mb, 0:1, at] = mean
        out[mb, 1:2, at] = jnp.sum(total, axis=0, keepdims=True)


def joint_moments(parts, rows):
    n = parts.shape[0]
    mean = jnp.sum(parts, axis=0)[0:1] * (1.0 / n)
    apart = parts[:, 0:1, :] - mean[None]
    squares = jnp.sum(parts, axis=0)[1:2] + rows * jnp.sum(apart * apart, axis=0)
    return mean, lax.rsqrt(squares * (1.0 / (n * rows)) + EPS_NORM)


def stem_forward(g, c):
    nb, rows, half = g.x.shape
    crops = rows // AREA
    mid = g.ws.shape[1]

    def swap():
        return c.partner(g.ws.at[c.half(c.o, half)], g.wsp, g.sem_sw)

    def give(mb):
        return c.partner(g.ss.at[mb], g.sr.at[mb], g.sem_sp.at[mb])

    def act(mb):
        return c.partner(g.ao.at[mb], g.ap.at[mb], g.sem_sa.at[mb])

    def begin():
        g.ao[...] = jnp.zeros(g.ao.shape, BF16)
        c.loaded("ws")
        c.ready()
        swap().start()
        for mb in range(nb):
            c.loaded("x", mb)
            g.sown[mb] = nn(g.x[mb], g.ws[c.half(c.h, half), :])
        swap().wait_recv()
        for mb in range(nb):
            g.ss[mb] = nn(g.x[mb], g.wsp[...]).astype(BF16)
            give(mb).start()

    def pre(mb):
        give(mb).wait_recv()
        g.ef[0] = g.sown[mb] + g.sr[mb].astype(F32)
        local_moments(g.ef, 0, rows, 7 * crops, mid, g.em)
        g.spre[mb] = g.ef[0].astype(BF16)
        g.sm[mb] = g.em[0]
        g.sbuf[mb, c.p] = g.sm[mb]
        c.spread(g.sm.at[mb], g.sbuf.at[mb, c.p], g.sem_ss.at[mb])

    def post(mb):
        c.take(g.sbuf.at[mb, pl.ds(0, c.n - 1)], g.sem_ss.at[mb], 1)
        mean, scale = joint_moments(g.sbuf[mb], float(rows))
        g.sst[mb, 0:1] = mean
        g.sst[mb, 1:2] = scale
        gain = scale * g.stem_gain[...]
        bias = g.stem_bias[...] - mean * gain
        for i in range(SIDE):
            post = g.spre[mb, pl.ds(i * SIDE * crops, SIDE * crops)].astype(F32) * gain + bias
            g.ao[mb, pl.ds((WIDE + 1 + WIDE * i) * crops, SIDE * crops)] = silu(post).astype(BF16)
        act(mb).start()

    def end():
        swap().wait_send()
        for mb in range(nb):
            give(mb).wait_send()
            act(mb).wait_send()
            c.take(g.sbuf.at[mb, pl.ds(0, c.n - 1)], g.sem_ss.at[mb], 0)

    return Phase(pre, post, begin, lambda mb: act(mb).wait_recv(), end)


def conv_rows(crops):
    return SIDE * WIDE * crops


def middle_forward(g, c):
    nb, rows, mid = g.mpre.shape
    crops = rows // AREA
    long = conv_rows(crops)

    def act(mb):
        return c.partner(g.mo.at[mb], g.mp.at[mb], g.sem_ma.at[mb])

    def pre(mb):
        if mb == 0:
            c.loaded("wm")
        total = None
        for tap in range(9):
            at = pl.ds((WIDE * (tap // 3) + tap % 3) * crops, long)
            part = nn(g.ao[mb, at], g.wm[tap, c.half(c.h, mid), :])
            total = part if total is None else total + part
            total = total + nn(g.ap[mb, at], g.wm[tap, c.half(c.o, mid), :])
        for i in range(SIDE):
            g.ef[0, pl.ds(i * SIDE * crops, SIDE * crops)] = total[
                i * WIDE * crops : (i * WIDE + SIDE) * crops
            ]
        local_moments(g.ef, 0, rows, 7 * crops, mid, g.em)
        g.mpre[mb] = g.ef[0].astype(BF16)
        g.mm[mb] = g.em[0]
        g.mbuf[mb, c.p] = g.mm[mb]
        c.spread(g.mm.at[mb], g.mbuf.at[mb, c.p], g.sem_ms.at[mb])

    def post(mb):
        c.take(g.mbuf.at[mb, pl.ds(0, c.n - 1)], g.sem_ms.at[mb], 1)
        mean, scale = joint_moments(g.mbuf[mb], float(rows))
        g.mst[mb, 0:1] = mean
        g.mst[mb, 1:2] = scale
        gain = scale * g.middle_gain[...]
        bias = g.middle_bias[...] - mean * gain
        for i in range(SIDE):
            at = pl.ds(i * SIDE * crops, SIDE * crops)
            g.mo[mb, at] = silu(g.mpre[mb, at].astype(F32) * gain + bias).astype(BF16)
        act(mb).start()

    def end():
        for mb in range(nb):
            act(mb).wait_send()
            c.take(g.mbuf.at[mb, pl.ds(0, c.n - 1)], g.sem_ms.at[mb], 0)

    return Phase(pre, post, c.ready, lambda mb: act(mb).wait_recv(), end)


def expand_forward(g, c):
    nb, rows, half = g.x.shape
    crops = rows // AREA
    lanes = 256

    def swap():
        return c.partner(g.we.at[:, c.half(c.o, half)], g.wep, g.sem_ew)

    def pool(mb):
        return c.partner(g.po.at[mb], g.pp.at[mb], g.sem_ep.at[mb])

    def early():
        c.loaded("we")
        c.ready()
        swap().start()

    def begin():
        early()
        swap().wait_recv()

    def pre(mb):
        for k in range(half // lanes):
            cols = pl.ds(k * lanes, lanes)
            own = g.we[:, pl.ds(pl.multiple_of(c.h * half + k * lanes, lanes), lanes)]
            g.ef[0] = nn(g.mo[mb], own) + nn(g.mp[mb], g.wep[:, cols])
            local_moments(g.ef, 0, rows, 7 * crops, lanes, g.em)
            g.epre[mb, :, cols] = g.ef[0].astype(BF16)
            g.esend[mb, :, cols] = g.em[0]
        g.ebuf[mb, c.p] = g.esend[mb]
        c.spread(g.esend.at[mb], g.ebuf.at[mb, c.p], g.sem_es.at[mb])

    def post(mb):
        c.take(g.ebuf.at[mb, pl.ds(0, c.n - 1)], g.sem_es.at[mb], 1)
        mean, scale = joint_moments(g.ebuf[mb], float(rows))
        g.est[mb, 0:1] = mean
        g.est[mb, 1:2] = scale
        for lo in range(0, half, lanes):
            cols = pl.ds(lo, lanes)
            gain = g.est[mb, 1:2, cols] * g.expand_gain[:, cols]
            bias = g.expand_bias[:, cols] - g.est[mb, 0:1, cols] * gain

            def pixels(i, total):
                for j in range(SIDE):
                    at = rows_at((i * SIDE + j) * crops, crops)
                    summed = g.epre[mb, at, cols].astype(F32) * gain + bias
                    summed = summed + g.x[mb, at, cols].astype(F32)
                    total = total + silu(summed)
                return total

            total = lax.fori_loop(0, SIDE, pixels, jnp.zeros((crops, lanes), F32))
            g.po[mb, :, cols] = (total * (1.0 / AREA)).astype(BF16)
        pool(mb).start()

    def end():
        swap().wait_send()
        for mb in range(nb):
            pool(mb).wait_send()
            c.take(g.ebuf.at[mb, pl.ds(0, c.n - 1)], g.sem_es.at[mb], 0)

    return Phase(
        pre, post, begin, lambda mb: pool(mb).wait_recv(), end, early=early,
        weights=lambda: swap().wait_recv(),
    )


def hidden_forward(g, c):
    nb, crops, half = g.po.shape
    part = crops // 2

    def trade(mb):
        return c.partner(g.pe.at[mb], g.pr.at[mb], g.sem_he.at[mb])

    def swap(mb):
        where = g.gath.at[mb, :, c.h]
        return c.partner(where, where, g.sem_hx.at[mb])

    def others(mb):
        return g.gath.at[mb, pl.ds(0, c.n - 1), c.h]

    def pre(mb):
        if mb == 0:
            c.loaded("wh")
        value = nn(g.po[mb], g.wh[c.half(c.h, half), :]) + nn(g.pp[mb], g.wh[c.half(c.o, half), :])
        g.hall[mb, c.p] = value.astype(BF16)
        mean = jnp.mean(value, axis=0, keepdims=True)
        g.hm[mb, 0:1] = mean
        g.hm[mb, 1:2] = jnp.sum((value - mean) * (value - mean), axis=0, keepdims=True)
        g.hbuf[mb, c.p] = g.hm[mb]
        c.spread(g.hm.at[mb], g.hbuf.at[mb, c.p], g.sem_hs.at[mb])

    def post(mb):
        c.take(g.hbuf.at[mb, pl.ds(0, c.n - 1)], g.sem_hs.at[mb], 1)
        mean, scale = joint_moments(g.hbuf[mb], float(crops))
        g.hst[mb, 0:1] = mean
        g.hst[mb, 1:2] = scale
        gain = scale * g.hidden_gain[...]
        bias = g.hidden_bias[...] - mean * gain
        act = silu(g.hall[mb, c.p].astype(F32) * gain + bias).astype(BF16)
        g.pe[mb] = nn(act, g.w2[...])
        trade(mb).start()

    def embed(mb):
        trade(mb).wait_recv()
        g.em2[mb] = (g.pe[mb] + g.pr[mb]).reshape(2, part, -1)
        g.gath[mb, c.p, c.h] = g.em2[mb, c.h]
        c.spread(g.em2.at[mb, c.h], g.gath.at[mb, c.p, c.h], g.sem_hg.at[mb])

    def mirror(mb):
        c.take(others(mb), g.sem_hg.at[mb], 1)
        swap(mb).start()

    def arrive(mb):
        swap(mb).wait_recv()

    def share(mb):
        g.pall[mb, c.p] = g.po[mb]
        c.spread(g.hall.at[mb, c.p], g.hall.at[mb, c.p], g.sem_hh.at[mb])

    def share_pooled(mb):
        c.spread(g.pall.at[mb, c.p], g.pall.at[mb, c.p], g.sem_pa.at[mb])

    def rows_in(mb):
        c.take(g.hall.at[mb, pl.ds(0, c.n - 1)], g.sem_hh.at[mb], 1)

    def pooled_swap():
        return c.partner(g.pall, g.qall, g.sem_pq)

    def pooled_in():
        for mb in range(nb):
            c.take(g.pall.at[mb, pl.ds(0, c.n - 1)], g.sem_pa.at[mb], 1)
        pooled_swap().start()

    def end():
        pooled_swap().wait_send()
        for mb in range(nb):
            c.take(g.hall.at[mb, pl.ds(0, c.n - 1)], g.sem_hh.at[mb], 0)
            c.take(g.pall.at[mb, pl.ds(0, c.n - 1)], g.sem_pa.at[mb], 0)
            trade(mb).wait_send()
            swap(mb).wait_send()
            c.take(g.hbuf.at[mb, pl.ds(0, c.n - 1)], g.sem_hs.at[mb], 0)
            c.take(others(mb), g.sem_hg.at[mb], 0)

    def all_arrive(mb):
        if mb == 0:
            for step in (embed, mirror, share, share_pooled, arrive, rows_in):
                for k in range(nb):
                    step(k)
            pooled_in()
            pooled_swap().wait_recv()

    return Phase(
        pre, post, c.ready, all_arrive, end, embed=embed, mirror=mirror, landed=arrive,
        share=share, share_pooled=share_pooled, rows_in=rows_in, pooled_in=pooled_in,
        pooled_swap=pooled_swap,
    )


def panel_steps(panel, start, lane, level):
    shape = panel.shape
    scaled = jnp.zeros(shape, F32)

    def wide(part):
        return jnp.broadcast_to(part, shape)

    for i in range(0, 8, 2):
        j = start + i
        one, two = lane == j, lane == j + 1
        c1, c2 = wide(panel[:, :, j : j + 1]), wide(panel[:, :, j + 1 : j + 2])
        r1, r2 = wide(panel[:, i : i + 1, :]), wide(panel[:, i + 1 : i + 2, :])
        a, b, d = wide(c1[:, i : i + 1]), wide(c1[:, i + 1 : i + 2]), wide(c2[:, i + 1 : i + 2])
        first = 1.0 / a
        second = a / (a * d - b * b)
        ratio = b * first
        r2 = r2 - ratio * r1
        m1 = jnp.where(one, 1.0, jnp.where(two, 0.0, r1))
        m2 = jnp.where(one, -ratio, jnp.where(two, 1.0, r2))
        l1 = c1 * first
        l2 = (c2 - l1 * b) * second
        cleared = jnp.where(jnp.logical_or(one, two), 0.0, panel)
        new = jnp.where(one, -ratio, r2)
        scaled = jnp.where(level == i, panel * first, jnp.where(level == i + 1, new * second, scaled))
        below = cleared - l1 * m1 - l2 * m2
        panel = jnp.where(level > i + 1, below, jnp.where(level == i + 1, new, panel))
    return panel, scaled


def eliminate(cov):
    total, width = cov.shape[0], cov.shape[1]
    pack = 8 * total
    side = -(-pack // width) * width
    lane = lax.broadcasted_iota(jnp.int32, (1, 1, width), 2)
    level = lax.broadcasted_iota(jnp.int32, (1, 8, width), 1)
    which = lax.broadcasted_iota(jnp.int32, (1, side), 1) // 8

    def product(left, right):
        return jnp.dot(left, right, precision=HIGH, preferred_element_type=F32)

    panel = cov[:, 0:8, :]
    for start in range(0, width, 8):
        panel, scaled = panel_steps(panel, start, lane, level)
        cov[:, start : start + 8, :] = panel
        after = start + 8
        if after == width:
            break
        inside = lane - start
        unit = jnp.where(inside == level, 1.0, 0.0)
        rows = jnp.where(jnp.logical_and(inside >= level, inside < 8), unit, panel)
        rows = rows.reshape(pack, width)
        scaled = scaled.reshape(pack, width)
        if side > pack:
            blank = jnp.zeros((side - pack, width), F32)
            rows = jnp.concatenate([rows, blank], axis=0)
            scaled = jnp.concatenate([scaled, blank], axis=0)
        flipped = scaled.T
        kept = jnp.logical_or(lane[0] < start, lane[0] >= after)
        near = flipped[after : after + 8]
        near = jnp.concatenate([jnp.where(which == k, near, 0.0) for k in range(total)], axis=0)
        change = product(near, rows).reshape(total, 8, width)
        panel = jnp.where(kept[None], cov[:, after : after + 8, :], 0.0) - change
        if after + 8 == width:
            continue
        far = flipped[after + 8 :]
        for k in range(total):
            change = product(jnp.where(which == k, far, 0.0), rows)
            cov[k, after + 8 :, :] = jnp.where(kept, cov[k, after + 8 :, :], 0.0) - change


def split(values):
    high = values.astype(BF16)
    return high, (values - high.astype(F32)).astype(BF16)


def fine(product, left, right):
    (a, b), (p, q) = split(left), split(right)
    return product(a, p) + (product(a, q) + product(b, p))


def whiten(g, c):
    nb, count = g.order.shape
    subs = g.sizes.shape[1]
    width = g.gath.shape[-1]
    pairs = g.pairs.shape[2]
    shape = (width, width)
    eye = lax.broadcasted_iota(jnp.int32, shape, 0) == lax.broadcasted_iota(jnp.int32, shape, 1)
    eye = eye.astype(F32)
    lower = lax.broadcasted_iota(jnp.int32, shape, 0) >= lax.broadcasted_iota(jnp.int32, shape, 1)
    lower = lower.astype(F32)
    strict = lower - eye
    crop_id = lax.broadcasted_iota(jnp.int32, (count, 1), 0)
    place = lax.broadcasted_iota(jnp.int32, (1, count), 1)

    def masks(mb):
        member = g.member[mb]
        return [(member == float(k)).astype(F32) for k in range(subs)]

    def apart(values, inside):
        return jnp.concatenate([values * mask for mask in inside], axis=1)

    def prepare(mb):
        end = jnp.int32(0)
        segment = jnp.zeros((1, count), F32)
        for k in range(subs - 1):
            end = end + g.sizes[mb, k]
            segment = segment + (place >= end).astype(F32)
        order = g.order[mb : mb + 1, :]
        member = jnp.sum(jnp.where(order == crop_id, segment, 0.0), axis=1, keepdims=True)
        g.member[mb] = jnp.broadcast_to(member, (count, width))
        embed = g.gath[mb].reshape(count, width)
        centred = jnp.zeros((count, width), F32)
        inside = masks(mb)
        for k in range(subs):
            centre = jnp.sum(embed * inside[k], axis=0, keepdims=True) / g.sizes[mb, k].astype(F32)
            centred = centred + (embed - centre) * inside[k]
        both = fine(tn, apart(centred, inside), centred)
        for k in range(subs):
            part = both[k * width : (k + 1) * width] / g.sizes[mb, k].astype(F32)
            g.cov[mb * subs + k] = part + RIDGE * eye
        g.cent[mb] = centred

    def factor_all():
        eliminate(g.cov)
        for k in range(nb * subs):
            inverse = g.cov[k]
            power = jnp.sum(inverse * eye, axis=1, keepdims=True)
            g.cov[k] = lax.rsqrt(power) * (inverse * strict + eye)
        g.loss[...] = jnp.zeros(g.loss.shape, F32)

    def rest(mb):
        inside = masks(mb)
        inverses = [g.cov[mb * subs + k] for k in range(subs)]
        white = fine(nt, apart(g.cent[mb], inside), jnp.concatenate(inverses, axis=1))
        power = jnp.sum(white * white, axis=1, keepdims=True)
        factor = lax.rsqrt(power + EPS_NORM)
        normed = white * factor
        first, second = g.pairs[mb, 0:1] == crop_id, g.pairs[mb, 1:2] == crop_id
        choose = (first.astype(F32) - second.astype(F32)).astype(BF16)
        high, rest_of = split(normed)
        differ = tn(choose, high) + tn(choose, rest_of)
        g.loss[...] = g.loss[...] + jnp.sum(differ * differ) * (1.0 / (pairs * nb))
        high, rest_of = split(differ)
        grad = (nn(choose, high) + nn(choose, rest_of)) * (2.0 * LOSS_SCALE / (nb * pairs))
        inner = jnp.sum(grad * white, axis=1, keepdims=True)
        grad = grad * factor - white * (factor * factor * factor * inner)
        low = tn(apart(grad, inside).astype(BF16), white.astype(BF16))
        sides, shift, shares = [], jnp.zeros((count, width), F32), []
        for k in range(subs):
            size = g.sizes[mb, k].astype(F32)
            part = low[k * width : (k + 1) * width]
            sides.append((part * lower + (part * strict).T).astype(BF16))
            shares.append(inside[k] / size)
            shift = shift + shares[k] * jnp.sum(grad * inside[k], axis=0, keepdims=True)
        shift = shift + nn(apart(white, shares).astype(BF16), jnp.concatenate(sides, axis=0))
        inverses = jnp.concatenate(inverses, axis=0).astype(BF16)
        delta = nn(apart(grad - shift, inside).astype(BF16), inverses)
        g.ed[mb] = delta.astype(BF16)

    def post(mb):
        if mb == 0:
            factor_all()
        rest(mb)

    return Phase(prepare, post)


def hidden_backward(g, c):
    nb, crops, half = g.pg.shape
    count, hid = c.n * crops, g.hall.shape[3]
    chunk = 256

    def give():
        return c.partner(g.pgs, g.pgr, g.sem_hp)

    def run():
        totals = jnp.zeros(g.hgrad.shape, F32)
        emb = jnp.zeros(g.gemb.shape, F32)
        for mb in range(nb):
            mean, scale = g.hst[mb, 0:1], g.hst[mb, 1:2]
            shift = -mean * scale
            one = two = jnp.zeros((1, hid), F32)
            for lo in range(0, count, chunk):
                at = pl.ds(lo, chunk)
                part = g.hall[mb, lo // crops : (lo + chunk) // crops].reshape(chunk, hid)
                normal = part.astype(F32) * scale + shift
                value = normal * g.hidden_gain[...] + g.hidden_bias[...]
                gate = sigmoid(value)
                delta = g.ed[mb, at]
                emb = emb + tn((value * gate).astype(BF16), delta)
                grad = nt(delta, g.w2[...]) * (gate * (1.0 + value * (1.0 - gate)))
                one = one + jnp.sum(grad, axis=0, keepdims=True)
                two = two + jnp.sum(grad * normal, axis=0, keepdims=True)
                g.hgf[at] = grad
            sums = jnp.concatenate([one, two], axis=0)
            totals = totals + sums
            a, b, k = norm_terms(g.hst, mb, g.hidden_gain[...], sums, float(count))
            for lo in range(0, count, chunk):
                at = pl.ds(lo, chunk)
                part = g.hall[mb, lo // crops : (lo + chunk) // crops].reshape(chunk, hid)
                g.hd[mb, at] = (g.hgf[at] * a + part.astype(F32) * b + k).astype(BF16)
        g.hgrad[...] = totals
        g.gemb[...] = emb
        c.ready()
        for mb in range(nb):
            own = g.hd[mb, rows_at(c.p * crops, crops)]
            g.pgs[mb] = nt(own, g.wh[c.half(c.o, half), :]).astype(BF16)
        give().start()

    def finish():
        for mb in range(nb):
            own = g.hd[mb, rows_at(c.p * crops, crops)]
            g.pg[mb] = nt(own, g.wh[c.half(c.h, half), :])
        give().wait_recv()
        g.pg[...] = (g.pg[...] + g.pgr[...].astype(F32)) * (1.0 / AREA)

    def weights():
        hd = g.hd[...].reshape(nb * count, hid)
        lanes = 256
        for which, rows in ((c.h, g.pall), (c.o, g.qall)):
            for lo in range(0, half, lanes):
                part = rows[:, :, :, lo : lo + lanes].reshape(nb * count, lanes)
                g.ghid[rows_at(which * half + lo, lanes), :] = tn(part, hd).astype(BF16)

    def end():
        give().wait_send()

    def pre(mb):
        if mb == 0:
            for step in (run, finish, weights):
                step()

    return Phase(pre, lambda mb: None, None, None, end, run=run, weights=weights, finish=finish)


def expand_backward(g, c):
    nb, rows, half = g.x.shape
    crops = rows // AREA
    mid = g.we.shape[0]
    lanes = 256
    total_rows = float(rows) * c.n

    def pre(mb):
        if mb == 0:
            g.egrad[...] = jnp.zeros(g.egrad.shape, F32)
        for lo in range(0, half, lanes):
            cols = pl.ds(lo, lanes)
            scale = g.est[mb, 1:2, cols]
            shift = -g.est[mb, 0:1, cols] * scale
            gain = g.expand_gain[:, cols]
            bias = g.expand_bias[:, cols]
            grad = g.pg[mb, :, cols]

            def pixels(i, carry):
                one, two = carry
                for j in range(SIDE):
                    at = rows_at((i * SIDE + j) * crops, crops)
                    normal = g.epre[mb, at, cols].astype(F32) * scale + shift
                    summed = normal * gain + bias + g.x[mb, at, cols].astype(F32)
                    part = grad * slope(summed)
                    g.sg[mb, at, cols] = part.astype(BF16)
                    one = one + part
                    two = two + part * normal
                return one, two

            zero = jnp.zeros((crops, lanes), F32)
            one, two = lax.fori_loop(0, SIDE, pixels, (zero, zero))
            g.ebm[mb, 0:1, cols] = jnp.sum(one, axis=0, keepdims=True)
            g.ebm[mb, 1:2, cols] = jnp.sum(two, axis=0, keepdims=True)
        g.ebb[mb, c.p] = g.ebm[mb]
        c.spread(g.ebm.at[mb], g.ebb.at[mb, c.p], g.sem_eb.at[mb])

    def give(mb):
        return c.partner(g.mgs.at[mb], g.mgr.at[mb], g.sem_mg.at[mb])

    def swap():
        return c.partner(g.gxs, g.gexp.at[c.half(c.h, mid)], g.sem_gx)

    def post(mb):
        c.take(g.ebb.at[mb, pl.ds(0, c.n - 1)], g.sem_eb.at[mb], 1)
        g.ebt[...] = jnp.sum(g.ebb[mb], axis=0)
        g.egrad[...] = g.egrad[...] + g.ebt[...]
        for lo in range(0, half, lanes):
            cols = pl.ds(lo, lanes)
            scale = g.est[mb, 1:2, cols]
            gain = g.expand_gain[:, cols] * scale
            slant = gain * g.ebt[1:2, cols] * (-1.0 / total_rows)
            base = gain * g.ebt[0:1, cols] * (-1.0 / total_rows)
            base = base - slant * scale * g.est[mb, 0:1, cols]
            slant = slant * scale

            def pixels(i, carry):
                for j in range(SIDE):
                    at = rows_at((i * SIDE + j) * crops, crops)
                    part = g.sg[mb, at, cols].astype(F32) * gain + base
                    part = part + g.epre[mb, at, cols].astype(F32) * slant
                    g.xd[mb, at, cols] = part.astype(BF16)
                return carry

            lax.fori_loop(0, SIDE, pixels, 0)
        g.mgs[mb] = nt(g.xd[mb], g.wep[...]).astype(BF16)
        give(mb).start()
        g.mg[mb] = nt(g.xd[mb], g.we[:, c.half(c.h, half)])

    def weights():
        xd = g.xd[...].reshape(nb * rows, half)
        g.gxs[...] = tn(g.mp[...].reshape(nb * rows, mid), xd).astype(BF16)
        swap().start()
        g.gexp[c.half(c.h, mid), :] = tn(g.mo[...].reshape(nb * rows, mid), xd).astype(BF16)

    def arrive(mb):
        give(mb).wait()
        g.mg[mb] = g.mg[mb] + g.mgr[mb].astype(F32)

    def weights_in():
        swap().wait_recv()

    def end():
        swap().wait_send()
        for mb in range(nb):
            c.take(g.ebb.at[mb, pl.ds(0, c.n - 1)], g.sem_eb.at[mb], 0)

    def end_alone():
        weights()
        weights_in()
        end()

    return Phase(
        pre, post, c.ready, arrive, end_alone, weights=weights, weights_in=weights_in, close=end
    )


def norm_slopes(c, mb, grad, pre, stats, gain, bias, sums, buf, sem, out):
    rows, mid = pre.shape[1:]
    scale = stats[mb, 1:2]
    shift = -stats[mb, 0:1] * scale
    chunk = rows // SIDE

    def image_row(i, carry):
        one, two = carry
        at = rows_at(i * chunk, chunk)
        normal = pre[mb, at].astype(F32) * scale + shift
        part = grad[mb, at] * slope(normal * gain[...] + bias[...])
        out[mb, at] = part
        one = one + jnp.sum(part.reshape(-1, 8, mid), axis=0)
        two = two + jnp.sum((part * normal).reshape(-1, 8, mid), axis=0)
        return one, two

    zero = jnp.zeros((8, mid), F32)
    one, two = lax.fori_loop(0, SIDE, image_row, (zero, zero))
    sums[mb, 0:1] = jnp.sum(one, axis=0, keepdims=True)
    sums[mb, 1:2] = jnp.sum(two, axis=0, keepdims=True)
    buf[mb, c.p] = sums[mb]
    c.spread(sums.at[mb], buf.at[mb, c.p], sem.at[mb])


def norm_terms(stats, mb, gain, sums, count):
    scale = stats[mb, 1:2]
    a = gain * scale
    slant = a * sums[1:2] * (-1.0 / count)
    k = a * sums[0:1] * (-1.0 / count) - slant * scale * stats[mb, 0:1]
    return a, slant * scale, k


def middle_backward(g, c):
    nb, rows, mid = g.mpre.shape
    crops = rows // AREA
    long = conv_rows(crops)
    count = float(rows) * c.n

    def begin():
        c.ready()
        g.mdg[...] = jnp.zeros(g.mdg.shape, BF16)
        g.mgrad[...] = jnp.zeros(g.mgrad.shape, F32)

    def pre(mb):
        norm_slopes(
            c, mb, g.mg, g.mpre, g.mst, g.middle_gain, g.middle_bias, g.mbm, g.mbb,
            g.sem_mb, g.mgf,
        )

    def give(mb):
        return c.partner(g.ags.at[mb], g.agr.at[mb], g.sem_ag.at[mb])

    def delta(mb):
        c.take(g.mbb.at[mb, pl.ds(0, c.n - 1)], g.sem_mb.at[mb], 1)
        sums = jnp.sum(g.mbb[mb], axis=0)
        g.mgrad[...] = g.mgrad[...] + sums
        a, b, k = norm_terms(g.mst, mb, g.middle_gain[...], sums, count)
        for i in range(SIDE):
            at = pl.ds(i * SIDE * crops, SIDE * crops)
            part = g.mgf[mb, at] * a + g.mpre[mb, at].astype(F32) * b + k
            g.mdg[mb, pl.ds((WIDE + 1 + WIDE * i) * crops, SIDE * crops)] = part.astype(BF16)
        g.mdt[:, mb * long : (mb + 1) * long] = g.mdg[mb, pl.ds((WIDE + 1) * crops, long)].T

    def spread(mb):
        for which, place in ((c.o, 0), (c.h, 1)):
            total = None
            for tap in range(9):
                at = pl.ds((WIDE * (2 - tap // 3) + 2 - tap % 3) * crops, long)
                part = nt(g.mdg[mb, at], g.wm[tap, c.half(which, mid), :])
                total = part if total is None else total + part
            for i in range(SIDE):
                at = pl.ds(i * SIDE * crops, SIDE * crops)
                part = total[i * WIDE * crops : (i * WIDE + SIDE) * crops]
                if place == 0:
                    g.ags[mb, at] = part.astype(BF16)
                else:
                    g.ag[mb, at] = part
            if place == 0:
                give(mb).start()

    def weights(out, first, taps):
        def one(i):
            tap = first + i
            at = pl.ds(pl.multiple_of((WIDE * (tap // 3) + tap % 3) * crops, crops), long)
            for act, which in ((g.ao, c.h), (g.ap, c.o)):
                field = jnp.concatenate([act[mb, at] for mb in range(nb)], axis=0)
                part = nn(g.mdt[...], field)
                out[c.half(2 * i + which, mid), :] = part.T.astype(BF16)

        each(taps, one)

    def arrive(mb):
        give(mb).wait()
        g.ag[mb] = g.ag[mb] + g.agr[mb].astype(F32)

    def end():
        for mb in range(nb):
            c.take(g.mbb.at[mb, pl.ds(0, c.n - 1)], g.sem_mb.at[mb], 0)

    def post(mb):
        delta(mb)
        spread(mb)

    def all_weights():
        weights(g.gmida, 0, 3)
        weights(g.gmidb, 3, 3)
        weights(g.gmidc, 6, 3)

    def end_alone():
        all_weights()
        end()

    return Phase(
        pre, post, begin, arrive, end_alone, delta=delta, spread=spread, weights=weights, close=end
    )


def stem_backward(g, c):
    nb, rows, mid = g.spre.shape
    half = g.x.shape[2]
    crops = rows // AREA
    count = float(rows) * c.n

    def begin():
        c.ready()
        g.sgrad[...] = jnp.zeros(g.sgrad.shape, F32)

    def pre(mb):
        norm_slopes(
            c, mb, g.ag, g.spre, g.sst, g.stem_gain, g.stem_bias, g.sbm, g.sbb,
            g.sem_sb, g.sgf,
        )

    def give(mb):
        return c.partner(g.sd.at[mb], g.sdp.at[mb], g.sem_sd.at[mb])

    def swap():
        return c.partner(g.gss, g.gstem.at[c.half(c.h, half)], g.sem_gs)

    def post(mb):
        c.take(g.sbb.at[mb, pl.ds(0, c.n - 1)], g.sem_sb.at[mb], 1)
        sums = jnp.sum(g.sbb[mb], axis=0)
        g.sgrad[...] = g.sgrad[...] + sums
        a, b, k = norm_terms(g.sst, mb, g.stem_gain[...], sums, count)
        for i in range(SIDE):
            at = pl.ds(i * SIDE * crops, SIDE * crops)
            g.sd[mb, at] = (g.sgf[mb, at] * a + g.spre[mb, at].astype(F32) * b + k).astype(BF16)
        give(mb).start()

    def weights():
        lanes = 256
        sd = g.sd[...].reshape(nb * rows, mid)
        sdp = g.sdp[...].reshape(nb * rows, mid)
        for lo in range(0, half, lanes):
            field = g.x[:, :, lo : lo + lanes].reshape(nb * rows, lanes)
            g.gss[lo : lo + lanes] = tn(field, sdp).astype(BF16)
            own = rows_at(c.h * half + lo, lanes)
            g.gstem[own, :] = tn(field, sd).astype(BF16)
        swap().start()

    def weights_in():
        swap().wait_recv()

    def end():
        swap().wait_send()
        for mb in range(nb):
            give(mb).wait_send()
            c.take(g.sbb.at[mb, pl.ds(0, c.n - 1)], g.sem_sb.at[mb], 0)

    def end_alone():
        weights()
        weights_in()
        end()

    return Phase(
        pre, post, begin, lambda mb: give(mb).wait_recv(), end_alone, weights=weights,
        weights_in=weights_in, close=end,
    )


def crops_backward(g, c):
    half = g.wsp.shape[0]

    def pre(mb):
        part = nt(g.sd[mb], g.ws[c.half(c.h, half), :]) + nt(g.sdp[mb], g.wsp[...])
        g.gcrops[mb] = (part + g.sg[mb].astype(F32)).astype(BF16)

    return Phase(pre, lambda mb: None)


class Total:
    def __init__(self, c, local, place, one, two, three, sems):
        self.done = 0
        self.c, self.local, self.place, self.sems = c, local, place, sems
        self.one, self.two, self.three = one, two, three
        self.long = local.shape[0] // 2
        x, y, self.z = c.p % 2, (c.p // 2) % 2, c.p // 4
        step_x, step_y = c.p + 1 - 2 * x, c.p + 2 - 4 * y
        self.ways = ((x, step_x, y, step_y), (y, step_y, x, step_x))
        self.half, self.quarter, self.piece = self.long // 2, self.long // 4, self.long // 16

    def copy(self, stream, step, src, dst, device):
        return pltpu.make_async_remote_copy(
            src_ref=src,
            dst_ref=dst,
            send_sem=self.sems.at[stream, step, 0],
            recv_sem=self.sems.at[stream, step, 1],
            device_id=(device, self.c.h),
            device_id_type=MESH,
        )

    def at(self, start, size):
        return pl.ds(pl.multiple_of(start, 16), size)

    def start(self, step):
        for stream in range(2):
            b1, d1, b2, d2 = self.ways[stream]
            base = stream * self.long
            kept = base + b1 * self.half
            core = kept + b2 * self.quarter
            if step == 0:
                src = self.local.at[self.at(base + (1 - b1) * self.half, self.half)]
                self.copy(stream, step, src, self.one.at[stream], d1).start()
            elif step == 1:
                src = self.one.at[stream, self.at((1 - b2) * self.quarter, self.quarter)]
                self.copy(stream, step, src, self.two.at[stream], d2).start()
            elif step == 4:
                self.keep(stream, core).wait()
                src = self.place(stream, core, self.quarter)
                self.copy(stream, step, src, src, d2).start()
            elif step == 5:
                src = self.place(stream, kept, self.half)
                self.copy(stream, step, src, src, d1).start()
            else:
                if step == 3:
                    self.keep(stream, core).start()
                for d in range(1, 4):
                    other = (self.z + d) % 4
                    device = self.c.p + 4 * (other - self.z)
                    if step == 2:
                        src = self.two.at[stream, self.at(other * self.piece, self.piece)]
                        dst = self.three.at[stream, 3 - d]
                    else:
                        src = self.two.at[stream, self.at(self.z * self.piece, self.piece)]
                        dst = self.place(stream, core + self.z * self.piece, self.piece)
                    self.copy(stream, step, src, dst, device).start()

    def keep(self, stream, core):
        piece = self.at(self.z * self.piece, self.piece)
        place = self.place(stream, core + self.z * self.piece, self.piece)
        return pltpu.make_async_copy(self.two.at[stream, piece], place, self.sems.at[stream, 6, 0])

    def wait(self, stream, step, which):
        blocks = {0: self.one, 1: self.two, 2: self.three, 3: self.three, 4: self.two, 5: self.one}
        self.c.take(blocks[step].at[stream], self.sems.at[stream, step], which)

    def take(self, step):
        for stream in range(2):
            self.wait(stream, step, 1)
            b1, d1, b2, d2 = self.ways[stream]
            kept = stream * self.long + b1 * self.half
            core = kept + b2 * self.quarter
            one, two, three = self.one.at[stream], self.two.at[stream], self.three.at[stream]
            if step == 0:
                self.add(one, 0, [(one, 0), (self.local, kept)], self.half)
            elif step == 1:
                self.add(two, 0, [(two, 0), (one, b2 * self.quarter)], self.quarter)
            elif step == 2:
                terms = [(two, self.z * self.piece)] + [(three.at[d], 0) for d in range(3)]
                self.add(two, self.z * self.piece, terms, self.piece)

    def add(self, out, start, terms, size):
        chunk = 16

        def one(i):
            total = None
            for ref, begin in terms:
                value = ref[rows_at(begin + i * chunk, chunk), :].astype(F32)
                total = value if total is None else total + value
            out[rows_at(start + i * chunk, chunk), :] = total.astype(BF16)

        each(size // chunk, one)

    def step(self):
        self.take(self.done)
        self.done += 1
        if self.done < 6:
            self.start(self.done)

    def close(self):
        for stream in range(2):
            for step in range(6):
                self.wait(stream, step, 0)


def whole_step(g, c):
    nb, half = g.x.shape[0], g.x.shape[2]
    mid = g.ws.shape[1]
    c.load("ws", 0, g.ws_in, g.ws, g.sem_in.at[0])
    for mb in range(nb):
        c.load("x", mb, g.x_in.at[mb], g.x.at[mb], g.sem_in.at[4 + mb])
    c.load("we", 0, g.we_in, g.we, g.sem_in.at[1])
    c.load("wm", 0, g.wm_in, g.wm, g.sem_in.at[2])
    c.load("wh", 0, g.wh_in, g.wh, g.sem_in.at[3])
    stem, middle, expand = stem_forward(g, c), middle_forward(g, c), expand_forward(g, c)
    hidden, white, hback = hidden_forward(g, c), whiten(g, c), hidden_backward(g, c)
    eback, mback, sback = expand_backward(g, c), middle_backward(g, c), stem_backward(g, c)
    field = crops_backward(g, c)

    def chain(first, second):
        first.post(0)
        for mb in range(1, nb):
            first.post(mb)
            first.arrive(mb - 1)
            second.pre(mb - 1)
        first.arrive(nb - 1)
        second.pre(nb - 1)

    stem.begin()
    expand.early()
    for mb in range(nb):
        stem.pre(mb)
    chain(stem, middle)
    expand.weights()
    chain(middle, expand)
    chain(expand, hidden)
    for step in (hidden.post, hidden.embed, hidden.mirror, hidden.share, hidden.share_pooled):
        for mb in range(nb):
            step(mb)
    for mb in range(nb):
        hidden.landed(mb)
        white.pre(mb)
    for mb in range(nb):
        white.post(mb)
    for phase in (stem, middle, expand):
        phase.end()

    def rows_of(out, first):
        return lambda stream, start, size: out.at[pl.ds(pl.multiple_of(first + start, 16), size)]

    def halves_of(out):
        def place(stream, start, size):
            at = pl.ds(pl.multiple_of(start - stream * mid, 16), size)
            return out.at[at, pl.ds(stream * half, half)]

        return place

    third = g.gmida.shape[0]
    exp = Total(c, g.gexp, halves_of(g.gexp_t), g.gexp_1, g.gexp_2, g.gexp_3, g.sem_gexp)
    place = [rows_of(g.gmid_t, i * third) for i in range(3)]
    one = Total(c, g.gmida, place[0], g.gmida_1, g.gmida_2, g.gmida_3, g.sem_gmida)
    two = Total(c, g.gmidb, place[1], g.gmidb_1, g.gmidb_2, g.gmidb_3, g.sem_gmidb)
    three = Total(c, g.gmidc, place[2], g.gmidc_1, g.gmidc_2, g.gmidc_3, g.sem_gmidc)
    last = Total(c, g.gstem, rows_of(g.gstem_t, 0), g.gstem_1, g.gstem_2, g.gstem_3, g.sem_gstem)

    for mb in range(nb):
        hidden.rows_in(mb)
    hback.run()
    hback.finish()
    for mb in range(nb):
        eback.pre(mb)
    mback.begin()
    sback.begin()
    hidden.pooled_in()
    eback.post(0)
    eback.post(1)
    eback.arrive(0)
    mback.pre(0)
    eback.post(2)
    eback.arrive(1)
    mback.pre(1)
    eback.weights()
    eback.arrive(2)
    mback.pre(2)
    eback.weights_in()
    exp.start(0)
    for mb in range(nb):
        mback.delta(mb)
    mback.weights(g.gmida, 0, 3)
    one.start(0)
    exp.step()
    mback.weights(g.gmidb, 3, 3)
    two.start(0)
    exp.step()
    one.step()
    mback.weights(g.gmidc, 6, 3)
    three.start(0)
    exp.step()
    two.step()
    mback.spread(0)
    one.step()
    exp.step()
    mback.spread(1)
    three.step()
    two.step()
    mback.arrive(0)
    sback.pre(0)
    mback.spread(2)
    one.step()
    exp.step()
    mback.arrive(1)
    sback.pre(1)
    three.step()
    two.step()
    mback.arrive(2)
    sback.pre(2)
    one.step()
    for mb in range(nb):
        sback.post(mb)
    three.step()
    exp.step()
    for mb in range(nb):
        sback.arrive(mb)
    sback.weights()
    two.step()
    one.step()
    sback.weights_in()
    last.start(0)
    hidden.pooled_swap().wait_recv()
    three.step()
    field.pre(0)
    one.step()
    two.step()
    field.pre(1)
    last.step()
    three.step()
    hback.weights()
    keep = pltpu.make_async_copy(g.ghid, g.ghid_t, g.sem_in.at[0])
    keep.start()
    last.step()
    field.pre(2)
    two.step()
    three.step()
    last.step()
    last.step()
    last.step()
    last.step()
    hidden.end()
    hback.end()
    for phase in (eback, mback, sback):
        phase.close()
    for total in (exp, one, two, three, last):
        total.close()
    keep.wait()


GRADS = ("gexp", "gmida", "gmidb", "gmidc", "gstem")


def names_of(functions):
    found, codes = set(), [function.__code__ for function in functions]
    while codes:
        code = codes.pop()
        found |= set(code.co_names)
        codes += [value for value in code.co_consts if isinstance(value, types.CodeType)]
    return found


def body(
    crops_in, stem_weight, middle_weight, expand_weight, stem_gain, stem_bias, middle_gain,
    middle_bias, expand_gain, expand_bias, hidden_weight, hidden_gain, hidden_bias, embed_weight,
    sub_sizes, crop_order, pair_index,
):
    nb, crops, area, half = crops_in.shape
    n = lax.axis_size("dp")
    rows = crops * area
    mid = stem_weight.shape[1]
    hid = hidden_weight.shape[1]
    width = embed_weight.shape[1]
    count = crop_order.shape[1]
    subs = sub_sizes.shape[1]
    long = conv_rows(crops)
    tall = long + 2 * (WIDE + 1) * crops

    def line(v):
        return v.reshape(1, -1)

    env = dict(
        x=crops_in.transpose(0, 2, 1, 3).reshape(nb, rows, half),
        ws=stem_weight,
        wm=middle_weight,
        we=expand_weight,
        wh=hidden_weight,
        w2=embed_weight,
        stem_gain=line(stem_gain),
        stem_bias=line(stem_bias),
        middle_gain=line(middle_gain),
        middle_bias=line(middle_bias),
        expand_gain=line(expand_gain),
        expand_bias=line(expand_bias),
        hidden_gain=line(hidden_gain),
        hidden_bias=line(hidden_bias),
        sizes=sub_sizes,
        order=crop_order,
        pairs=pair_index.transpose(0, 2, 1),
    )
    table = dict(
        wsp=((half, mid), BF16),
        spre=((nb, rows, mid), BF16),
        sst=((nb, 2, mid), F32),
        ao=((nb, tall, mid), BF16),
        ap=((nb, tall, mid), BF16),
        ss=((nb, rows, mid), BF16),
        sr=((nb, rows, mid), BF16),
        sm=((nb, 2, mid), F32),
        sbuf=((nb, n, 2, mid), F32),
        mpre=((nb, rows, mid), BF16),
        mst=((nb, 2, mid), F32),
        mo=((nb, rows, mid), BF16),
        mp=((nb, rows, mid), BF16),
        mm=((nb, 2, mid), F32),
        mbuf=((nb, n, 2, mid), F32),
        wep=((mid, half), BF16),
        ef=((1, rows, 256), F32),
        em=((1, 2, 256), F32),
        esend=((nb, 2, half), F32),
        ebuf=((nb, n, 2, half), F32),
        epre=((nb, rows, half), BF16),
        est=((nb, 2, half), F32),
        po=((nb, crops, half), BF16),
        pp=((nb, crops, half), BF16),
        hall=((nb, n, crops, hid), BF16),
        pall=((nb, n, crops, half), BF16),
        qall=((nb, n, crops, half), BF16),
        sown=((nb, rows, mid), F32),
        hm=((nb, 2, hid), F32),
        hbuf=((nb, n, 2, hid), F32),
        hst=((nb, 2, hid), F32),
        pe=((nb, crops, width), F32),
        pr=((nb, crops, width), F32),
        em2=((nb, 2, crops // 2, width), F32),
        gath=((nb, n, 2, crops // 2, width), F32),
        member=((nb, count, width), F32),
        cent=((nb, count, width), F32),
        cov=((nb * subs, width, width), F32),
        loss=((1, width), F32),
        ed=((nb, count, width), BF16),
        gemb=((hid, width), F32),
        hgf=((count, hid), F32),
        hgrad=((2, hid), F32),
        hd=((nb, count, hid), BF16),
        pgs=((nb, crops, half), BF16),
        pgr=((nb, crops, half), BF16),
        ghid=((2 * half, hid), BF16),
        pg=((nb, crops, half), F32),
        sg=((nb, rows, half), BF16),
        ebm=((nb, 2, half), F32),
        ebt=((2, half), F32),
        ebb=((nb, n, 2, half), F32),
        egrad=((2, half), F32),
        xd=((nb, rows, half), BF16),
        mgs=((nb, rows, mid), BF16),
        mgr=((nb, rows, mid), BF16),
        mg=((nb, rows, mid), F32),
        gxs=((mid, half), BF16),
        gexp=((2 * mid, half), BF16),
        mdg=((nb, tall, mid), BF16),
        mdt=((mid, nb * long), BF16),
        mgf=((nb, rows, mid), F32),
        mbm=((nb, 2, mid), F32),
        mbb=((nb, n, 2, mid), F32),
        mgrad=((2, mid), F32),
        ags=((nb, rows, mid), BF16),
        agr=((nb, rows, mid), BF16),
        ag=((nb, rows, mid), F32),
        gmida=((6 * mid, mid), BF16),
        gmidb=((6 * mid, mid), BF16),
        gmidc=((6 * mid, mid), BF16),
        sgf=((nb, rows, mid), F32),
        sbm=((nb, 2, mid), F32),
        sbb=((nb, n, 2, mid), F32),
        sgrad=((2, mid), F32),
        sd=((nb, rows, mid), BF16),
        sdp=((nb, rows, mid), BF16),
        gss=((half, mid), BF16),
        gstem=((2 * half, mid), BF16),
        gcrops=((nb, rows, half), BF16),
    )
    pair = (2,)
    pairs = (nb, 2)
    sems = dict(
        sem_sw=pair, sem_sp=pairs, sem_ss=pairs, sem_sa=pairs, sem_ms=pairs, sem_ma=pairs,
        sem_ew=pair, sem_es=pairs, sem_ep=pairs, sem_hs=pairs, sem_he=pairs, sem_hg=pairs,
        sem_hx=pairs, sem_hh=pairs, sem_pa=pairs, sem_pq=pair, sem_hp=pair, sem_eb=pairs, sem_mg=pairs, sem_gx=pair,
        sem_mb=pairs, sem_ag=pairs, sem_sb=pairs, sem_sd=pairs, sem_gs=pair,
    )
    phases = [
        stem_forward, middle_forward, expand_forward, hidden_forward, whiten, hidden_backward,
        expand_backward, middle_backward, stem_backward, crops_backward,
    ]
    block = n == 16
    final = set(GRADS) | {"loss", "gcrops", "sgrad", "mgrad", "egrad", "hgrad", "ghid", "gemb"}
    shared = {}
    if block:
        shared = dict(
            xd="epre", mgs="ss", ags="ss", agr="sr", mgf="mg", ag="mg", sgf="mg", sd="mo",
            sdp="mp", gcrops="sg", sown="mg", gxs="wep", ghid="wh",
        )
        groups = [phases + [whole_step]]
        final -= set(GRADS) | {"ghid"}
        whole = dict(
            gexp_t=((mid, 2 * half), BF16), gmid_t=((18 * mid, mid), BF16),
            gstem_t=((2 * half, mid), BF16), ghid_t=((2 * half, hid), BF16),
        )
        final |= set(whole)
        table.update(whole)
        for name in GRADS:
            tall, cols = table[name][0]
            table[name + "_1"] = ((2, tall // 4, cols), BF16)
            table[name + "_2"] = ((2, tall // 8, cols), BF16)
            table[name + "_3"] = ((2, 3, tall // 32, cols), BF16)
            sems["sem_" + name] = (2, 7, 2)
        sems.update(sem_in=(4 + nb,))
        for name in ("x", "ws", "wm", "we", "wh"):
            env[name + "_in"] = env.pop(name)
            table[name] = (env[name + "_in"].shape, BF16)
    else:
        groups = [[phase] for phase in phases]

    vmem = pl.BlockSpec(memory_space=pltpu.VMEM)
    smem = pl.BlockSpec(memory_space=pltpu.SMEM)
    hbm = pl.BlockSpec(memory_space=pl.ANY)
    used = [names_of(group + [norm_slopes, norm_terms]) for group in groups]
    for number, group in enumerate(groups):
        later = final.union(*used[number + 1 :])
        here = used[number]
        reads = [name for name in env if name in here]
        made = [name for name in table if name in here and name not in env]
        sem_names = [name for name in sems if name in here]
        own = [name for name in made if name not in shared]
        bases = {shared[name] for name in made if name in shared and name in later}
        outs = [name for name in own if name in later or name in bases]
        scratch = [name for name in own if name not in outs]
        names = reads + outs + scratch + sem_names
        remote = bool(sem_names)

        def kernel(*refs, group=group, names=names, remote=remote):
            c = Ctx(n, remote, remote)
            g = types.SimpleNamespace(**dict(zip(names, refs)))
            for name, base in shared.items():
                setattr(g, name, getattr(g, base))
            if block:
                whole_step(g, c)
            else:
                group[0](g, c).alone(nb)

        params = dict(vmem_limit_bytes=62 * 2**20)
        if remote:
            params.update(collective_id=number, has_side_effects=True)
        results = pl.pallas_call(
            kernel,
            out_shape=[jax.ShapeDtypeStruct(*table[name]) for name in outs],
            in_specs=[
                smem if name == "sizes" else hbm if name[-3:] == "_in" else vmem for name in reads
            ],
            out_specs=[hbm if name[-2:] == "_t" else vmem for name in outs],
            scratch_shapes=[pltpu.VMEM(*table[name]) for name in scratch]
            + [DMA(sems[name]) for name in sem_names],
            compiler_params=pltpu.CompilerParams(**params),
            name=group[-1].__name__,
        )(*[env[name] for name in reads])
        env.update(zip(outs, results))

    for name, base in shared.items():
        if name in final:
            env[name] = env[base]
    if block:
        gexp, gmid, gstem = env["gexp_t"], env["gmid_t"], env["gstem_t"]
        ghid = env["ghid_t"]
    else:
        gexp, *gmid, gstem = lax.psum([env[name] for name in GRADS], "dp")
        gexp = gexp.reshape(2, mid, half).transpose(1, 0, 2).reshape(mid, 2 * half)
        gmid = jnp.concatenate(gmid, axis=0)
        ghid = env["ghid"]
    field = env["gcrops"].astype(F32).reshape(nb, area, crops, half).transpose(0, 2, 1, 3)
    return (
        env["loss"][0, 0],
        field,
        gstem.astype(F32),
        gmid.astype(F32).reshape(9, 2 * mid, mid),
        gexp.astype(F32),
        env["sgrad"][1],
        env["sgrad"][0],
        env["mgrad"][1],
        env["mgrad"][0],
        env["egrad"][1],
        env["egrad"][0],
        ghid.astype(F32),
        env["hgrad"][1],
        env["hgrad"][0],
        env["gemb"],
    )


def solution(mesh):
    return jax.shard_map(
        body,
        mesh=mesh,
        in_specs=(
            P(None, "dp", None, "chan"),
            P(None, "chan"),
            P(None, None, "chan"),
            P("chan", None),
            P("chan"),
            P("chan"),
            P("chan"),
            P("chan"),
            P("chan"),
            P("chan"),
            P(None, "chan"),
            P("chan"),
            P("chan"),
            P("chan", None),
            P(),
            P(),
            P(),
        ),
        out_specs=(
            P(),
            P(None, "dp", None, "chan"),
            P(None, "chan"),
            P(None, None, "chan"),
            P("chan", None),
            P("chan"),
            P("chan"),
            P("chan"),
            P("chan"),
            P("chan"),
            P("chan"),
            P(None, "chan"),
            P("chan"),
            P("chan"),
            P("chan", None),
        ),
        check_vma=False,
    )
```

```python
import types

import jax
import jax.numpy as jnp
from jax import lax
from jax.experimental import pallas as pl
from jax.experimental.pallas import tpu as pltpu
from jax.sharding import PartitionSpec as P

SIDE = 7
AREA = SIDE * SIDE
WIDE = SIDE + 1
EPS_NORM = 1e-05
RIDGE = 0.5
LOSS_SCALE = 8192.0
HIGH = lax.Precision.HIGHEST
MESH = pl.DeviceIdType.MESH
F32 = jnp.float32
BF16 = jnp.bfloat16
DMA = pltpu.SemaphoreType.DMA


def nn(left, right):
    return jnp.dot(left, right, preferred_element_type=F32)


def nt(left, right, precision=None):
    return lax.dot_general(
        left, right, (((1,), (1,)), ((), ())), precision=precision, preferred_element_type=F32
    )


def tn(left, right, precision=None):
    return lax.dot_general(
        left, right, (((0,), (0,)), ((), ())), precision=precision, preferred_element_type=F32
    )


def sigmoid(values):
    return 0.5 * jnp.tanh(0.5 * values) + 0.5


def silu(values):
    return values * sigmoid(values)


def slope(values):
    part = sigmoid(values)
    return part * (1.0 + values * (1.0 - part))


def rows_at(start, size):
    return pl.ds(pl.multiple_of(start, size if size % 16 else 16), size)


class Ctx:
    def __init__(self, devices, partner, peers):
        self.n = devices
        self.p = lax.axis_index("dp")
        self.h = lax.axis_index("chan")
        self.o = 1 - self.h
        self.waits = 0
        self.loads = {}
        if partner or peers:
            barrier = pltpu.get_barrier_semaphore()
            if partner:
                pl.semaphore_signal(barrier, inc=1, device_id=(self.p, self.o), device_id_type=MESH)
                self.waits += 1
            if peers:

                def greet(d, carry):
                    pl.semaphore_signal(
                        barrier,
                        inc=1,
                        device_id=(lax.rem(self.p + d, self.n), self.h),
                        device_id_type=MESH,
                    )
                    return carry

                lax.fori_loop(1, self.n, greet, 0)
                self.waits += self.n - 1

    def ready(self):
        if self.waits:
            pl.semaphore_wait(pltpu.get_barrier_semaphore(), self.waits)
            self.waits = 0

    def load(self, name, index, src, dst, sem):
        self.loads[name, index] = pltpu.make_async_copy(src, dst, sem)
        self.loads[name, index].start()

    def loaded(self, name, index=0):
        copy = self.loads.pop((name, index), None)
        if copy is not None:
            copy.wait()

    def half(self, which, size):
        return pl.ds(pl.multiple_of(which * size, size), size)

    def partner(self, src, dst, sems):
        return pltpu.make_async_remote_copy(
            src_ref=src,
            dst_ref=dst,
            send_sem=sems.at[0],
            recv_sem=sems.at[1],
            device_id=(self.p, self.o),
            device_id_type=MESH,
        )

    def spread(self, src, dst, sems):
        def one(d, carry):
            pltpu.make_async_remote_copy(
                src_ref=src,
                dst_ref=dst,
                send_sem=sems.at[0],
                recv_sem=sems.at[1],
                device_id=(lax.rem(self.p + d, self.n), self.h),
                device_id_type=MESH,
            ).start()
            return carry

        lax.fori_loop(1, self.n, one, 0)

    def relay(self, ref, sems, stage):
        q, z = self.p % 4, self.p // 4
        x, y = q % 2, q // 2
        if stage == 0:
            blocks = [(ref.at[q, z], self.p + 4 * ((z + d) % 4 - z)) for d in range(1, 4)]
        elif stage == 1:
            blocks = [(ref.at[q], self.p + 1 - 2 * x)]
        else:
            blocks = [(ref.at[pl.ds(2 * y, 2)], self.p + 2 - 4 * y)]
        return [
            pltpu.make_async_remote_copy(
                src_ref=block,
                dst_ref=block,
                send_sem=sems.at[stage, 0],
                recv_sem=sems.at[stage, 1],
                device_id=(device, self.h),
                device_id_type=MESH,
            )
            for block, device in blocks
        ]

    def relay_wait(self, ref, sems, stage, which):
        blocks = (ref.at[0, pl.ds(0, 3)], ref.at[0], ref.at[pl.ds(0, 2)])[stage]
        self.take(blocks, sems.at[stage], which)

    def take(self, blocks, sems, which):
        pltpu.make_async_copy(blocks, blocks, sems.at[which]).wait()


class Phase:
    def __init__(self, pre, post, begin=None, arrive=None, end=None, **more):
        nothing = lambda *_: None
        self.pre, self.post = pre, post
        self.begin, self.arrive, self.end = begin or nothing, arrive or nothing, end or nothing
        self.__dict__.update(more)

    def alone(self, nb):
        self.begin()
        for step in (self.pre, self.post, self.arrive):
            for mb in range(nb):
                step(mb)
        self.end()


def each(count, body):
    lax.fori_loop(0, count, lambda i, c: (body(i), c)[1], 0)


def local_moments(ref, mb, rows, chunk, cols, out):
    lanes = 256
    for lo in range(0, cols, lanes):
        at = pl.ds(lo, lanes)

        def add(i, total):
            part = ref[mb, rows_at(i * chunk, chunk), at]
            return total + jnp.sum(part.reshape(-1, 8, lanes), axis=0)

        total = lax.fori_loop(0, rows // chunk, add, jnp.zeros((8, lanes), F32))
        mean = jnp.sum(total, axis=0, keepdims=True) * (1.0 / rows)

        def square(i, total):
            part = ref[mb, rows_at(i * chunk, chunk), at] - mean
            return total + jnp.sum((part * part).reshape(-1, 8, lanes), axis=0)

        total = lax.fori_loop(0, rows // chunk, square, jnp.zeros((8, lanes), F32))
        out[mb, 0:1, at] = mean
        out[mb, 1:2, at] = jnp.sum(total, axis=0, keepdims=True)


def joint_moments(parts, rows):
    n = parts.shape[0]
    mean = jnp.sum(parts, axis=0)[0:1] * (1.0 / n)
    apart = parts[:, 0:1, :] - mean[None]
    squares = jnp.sum(parts, axis=0)[1:2] + rows * jnp.sum(apart * apart, axis=0)
    return mean, lax.rsqrt(squares * (1.0 / (n * rows)) + EPS_NORM)


def stem_forward(g, c):
    nb, rows, half = g.x.shape
    crops = rows // AREA
    mid = g.ws.shape[1]

    def swap():
        return c.partner(g.ws.at[c.half(c.o, half)], g.wsp, g.sem_sw)

    def give(mb):
        return c.partner(g.ss.at[mb], g.sr.at[mb], g.sem_sp.at[mb])

    def act(mb):
        return c.partner(g.ao.at[mb], g.ap.at[mb], g.sem_sa.at[mb])

    def begin():
        g.ao[...] = jnp.zeros(g.ao.shape, BF16)
        c.loaded("ws")
        c.ready()
        swap().start()
        for mb in range(nb):
            c.loaded("x", mb)
            g.sown[mb] = nn(g.x[mb], g.ws[c.half(c.h, half), :])
        swap().wait_recv()
        for mb in range(nb):
            g.ss[mb] = nn(g.x[mb], g.wsp[...]).astype(BF16)
            give(mb).start()

    def pre(mb):
        give(mb).wait_recv()
        g.ef[0] = g.sown[mb] + g.sr[mb].astype(F32)
        local_moments(g.ef, 0, rows, 7 * crops, mid, g.em)
        g.spre[mb] = g.ef[0].astype(BF16)
        g.sm[mb] = g.em[0]
        g.sbuf[mb, c.p] = g.sm[mb]
        c.spread(g.sm.at[mb], g.sbuf.at[mb, c.p], g.sem_ss.at[mb])

    def post(mb):
        c.take(g.sbuf.at[mb, pl.ds(0, c.n - 1)], g.sem_ss.at[mb], 1)
        mean, scale = joint_moments(g.sbuf[mb], float(rows))
        g.sst[mb, 0:1] = mean
        g.sst[mb, 1:2] = scale
        gain = scale * g.stem_gain[...]
        bias = g.stem_bias[...] - mean * gain
        for i in range(SIDE):
            post = g.spre[mb, pl.ds(i * SIDE * crops, SIDE * crops)].astype(F32) * gain + bias
            g.ao[mb, pl.ds((WIDE + 1 + WIDE * i) * crops, SIDE * crops)] = silu(post).astype(BF16)
        act(mb).start()

    def end():
        swap().wait_send()
        for mb in range(nb):
            give(mb).wait_send()
            act(mb).wait_send()
            c.take(g.sbuf.at[mb, pl.ds(0, c.n - 1)], g.sem_ss.at[mb], 0)

    return Phase(pre, post, begin, lambda mb: act(mb).wait_recv(), end)


def conv_rows(crops):
    return SIDE * WIDE * crops


def middle_forward(g, c):
    nb, rows, mid = g.mpre.shape
    crops = rows // AREA
    long = conv_rows(crops)

    def act(mb):
        return c.partner(g.mo.at[mb], g.mp.at[mb], g.sem_ma.at[mb])

    def pre(mb):
        if mb == 0:
            c.loaded("wm")
        total = None
        for tap in range(9):
            at = pl.ds((WIDE * (tap // 3) + tap % 3) * crops, long)
            part = nn(g.ao[mb, at], g.wm[tap, c.half(c.h, mid), :])
            total = part if total is None else total + part
            total = total + nn(g.ap[mb, at], g.wm[tap, c.half(c.o, mid), :])
        for i in range(SIDE):
            g.ef[0, pl.ds(i * SIDE * crops, SIDE * crops)] = total[
                i * WIDE * crops : (i * WIDE + SIDE) * crops
            ]
        local_moments(g.ef, 0, rows, 7 * crops, mid, g.em)
        g.mpre[mb] = g.ef[0].astype(BF16)
        g.mm[mb] = g.em[0]
        g.mbuf[mb, c.p] = g.mm[mb]
        c.spread(g.mm.at[mb], g.mbuf.at[mb, c.p], g.sem_ms.at[mb])

    def post(mb):
        c.take(g.mbuf.at[mb, pl.ds(0, c.n - 1)], g.sem_ms.at[mb], 1)
        mean, scale = joint_moments(g.mbuf[mb], float(rows))
        g.mst[mb, 0:1] = mean
        g.mst[mb, 1:2] = scale
        gain = scale * g.middle_gain[...]
        bias = g.middle_bias[...] - mean * gain
        for i in range(SIDE):
            at = pl.ds(i * SIDE * crops, SIDE * crops)
            g.mo[mb, at] = silu(g.mpre[mb, at].astype(F32) * gain + bias).astype(BF16)
        act(mb).start()

    def end():
        for mb in range(nb):
            act(mb).wait_send()
            c.take(g.mbuf.at[mb, pl.ds(0, c.n - 1)], g.sem_ms.at[mb], 0)

    return Phase(pre, post, c.ready, lambda mb: act(mb).wait_recv(), end)


def expand_forward(g, c):
    nb, rows, half = g.x.shape
    crops = rows // AREA
    lanes = 256

    def swap():
        return c.partner(g.we.at[:, c.half(c.o, half)], g.wep, g.sem_ew)

    def pool(mb):
        return c.partner(g.po.at[mb], g.pp.at[mb], g.sem_ep.at[mb])

    def early():
        c.loaded("we")
        c.ready()
        swap().start()

    def begin():
        early()
        swap().wait_recv()

    def pre(mb):
        for k in range(half // lanes):
            cols = pl.ds(k * lanes, lanes)
            own = g.we[:, pl.ds(pl.multiple_of(c.h * half + k * lanes, lanes), lanes)]
            g.ef[0] = nn(g.mo[mb], own) + nn(g.mp[mb], g.wep[:, cols])
            local_moments(g.ef, 0, rows, 7 * crops, lanes, g.em)
            g.epre[mb, :, cols] = g.ef[0].astype(BF16)
            g.esend[mb, :, cols] = g.em[0]
        g.ebuf[mb, c.p] = g.esend[mb]
        c.spread(g.esend.at[mb], g.ebuf.at[mb, c.p], g.sem_es.at[mb])

    def post(mb):
        c.take(g.ebuf.at[mb, pl.ds(0, c.n - 1)], g.sem_es.at[mb], 1)
        mean, scale = joint_moments(g.ebuf[mb], float(rows))
        g.est[mb, 0:1] = mean
        g.est[mb, 1:2] = scale
        for lo in range(0, half, lanes):
            cols = pl.ds(lo, lanes)
            gain = g.est[mb, 1:2, cols] * g.expand_gain[:, cols]
            bias = g.expand_bias[:, cols] - g.est[mb, 0:1, cols] * gain

            def pixels(i, total):
                for j in range(SIDE):
                    at = rows_at((i * SIDE + j) * crops, crops)
                    summed = g.epre[mb, at, cols].astype(F32) * gain + bias
                    summed = summed + g.x[mb, at, cols].astype(F32)
                    total = total + silu(summed)
                return total

            total = lax.fori_loop(0, SIDE, pixels, jnp.zeros((crops, lanes), F32))
            g.po[mb, :, cols] = (total * (1.0 / AREA)).astype(BF16)
        pool(mb).start()

    def end():
        swap().wait_send()
        for mb in range(nb):
            pool(mb).wait_send()
            c.take(g.ebuf.at[mb, pl.ds(0, c.n - 1)], g.sem_es.at[mb], 0)

    return Phase(
        pre, post, begin, lambda mb: pool(mb).wait_recv(), end, early=early,
        weights=lambda: swap().wait_recv(),
    )


def hidden_forward(g, c):
    nb, crops, half = g.po.shape
    part = crops // 2

    def trade(mb):
        return c.partner(g.pe.at[mb], g.pr.at[mb], g.sem_he.at[mb])

    def swap(mb):
        where = g.gath.at[mb, :, c.h]
        return c.partner(where, where, g.sem_hx.at[mb])

    def others(mb):
        return g.gath.at[mb, pl.ds(0, c.n - 1), c.h]

    def pre(mb):
        if mb == 0:
            c.loaded("wh")
        value = nn(g.po[mb], g.wh[c.half(c.h, half), :]) + nn(g.pp[mb], g.wh[c.half(c.o, half), :])
        g.hall[c.p % 4, c.p // 4, mb] = value.astype(BF16)
        mean = jnp.mean(value, axis=0, keepdims=True)
        g.hm[mb, 0:1] = mean
        g.hm[mb, 1:2] = jnp.sum((value - mean) * (value - mean), axis=0, keepdims=True)
        g.hbuf[mb, c.p] = g.hm[mb]
        c.spread(g.hm.at[mb], g.hbuf.at[mb, c.p], g.sem_hs.at[mb])

    def post(mb):
        c.take(g.hbuf.at[mb, pl.ds(0, c.n - 1)], g.sem_hs.at[mb], 1)
        mean, scale = joint_moments(g.hbuf[mb], float(crops))
        g.hst[mb, 0:1] = mean
        g.hst[mb, 1:2] = scale
        gain = scale * g.hidden_gain[...]
        bias = g.hidden_bias[...] - mean * gain
        act = silu(g.hall[c.p % 4, c.p // 4, mb].astype(F32) * gain + bias).astype(BF16)
        g.pe[mb] = nn(act, g.w2[...])
        trade(mb).start()

    def embed(mb):
        trade(mb).wait_recv()
        g.em2[mb] = (g.pe[mb] + g.pr[mb]).reshape(2, part, -1)
        g.gath[mb, c.p, c.h] = g.em2[mb, c.h]
        c.spread(g.em2.at[mb, c.h], g.gath.at[mb, c.p, c.h], g.sem_hg.at[mb])

    def mirror(mb):
        c.take(others(mb), g.sem_hg.at[mb], 1)
        swap(mb).start()

    def arrive(mb):
        swap(mb).wait_recv()

    def relay(name, stage):
        ref, sems = (g.hall, g.sem_hh) if name == "h" else (g.pall, g.sem_pa)
        if stage == 0 and name == "p":
            g.pall[c.p % 4, c.p // 4] = g.po[...]
        if stage > 0:
            c.relay_wait(ref, sems, stage - 1, 1)
        if stage < 3:
            for copy in c.relay(ref, sems, stage):
                copy.start()

    def direct(ref, sems):
        own = ref.at[c.p % 4, c.p // 4]
        c.spread(own, own, sems.at[0])
        for which in (1, 0):
            c.take(ref.at[pl.ds(0, 3)], sems.at[0], which)
            c.take(ref.at[0, pl.ds(0, c.n // 4 - 1)], sems.at[0], which)

    def pooled_swap():
        return c.partner(g.pall, g.qall, g.sem_pq)

    def end():
        pooled_swap().wait_send()
        for mb in range(nb):
            trade(mb).wait_send()
            swap(mb).wait_send()
            c.take(g.hbuf.at[mb, pl.ds(0, c.n - 1)], g.sem_hs.at[mb], 0)
            c.take(others(mb), g.sem_hg.at[mb], 0)

    def end_relay():
        for ref, sems in ((g.hall, g.sem_hh), (g.pall, g.sem_pa)):
            for stage in range(3):
                c.relay_wait(ref, sems, stage, 0)

    def all_arrive(mb):
        if mb == 0:
            for step in (embed, mirror, arrive):
                for k in range(nb):
                    step(k)
            g.pall[c.p % 4, c.p // 4] = g.po[...]
            direct(g.hall, g.sem_hh)
            direct(g.pall, g.sem_pa)
            pooled_swap().start()
            pooled_swap().wait_recv()

    return Phase(
        pre, post, c.ready, all_arrive, end, embed=embed, mirror=mirror, landed=arrive,
        relay=relay, pooled_swap=pooled_swap, end_relay=end_relay,
    )


def panel_steps(panel, start, lane, level):
    shape = panel.shape
    scaled = jnp.zeros(shape, F32)

    def wide(part):
        return jnp.broadcast_to(part, shape)

    for i in range(0, 8, 2):
        j = start + i
        one, two = lane == j, lane == j + 1
        c1, c2 = wide(panel[:, :, j : j + 1]), wide(panel[:, :, j + 1 : j + 2])
        r1, r2 = wide(panel[:, i : i + 1, :]), wide(panel[:, i + 1 : i + 2, :])
        a, b, d = wide(c1[:, i : i + 1]), wide(c1[:, i + 1 : i + 2]), wide(c2[:, i + 1 : i + 2])
        first = 1.0 / a
        second = a / (a * d - b * b)
        ratio = b * first
        r2 = r2 - ratio * r1
        m1 = jnp.where(one, 1.0, jnp.where(two, 0.0, r1))
        m2 = jnp.where(one, -ratio, jnp.where(two, 1.0, r2))
        l1 = c1 * first
        l2 = (c2 - l1 * b) * second
        cleared = jnp.where(jnp.logical_or(one, two), 0.0, panel)
        new = jnp.where(one, -ratio, r2)
        scaled = jnp.where(level == i, panel * first, jnp.where(level == i + 1, new * second, scaled))
        below = cleared - l1 * m1 - l2 * m2
        panel = jnp.where(level > i + 1, below, jnp.where(level == i + 1, new, panel))
    return panel, scaled


def eliminate(cov, between):
    total, width = cov.shape[0], cov.shape[1]
    pack = 8 * total
    side = -(-pack // width) * width
    lane = lax.broadcasted_iota(jnp.int32, (1, 1, width), 2)
    level = lax.broadcasted_iota(jnp.int32, (1, 8, width), 1)
    which = lax.broadcasted_iota(jnp.int32, (1, side), 1) // 8

    def product(left, right):
        return jnp.dot(left, right, precision=HIGH, preferred_element_type=F32)

    panel = cov[:, 0:8, :]
    for start in range(0, width, 8):
        between(start)
        panel, scaled = panel_steps(panel, start, lane, level)
        cov[:, start : start + 8, :] = panel
        after = start + 8
        if after == width:
            break
        inside = lane - start
        unit = jnp.where(inside == level, 1.0, 0.0)
        rows = jnp.where(jnp.logical_and(inside >= level, inside < 8), unit, panel)
        rows = rows.reshape(pack, width)
        scaled = scaled.reshape(pack, width)
        if side > pack:
            blank = jnp.zeros((side - pack, width), F32)
            rows = jnp.concatenate([rows, blank], axis=0)
            scaled = jnp.concatenate([scaled, blank], axis=0)
        flipped = scaled.T
        kept = jnp.logical_or(lane[0] < start, lane[0] >= after)
        near = flipped[after : after + 8]
        near = jnp.concatenate([jnp.where(which == k, near, 0.0) for k in range(total)], axis=0)
        change = product(near, rows).reshape(total, 8, width)
        panel = jnp.where(kept[None], cov[:, after : after + 8, :], 0.0) - change
        if after + 8 == width:
            continue
        far = flipped[after + 8 :]
        for k in range(total):
            change = product(jnp.where(which == k, far, 0.0), rows)
            cov[k, after + 8 :, :] = jnp.where(kept, cov[k, after + 8 :, :], 0.0) - change


def split(values):
    high = values.astype(BF16)
    return high, (values - high.astype(F32)).astype(BF16)


def fine(product, left, right):
    (a, b), (p, q) = split(left), split(right)
    return product(a, p) + (product(a, q) + product(b, p))


def whiten(g, c):
    nb, count = g.order.shape
    subs = g.sizes.shape[1]
    width = g.gath.shape[-1]
    pairs = g.pairs.shape[2]
    shape = (width, width)
    eye = lax.broadcasted_iota(jnp.int32, shape, 0) == lax.broadcasted_iota(jnp.int32, shape, 1)
    eye = eye.astype(F32)
    lower = lax.broadcasted_iota(jnp.int32, shape, 0) >= lax.broadcasted_iota(jnp.int32, shape, 1)
    lower = lower.astype(F32)
    strict = lower - eye
    crop_id = lax.broadcasted_iota(jnp.int32, (count, 1), 0)
    place = lax.broadcasted_iota(jnp.int32, (1, count), 1)

    def masks(mb):
        member = g.member[mb]
        return [(member == float(k)).astype(F32) for k in range(subs)]

    def apart(values, inside):
        return jnp.concatenate([values * mask for mask in inside], axis=1)

    def prepare(mb):
        end = jnp.int32(0)
        segment = jnp.zeros((1, count), F32)
        for k in range(subs - 1):
            end = end + g.sizes[mb, k]
            segment = segment + (place >= end).astype(F32)
        order = g.order[mb : mb + 1, :]
        member = jnp.sum(jnp.where(order == crop_id, segment, 0.0), axis=1, keepdims=True)
        g.member[mb] = jnp.broadcast_to(member, (count, width))
        embed = g.gath[mb].reshape(count, width)
        centred = jnp.zeros((count, width), F32)
        inside = masks(mb)
        for k in range(subs):
            centre = jnp.sum(embed * inside[k], axis=0, keepdims=True) / g.sizes[mb, k].astype(F32)
            centred = centred + (embed - centre) * inside[k]
        both = fine(tn, apart(centred, inside), centred)
        for k in range(subs):
            part = both[k * width : (k + 1) * width] / g.sizes[mb, k].astype(F32)
            g.cov[mb * subs + k] = part + RIDGE * eye
        g.cent[mb] = centred

    def factor_all(between):
        eliminate(g.cov, between)
        for k in range(nb * subs):
            inverse = g.cov[k]
            power = jnp.sum(inverse * eye, axis=1, keepdims=True)
            g.cov[k] = lax.rsqrt(power) * (inverse * strict + eye)
        g.loss[...] = jnp.zeros(g.loss.shape, F32)

    def rest(mb):
        inside = masks(mb)
        inverses = [g.cov[mb * subs + k] for k in range(subs)]
        white = fine(nt, apart(g.cent[mb], inside), jnp.concatenate(inverses, axis=1))
        power = jnp.sum(white * white, axis=1, keepdims=True)
        factor = lax.rsqrt(power + EPS_NORM)
        normed = white * factor
        first, second = g.pairs[mb, 0:1] == crop_id, g.pairs[mb, 1:2] == crop_id
        choose = (first.astype(F32) - second.astype(F32)).astype(BF16)
        high, rest_of = split(normed)
        differ = tn(choose, high) + tn(choose, rest_of)
        g.loss[...] = g.loss[...] + jnp.sum(differ * differ) * (1.0 / (pairs * nb))
        high, rest_of = split(differ)
        grad = (nn(choose, high) + nn(choose, rest_of)) * (2.0 * LOSS_SCALE / (nb * pairs))
        inner = jnp.sum(grad * white, axis=1, keepdims=True)
        grad = grad * factor - white * (factor * factor * factor * inner)
        low = tn(apart(grad, inside).astype(BF16), white.astype(BF16))
        sides, shift, shares = [], jnp.zeros((count, width), F32), []
        for k in range(subs):
            size = g.sizes[mb, k].astype(F32)
            part = low[k * width : (k + 1) * width]
            sides.append((part * lower + (part * strict).T).astype(BF16))
            shares.append(inside[k] / size)
            shift = shift + shares[k] * jnp.sum(grad * inside[k], axis=0, keepdims=True)
        shift = shift + nn(apart(white, shares).astype(BF16), jnp.concatenate(sides, axis=0))
        inverses = jnp.concatenate(inverses, axis=0).astype(BF16)
        delta = nn(apart(grad - shift, inside).astype(BF16), inverses)
        g.ed[mb] = delta.astype(BF16)

    def post(mb):
        if mb == 0:
            factor_all(lambda start: None)
        rest(mb)

    return Phase(prepare, post, factor_all=factor_all, rest=rest)


def hidden_backward(g, c):
    nb, crops, half = g.pg.shape
    count, hid = c.n * crops, g.hall.shape[4]
    chunk = 256

    def give():
        return c.partner(g.pgs, g.pgr, g.sem_hp)

    def rows_of(ref, mb, lo, size, cols):
        parts = []
        for z in range(lo // (4 * crops), (lo + size) // (4 * crops)):
            parts.append(ref[:, z, mb, :, cols].reshape(4 * crops, -1))
        return jnp.concatenate(parts, axis=0)

    def run():
        totals = jnp.zeros((2, hid), F32)
        emb = jnp.zeros(g.gemb.shape, F32)
        for mb in range(nb):
            mean, scale = g.hst[mb, 0:1], g.hst[mb, 1:2]
            shift = -mean * scale
            one = two = jnp.zeros((1, hid), F32)
            for lo in range(0, count, chunk):
                at = pl.ds(lo, chunk)
                part = rows_of(g.hall, mb, lo, chunk, slice(None))
                normal = part.astype(F32) * scale + shift
                value = normal * g.hidden_gain[...] + g.hidden_bias[...]
                gate = sigmoid(value)
                delta = g.ed[mb, at]
                emb = emb + tn((value * gate).astype(BF16), delta)
                grad = nt(delta, g.w2[...]) * (gate * (1.0 + value * (1.0 - gate)))
                one = one + jnp.sum(grad, axis=0, keepdims=True)
                two = two + jnp.sum(grad * normal, axis=0, keepdims=True)
                g.hgf[at] = grad
            sums = jnp.concatenate([one, two], axis=0)
            totals = totals + sums
            a, b, k = norm_terms(g.hst, mb, g.hidden_gain[...], sums, float(count))
            for lo in range(0, count, chunk):
                at = pl.ds(lo, chunk)
                part = rows_of(g.hall, mb, lo, chunk, slice(None))
                g.hd[mb, at] = (g.hgf[at] * a + part.astype(F32) * b + k).astype(BF16)
        g.hbias[...] = totals[0:1]
        g.hgain[...] = totals[1:2]
        g.gemb[...] = emb
        c.ready()
        for mb in range(nb):
            own = g.hd[mb, rows_at(c.p * crops, crops)]
            g.pgs[mb] = nt(own, g.wh[c.half(c.o, half), :]).astype(BF16)
        give().start()

    def finish():
        for mb in range(nb):
            own = g.hd[mb, rows_at(c.p * crops, crops)]
            g.pg[mb] = nt(own, g.wh[c.half(c.h, half), :])
        give().wait_recv()
        g.pg[...] = (g.pg[...] + g.pgr[...].astype(F32)) * (1.0 / AREA)

    def weights():
        hd = g.hd[...].reshape(nb * count, hid)
        lanes = 256
        for which, rows in ((c.h, g.pall), (c.o, g.qall)):
            for lo in range(0, half, lanes):
                part = [rows_of(rows, mb, 0, count, slice(lo, lo + lanes)) for mb in range(nb)]
                part = jnp.concatenate(part, axis=0)
                g.ghid[rows_at(which * half + lo, lanes), :] = tn(part, hd).astype(BF16)

    def end():
        give().wait_send()

    def pre(mb):
        if mb == 0:
            for step in (run, finish, weights):
                step()

    return Phase(pre, lambda mb: None, None, None, end, run=run, weights=weights, finish=finish)


def expand_backward(g, c):
    nb, rows, half = g.x.shape
    crops = rows // AREA
    mid = g.we.shape[0]
    lanes = 256
    total_rows = float(rows) * c.n

    def pre(mb):
        if mb == 0:
            g.egain[...] = jnp.zeros(g.egain.shape, F32)
            g.ebias[...] = jnp.zeros(g.ebias.shape, F32)
        for lo in range(0, half, lanes):
            cols = pl.ds(lo, lanes)
            scale = g.est[mb, 1:2, cols]
            shift = -g.est[mb, 0:1, cols] * scale
            gain = g.expand_gain[:, cols]
            bias = g.expand_bias[:, cols]
            grad = g.pg[mb, :, cols]

            def pixels(i, carry):
                one, two = carry
                for j in range(SIDE):
                    at = rows_at((i * SIDE + j) * crops, crops)
                    normal = g.epre[mb, at, cols].astype(F32) * scale + shift
                    summed = normal * gain + bias + g.x[mb, at, cols].astype(F32)
                    part = grad * slope(summed)
                    g.sg[mb, at, cols] = part.astype(BF16)
                    one = one + part
                    two = two + part * normal
                return one, two

            zero = jnp.zeros((crops, lanes), F32)
            one, two = lax.fori_loop(0, SIDE, pixels, (zero, zero))
            g.ebm[mb, 0:1, cols] = jnp.sum(one, axis=0, keepdims=True)
            g.ebm[mb, 1:2, cols] = jnp.sum(two, axis=0, keepdims=True)
        g.ebb[mb, c.p] = g.ebm[mb]
        c.spread(g.ebm.at[mb], g.ebb.at[mb, c.p], g.sem_eb.at[mb])

    def give(mb):
        return c.partner(g.mgs.at[mb], g.mgr.at[mb], g.sem_mg.at[mb])

    def swap():
        return c.partner(g.gxs, g.gexp.at[c.half(c.h, mid)], g.sem_gx)

    def post(mb):
        c.take(g.ebb.at[mb, pl.ds(0, c.n - 1)], g.sem_eb.at[mb], 1)
        g.ebt[...] = jnp.sum(g.ebb[mb], axis=0)
        g.ebias[...] = g.ebias[...] + g.ebt[0:1]
        g.egain[...] = g.egain[...] + g.ebt[1:2]
        for lo in range(0, half, lanes):
            cols = pl.ds(lo, lanes)
            scale = g.est[mb, 1:2, cols]
            gain = g.expand_gain[:, cols] * scale
            slant = gain * g.ebt[1:2, cols] * (-1.0 / total_rows)
            base = gain * g.ebt[0:1, cols] * (-1.0 / total_rows)
            base = base - slant * scale * g.est[mb, 0:1, cols]
            slant = slant * scale

            def pixels(i, carry):
                for j in range(SIDE):
                    at = rows_at((i * SIDE + j) * crops, crops)
                    part = g.sg[mb, at, cols].astype(F32) * gain + base
                    part = part + g.epre[mb, at, cols].astype(F32) * slant
                    g.xd[mb, at, cols] = part.astype(BF16)
                return carry

            lax.fori_loop(0, SIDE, pixels, 0)
        g.mgs[mb] = nt(g.xd[mb], g.wep[...]).astype(BF16)
        give(mb).start()
        g.mg[mb] = nt(g.xd[mb], g.we[:, c.half(c.h, half)])

    def weights():
        xd = g.xd[...].reshape(nb * rows, half)
        g.gxs[...] = tn(g.mp[...].reshape(nb * rows, mid), xd).astype(BF16)
        swap().start()
        g.gexp[c.half(c.h, mid), :] = tn(g.mo[...].reshape(nb * rows, mid), xd).astype(BF16)

    def arrive(mb):
        give(mb).wait()
        g.mg[mb] = g.mg[mb] + g.mgr[mb].astype(F32)

    def weights_in():
        swap().wait_recv()

    def end():
        swap().wait_send()
        for mb in range(nb):
            c.take(g.ebb.at[mb, pl.ds(0, c.n - 1)], g.sem_eb.at[mb], 0)

    def end_alone():
        weights()
        weights_in()
        end()

    return Phase(
        pre, post, c.ready, arrive, end_alone, weights=weights, weights_in=weights_in, close=end
    )


def norm_slopes(c, mb, grad, pre, stats, gain, bias, sums, buf, sem, out):
    rows, mid = pre.shape[1:]
    scale = stats[mb, 1:2]
    shift = -stats[mb, 0:1] * scale
    chunk = rows // SIDE

    def image_row(i, carry):
        one, two = carry
        at = rows_at(i * chunk, chunk)
        normal = pre[mb, at].astype(F32) * scale + shift
        part = grad[mb, at] * slope(normal * gain[...] + bias[...])
        out[mb, at] = part
        one = one + jnp.sum(part.reshape(-1, 8, mid), axis=0)
        two = two + jnp.sum((part * normal).reshape(-1, 8, mid), axis=0)
        return one, two

    zero = jnp.zeros((8, mid), F32)
    one, two = lax.fori_loop(0, SIDE, image_row, (zero, zero))
    sums[mb, 0:1] = jnp.sum(one, axis=0, keepdims=True)
    sums[mb, 1:2] = jnp.sum(two, axis=0, keepdims=True)
    buf[mb, c.p] = sums[mb]
    c.spread(sums.at[mb], buf.at[mb, c.p], sem.at[mb])


def norm_terms(stats, mb, gain, sums, count):
    scale = stats[mb, 1:2]
    a = gain * scale
    slant = a * sums[1:2] * (-1.0 / count)
    k = a * sums[0:1] * (-1.0 / count) - slant * scale * stats[mb, 0:1]
    return a, slant * scale, k


def middle_backward(g, c):
    nb, rows, mid = g.mpre.shape
    crops = rows // AREA
    long = conv_rows(crops)
    count = float(rows) * c.n

    def begin():
        c.ready()
        g.mdg[...] = jnp.zeros(g.mdg.shape, BF16)
        g.mgain[...] = jnp.zeros(g.mgain.shape, F32)
        g.mbias[...] = jnp.zeros(g.mbias.shape, F32)

    def pre(mb):
        norm_slopes(
            c, mb, g.mg, g.mpre, g.mst, g.middle_gain, g.middle_bias, g.mbm, g.mbb,
            g.sem_mb, g.mgf,
        )

    def give(mb):
        return c.partner(g.ags.at[mb], g.agr.at[mb], g.sem_ag.at[mb])

    def delta(mb):
        c.take(g.mbb.at[mb, pl.ds(0, c.n - 1)], g.sem_mb.at[mb], 1)
        sums = jnp.sum(g.mbb[mb], axis=0)
        g.mbias[...] = g.mbias[...] + sums[0:1]
        g.mgain[...] = g.mgain[...] + sums[1:2]
        a, b, k = norm_terms(g.mst, mb, g.middle_gain[...], sums, count)
        for i in range(SIDE):
            at = pl.ds(i * SIDE * crops, SIDE * crops)
            part = g.mgf[mb, at] * a + g.mpre[mb, at].astype(F32) * b + k
            g.mdg[mb, pl.ds((WIDE + 1 + WIDE * i) * crops, SIDE * crops)] = part.astype(BF16)
        g.mdt[:, mb * long : (mb + 1) * long] = g.mdg[mb, pl.ds((WIDE + 1) * crops, long)].T

    def spread(mb):
        for which, place in ((c.o, 0), (c.h, 1)):
            total = None
            for tap in range(9):
                at = pl.ds((WIDE * (2 - tap // 3) + 2 - tap % 3) * crops, long)
                part = nt(g.mdg[mb, at], g.wm[tap, c.half(which, mid), :])
                total = part if total is None else total + part
            for i in range(SIDE):
                at = pl.ds(i * SIDE * crops, SIDE * crops)
                part = total[i * WIDE * crops : (i * WIDE + SIDE) * crops]
                if place == 0:
                    g.ags[mb, at] = part.astype(BF16)
                else:
                    g.ag[mb, at] = part
            if place == 0:
                give(mb).start()

    def weights(out, first, taps):
        def one(i):
            tap = first + i
            at = pl.ds(pl.multiple_of((WIDE * (tap // 3) + tap % 3) * crops, crops), long)
            for act, which in ((g.ao, c.h), (g.ap, c.o)):
                field = jnp.concatenate([act[mb, at] for mb in range(nb)], axis=0)
                part = nn(g.mdt[...], field)
                out[c.half(2 * i + which, mid), :] = part.T.astype(BF16)

        each(taps, one)

    def arrive(mb):
        give(mb).wait()
        g.ag[mb] = g.ag[mb] + g.agr[mb].astype(F32)

    def end():
        for mb in range(nb):
            c.take(g.mbb.at[mb, pl.ds(0, c.n - 1)], g.sem_mb.at[mb], 0)

    def post(mb):
        delta(mb)
        spread(mb)

    def all_weights():
        weights(g.gmida, 0, 3)
        weights(g.gmidb, 3, 3)
        weights(g.gmidc, 6, 3)

    def end_alone():
        all_weights()
        end()

    return Phase(
        pre, post, begin, arrive, end_alone, delta=delta, spread=spread, weights=weights, close=end
    )


def stem_backward(g, c):
    nb, rows, mid = g.spre.shape
    half = g.x.shape[2]
    crops = rows // AREA
    count = float(rows) * c.n

    def begin():
        c.ready()
        g.sgain[...] = jnp.zeros(g.sgain.shape, F32)
        g.sbias[...] = jnp.zeros(g.sbias.shape, F32)

    def pre(mb):
        norm_slopes(
            c, mb, g.ag, g.spre, g.sst, g.stem_gain, g.stem_bias, g.sbm, g.sbb,
            g.sem_sb, g.sgf,
        )

    def give(mb):
        return c.partner(g.sd.at[mb], g.sdp.at[mb], g.sem_sd.at[mb])

    def swap():
        return c.partner(g.gss, g.gstem.at[c.half(c.h, half)], g.sem_gs)

    def post(mb):
        c.take(g.sbb.at[mb, pl.ds(0, c.n - 1)], g.sem_sb.at[mb], 1)
        sums = jnp.sum(g.sbb[mb], axis=0)
        g.sbias[...] = g.sbias[...] + sums[0:1]
        g.sgain[...] = g.sgain[...] + sums[1:2]
        a, b, k = norm_terms(g.sst, mb, g.stem_gain[...], sums, count)
        for i in range(SIDE):
            at = pl.ds(i * SIDE * crops, SIDE * crops)
            g.sd[mb, at] = (g.sgf[mb, at] * a + g.spre[mb, at].astype(F32) * b + k).astype(BF16)
        give(mb).start()

    def weights():
        lanes = 256
        sd = g.sd[...].reshape(nb * rows, mid)
        sdp = g.sdp[...].reshape(nb * rows, mid)
        for lo in range(0, half, lanes):
            field = g.x[:, :, lo : lo + lanes].reshape(nb * rows, lanes)
            g.gss[lo : lo + lanes] = tn(field, sdp).astype(BF16)
            own = rows_at(c.h * half + lo, lanes)
            g.gstem[own, :] = tn(field, sd).astype(BF16)
        swap().start()

    def weights_in():
        swap().wait_recv()

    def end():
        swap().wait_send()
        for mb in range(nb):
            give(mb).wait_send()
            c.take(g.sbb.at[mb, pl.ds(0, c.n - 1)], g.sem_sb.at[mb], 0)

    def end_alone():
        weights()
        weights_in()
        end()

    return Phase(
        pre, post, begin, lambda mb: give(mb).wait_recv(), end_alone, weights=weights,
        weights_in=weights_in, close=end,
    )


def crops_backward(g, c):
    half = g.wsp.shape[0]

    def pre(mb):
        part = nt(g.sd[mb], g.ws[c.half(c.h, half), :]) + nt(g.sdp[mb], g.wsp[...])
        g.gcrops[mb] = (part + g.sg[mb].astype(F32)).astype(BF16)

    return Phase(pre, lambda mb: None)


class Total:
    def __init__(self, c, local, place, one, two, three, sems):
        self.done = 0
        self.c, self.local, self.place, self.sems = c, local, place, sems
        self.one, self.two, self.three = one, two, three
        self.long = local.shape[0] // 2
        x, y, self.z = c.p % 2, (c.p // 2) % 2, c.p // 4
        step_x, step_y = c.p + 1 - 2 * x, c.p + 2 - 4 * y
        self.ways = ((x, step_x, y, step_y), (y, step_y, x, step_x))
        self.half, self.quarter, self.piece = self.long // 2, self.long // 4, self.long // 16

    def copy(self, stream, step, src, dst, device):
        return pltpu.make_async_remote_copy(
            src_ref=src,
            dst_ref=dst,
            send_sem=self.sems.at[stream, step, 0],
            recv_sem=self.sems.at[stream, step, 1],
            device_id=(device, self.c.h),
            device_id_type=MESH,
        )

    def at(self, start, size):
        return pl.ds(pl.multiple_of(start, 16), size)

    def start(self, step):
        for stream in range(2):
            b1, d1, b2, d2 = self.ways[stream]
            base = stream * self.long
            kept = base + b1 * self.half
            core = kept + b2 * self.quarter
            if step == 0:
                src = self.local.at[self.at(base + (1 - b1) * self.half, self.half)]
                self.copy(stream, step, src, self.one.at[stream], d1).start()
            elif step == 1:
                src = self.one.at[stream, self.at((1 - b2) * self.quarter, self.quarter)]
                self.copy(stream, step, src, self.two.at[stream], d2).start()
            elif step == 4:
                self.keep(stream, core).wait()
                src = self.place(stream, core, self.quarter)
                self.copy(stream, step, src, src, d2).start()
            elif step == 5:
                src = self.place(stream, kept, self.half)
                self.copy(stream, step, src, src, d1).start()
            else:
                if step == 3:
                    self.keep(stream, core).start()
                for d in range(1, 4):
                    other = (self.z + d) % 4
                    device = self.c.p + 4 * (other - self.z)
                    if step == 2:
                        src = self.two.at[stream, self.at(other * self.piece, self.piece)]
                        dst = self.three.at[stream, 3 - d]
                    else:
                        src = self.two.at[stream, self.at(self.z * self.piece, self.piece)]
                        dst = self.place(stream, core + self.z * self.piece, self.piece)
                    self.copy(stream, step, src, dst, device).start()

    def keep(self, stream, core):
        piece = self.at(self.z * self.piece, self.piece)
        place = self.place(stream, core + self.z * self.piece, self.piece)
        return pltpu.make_async_copy(self.two.at[stream, piece], place, self.sems.at[stream, 6, 0])

    def wait(self, stream, step, which):
        blocks = {0: self.one, 1: self.two, 2: self.three, 3: self.three, 4: self.two, 5: self.one}
        self.c.take(blocks[step].at[stream], self.sems.at[stream, step], which)

    def take(self, step):
        for stream in range(2):
            self.wait(stream, step, 1)
            b1, d1, b2, d2 = self.ways[stream]
            kept = stream * self.long + b1 * self.half
            core = kept + b2 * self.quarter
            one, two, three = self.one.at[stream], self.two.at[stream], self.three.at[stream]
            if step == 0:
                self.add(one, 0, [(one, 0), (self.local, kept)], self.half)
            elif step == 1:
                self.add(two, 0, [(two, 0), (one, b2 * self.quarter)], self.quarter)
            elif step == 2:
                terms = [(two, self.z * self.piece)] + [(three.at[d], 0) for d in range(3)]
                self.add(two, self.z * self.piece, terms, self.piece)

    def add(self, out, start, terms, size):
        chunk = 16

        def one(i):
            total = None
            for ref, begin in terms:
                value = ref[rows_at(begin + i * chunk, chunk), :].astype(F32)
                total = value if total is None else total + value
            out[rows_at(start + i * chunk, chunk), :] = total.astype(BF16)

        each(size // chunk, one)

    def step(self):
        self.take(self.done)
        self.done += 1
        if self.done < 6:
            self.start(self.done)

    def close(self):
        for stream in range(2):
            for step in range(6):
                self.wait(stream, step, 0)


def whole_step(g, c):
    nb, half = g.x.shape[0], g.x.shape[2]
    mid = g.ws.shape[1]
    c.load("ws", 0, g.ws_in, g.ws, g.sem_in.at[0])
    for mb in range(nb):
        c.load("x", mb, g.x_in.at[mb], g.x.at[mb], g.sem_in.at[4 + mb])
    c.load("we", 0, g.we_in, g.we, g.sem_in.at[1])
    c.load("wm", 0, g.wm_in, g.wm, g.sem_in.at[2])
    c.load("wh", 0, g.wh_in, g.wh, g.sem_in.at[3])
    stem, middle, expand = stem_forward(g, c), middle_forward(g, c), expand_forward(g, c)
    hidden, white, hback = hidden_forward(g, c), whiten(g, c), hidden_backward(g, c)
    eback, mback, sback = expand_backward(g, c), middle_backward(g, c), stem_backward(g, c)
    field = crops_backward(g, c)

    def chain(first, second):
        first.post(0)
        for mb in range(1, nb):
            first.post(mb)
            first.arrive(mb - 1)
            second.pre(mb - 1)
        first.arrive(nb - 1)
        second.pre(nb - 1)

    stem.begin()
    expand.early()
    for mb in range(nb):
        stem.pre(mb)
    chain(stem, middle)
    expand.weights()
    chain(middle, expand)
    chain(expand, hidden)
    for step in (hidden.post, hidden.embed, hidden.mirror):
        for mb in range(nb):
            step(mb)
    hidden.relay("h", 0)
    hidden.relay("p", 0)
    for mb in range(nb):
        hidden.landed(mb)
        white.pre(mb)

    def between(start):
        if start == 32:
            hidden.relay("h", 1)
        if start == 64:
            hidden.relay("h", 2)
        if start == 88:
            hidden.relay("p", 1)

    white.factor_all(between)
    for mb in range(nb):
        white.rest(mb)
    for phase in (stem, middle, expand):
        phase.end()

    def rows_of(out, first):
        return lambda stream, start, size: out.at[pl.ds(pl.multiple_of(first + start, 16), size)]

    def halves_of(out):
        def place(stream, start, size):
            at = pl.ds(pl.multiple_of(start - stream * mid, 16), size)
            return out.at[at, pl.ds(stream * half, half)]

        return place

    third = g.gmida.shape[0]
    exp = Total(c, g.gexp, halves_of(g.gexp_t), g.gexp_1, g.gexp_2, g.gexp_3, g.sem_gexp)
    place = [rows_of(g.gmid_t, i * third) for i in range(3)]
    one = Total(c, g.gmida, place[0], g.gmida_1, g.gmida_2, g.gmida_3, g.sem_gmida)
    two = Total(c, g.gmidb, place[1], g.gmidb_1, g.gmidb_2, g.gmidb_3, g.sem_gmidb)
    three = Total(c, g.gmidc, place[2], g.gmidc_1, g.gmidc_2, g.gmidc_3, g.sem_gmidc)
    last, rest = (
        Total(
            c, g.gstem.at[pl.ds(i * half, half)], rows_of(g.gstem_t, i * half), g.gstem_1.at[i],
            g.gstem_2.at[i], g.gstem_3.at[i], g.sem_gstem.at[i],
        )
        for i in range(2)
    )
    keep = pltpu.make_async_copy(g.ghid, g.ghid_t, g.sem_in.at[0])

    hidden.relay("h", 3)
    hback.run()
    hidden.relay("p", 2)
    hback.finish()
    for mb in range(nb):
        eback.pre(mb)
    mback.begin()
    sback.begin()
    hidden.relay("p", 3)
    hidden.pooled_swap().start()
    eback.post(0)
    eback.post(1)
    eback.arrive(0)
    mback.pre(0)
    eback.post(2)
    eback.arrive(1)
    mback.pre(1)
    eback.weights()
    eback.arrive(2)
    mback.pre(2)
    eback.weights_in()
    exp.start(0)
    mback.delta(0)
    mback.delta(1)
    mback.delta(2)
    mback.weights(g.gmida, 0, 3)
    one.start(0)
    mback.weights(g.gmidb, 3, 3)
    exp.step()
    two.start(0)
    mback.weights(g.gmidc, 6, 3)
    one.step()
    three.start(0)
    mback.spread(0)
    exp.step()
    mback.spread(1)
    two.step()
    mback.arrive(0)
    sback.pre(0)
    mback.spread(2)
    exp.step()
    one.step()
    mback.arrive(1)
    sback.pre(1)
    mback.arrive(2)
    sback.pre(2)
    three.step()
    sback.post(0)
    two.step()
    sback.post(1)
    sback.post(2)
    exp.step()
    three.step()
    for mb in range(nb):
        sback.arrive(mb)
    sback.weights()
    exp.step()
    one.step()
    sback.weights_in()
    last.start(0)
    rest.start(0)
    field.pre(0)
    two.step()
    field.pre(1)
    field.pre(2)
    hidden.pooled_swap().wait_recv()
    hback.weights()
    keep.start()
    exp.step()
    three.step()
    last.step()
    one.step()
    rest.step()
    last.step()
    two.step()
    one.step()
    rest.step()
    two.step()
    three.step()
    last.step()
    one.step()
    rest.step()
    two.step()
    last.step()
    three.step()
    rest.step()
    last.step()
    three.step()
    rest.step()
    last.step()
    rest.step()
    gains = (g.sgain, g.sbias, g.mgain, g.mbias, g.egain, g.ebias, g.hgain, g.hbias)
    for row, value in enumerate(gains):
        g.norms[row : row + 1, : value.shape[1]] = value[...]
    hidden.end()
    hidden.end_relay()
    hback.end()
    for phase in (eback, mback, sback):
        phase.close()
    for total in (exp, one, two, three, last, rest):
        total.close()
    keep.wait()


def widen(arrays, norms, widths):
    whole = [(array.shape, 2 if array.size > 2**20 else 1) for array in arrays]
    parts = []
    for number, (shape, cuts) in enumerate(whole):
        if len(shape) == 3:
            cut = -(-shape[1] // 32) * 16
            parts += [
                (number, (i, pl.ds(start, size)), (size, shape[2]))
                for i in range(shape[0])
                for start, size in ((0, cut), (cut, shape[1] - cut))
            ]
        else:
            size = shape[0] // cuts
            parts += [(number, (pl.ds(i * size, size),), (size, shape[1])) for i in range(cuts)]
    count, many = len(arrays), len(parts)

    def kernel(*refs):
        sources, lines = refs[:count], refs[count]
        results = refs[count + 1 : 2 * count + 1]
        rows = refs[2 * count + 1 : 2 * count + 1 + len(widths)]
        narrow = refs[2 * count + 1 + len(widths) : 2 * count + 1 + len(widths) + many]
        wide = refs[2 * count + 1 + len(widths) + many : -2]
        sem_a, sem_b = refs[-2:]
        ins, outs = [], []
        for i, (number, where, _) in enumerate(parts):
            ins.append(pltpu.make_async_copy(sources[number].at[where], narrow[i], sem_a.at[i]))
            outs.append(pltpu.make_async_copy(wide[i], results[number].at[where], sem_b.at[i]))
            ins[i].start()
        for row, width in enumerate(widths):
            rows[row][...] = lines[row : row + 1, :width]
        for i, (_, _, (tall, _)) in enumerate(parts):
            ins[i].wait()

            def cast(j, i=i):
                at = rows_at(j * 16, 16)
                wide[i][at, :] = narrow[i][at, :].astype(F32)

            each(tall // 16, cast)
            outs[i].start()
        for copy in outs:
            copy.wait()

    hbm, vmem = pl.BlockSpec(memory_space=pl.ANY), pl.BlockSpec(memory_space=pltpu.VMEM)
    results = pl.pallas_call(
        kernel,
        out_shape=[jax.ShapeDtypeStruct(array.shape, F32) for array in arrays]
        + [jax.ShapeDtypeStruct((1, width), F32) for width in widths],
        in_specs=[hbm] * count + [vmem],
        out_specs=[hbm] * count + [vmem] * len(widths),
        scratch_shapes=[pltpu.VMEM(size, BF16) for _, _, size in parts]
        + [pltpu.VMEM(size, F32) for _, _, size in parts]
        + [DMA((many,)), DMA((many,))],
        compiler_params=pltpu.CompilerParams(vmem_limit_bytes=60 * 2**20),
        name="widen",
    )(*arrays, norms)
    return results[:count], results[count:]


NORMS = ("sgain", "sbias", "mgain", "mbias", "egain", "ebias", "hgain", "hbias")
GRADS = ("gexp", "gmida", "gmidb", "gmidc", "gstem")


def names_of(functions):
    found, codes = set(), [function.__code__ for function in functions]
    while codes:
        code = codes.pop()
        found |= set(code.co_names)
        codes += [value for value in code.co_consts if isinstance(value, types.CodeType)]
    return found


def body(
    crops_in, stem_weight, middle_weight, expand_weight, stem_gain, stem_bias, middle_gain,
    middle_bias, expand_gain, expand_bias, hidden_weight, hidden_gain, hidden_bias, embed_weight,
    sub_sizes, crop_order, pair_index,
):
    nb, crops, area, half = crops_in.shape
    n = lax.axis_size("dp")
    rows = crops * area
    mid = stem_weight.shape[1]
    hid = hidden_weight.shape[1]
    width = embed_weight.shape[1]
    count = crop_order.shape[1]
    subs = sub_sizes.shape[1]
    long = conv_rows(crops)
    tall = long + 2 * (WIDE + 1) * crops

    def line(v):
        return v.reshape(1, -1)

    env = dict(
        x=crops_in.transpose(0, 2, 1, 3).reshape(nb, rows, half),
        ws=stem_weight,
        wm=middle_weight,
        we=expand_weight,
        wh=hidden_weight,
        w2=embed_weight,
        stem_gain=line(stem_gain),
        stem_bias=line(stem_bias),
        middle_gain=line(middle_gain),
        middle_bias=line(middle_bias),
        expand_gain=line(expand_gain),
        expand_bias=line(expand_bias),
        hidden_gain=line(hidden_gain),
        hidden_bias=line(hidden_bias),
        sizes=sub_sizes,
        order=crop_order,
        pairs=pair_index.transpose(0, 2, 1),
    )
    table = dict(
        wsp=((half, mid), BF16),
        spre=((nb, rows, mid), BF16),
        sst=((nb, 2, mid), F32),
        ao=((nb, tall, mid), BF16),
        ap=((nb, tall, mid), BF16),
        ss=((nb, rows, mid), BF16),
        sr=((nb, rows, mid), BF16),
        sm=((nb, 2, mid), F32),
        sbuf=((nb, n, 2, mid), F32),
        mpre=((nb, rows, mid), BF16),
        mst=((nb, 2, mid), F32),
        mo=((nb, rows, mid), BF16),
        mp=((nb, rows, mid), BF16),
        mm=((nb, 2, mid), F32),
        mbuf=((nb, n, 2, mid), F32),
        wep=((mid, half), BF16),
        ef=((1, rows, 256), F32),
        em=((1, 2, 256), F32),
        esend=((nb, 2, half), F32),
        ebuf=((nb, n, 2, half), F32),
        epre=((nb, rows, half), BF16),
        est=((nb, 2, half), F32),
        po=((nb, crops, half), BF16),
        pp=((nb, crops, half), BF16),
        hall=((4, n // 4, nb, crops, hid), BF16),
        pall=((4, n // 4, nb, crops, half), BF16),
        qall=((4, n // 4, nb, crops, half), BF16),
        sown=((nb, rows, mid), F32),
        hm=((nb, 2, hid), F32),
        hbuf=((nb, n, 2, hid), F32),
        hst=((nb, 2, hid), F32),
        pe=((nb, crops, width), F32),
        pr=((nb, crops, width), F32),
        em2=((nb, 2, crops // 2, width), F32),
        gath=((nb, n, 2, crops // 2, width), F32),
        member=((nb, count, width), F32),
        cent=((nb, count, width), F32),
        cov=((nb * subs, width, width), F32),
        loss=((1, width), F32),
        ed=((nb, count, width), BF16),
        gemb=((hid, width), F32),
        hgf=((count, hid), F32),
        hgain=((1, hid), F32),
        hbias=((1, hid), F32),
        hd=((nb, count, hid), BF16),
        pgs=((nb, crops, half), BF16),
        pgr=((nb, crops, half), BF16),
        ghid=((2 * half, hid), BF16),
        pg=((nb, crops, half), F32),
        sg=((nb, rows, half), BF16),
        ebm=((nb, 2, half), F32),
        ebt=((2, half), F32),
        ebb=((nb, n, 2, half), F32),
        egain=((1, half), F32),
        ebias=((1, half), F32),
        xd=((nb, rows, half), BF16),
        mgs=((nb, rows, mid), BF16),
        mgr=((nb, rows, mid), BF16),
        mg=((nb, rows, mid), F32),
        gxs=((mid, half), BF16),
        gexp=((2 * mid, half), BF16),
        mdg=((nb, tall, mid), BF16),
        mdt=((mid, nb * long), BF16),
        mgf=((nb, rows, mid), F32),
        mbm=((nb, 2, mid), F32),
        mbb=((nb, n, 2, mid), F32),
        mgain=((1, mid), F32),
        mbias=((1, mid), F32),
        ags=((nb, rows, mid), BF16),
        agr=((nb, rows, mid), BF16),
        ag=((nb, rows, mid), F32),
        gmida=((6 * mid, mid), BF16),
        gmidb=((6 * mid, mid), BF16),
        gmidc=((6 * mid, mid), BF16),
        sgf=((nb, rows, mid), F32),
        sbm=((nb, 2, mid), F32),
        sbb=((nb, n, 2, mid), F32),
        sgain=((1, mid), F32),
        sbias=((1, mid), F32),
        sd=((nb, rows, mid), BF16),
        sdp=((nb, rows, mid), BF16),
        gss=((half, mid), BF16),
        gstem=((2 * half, mid), BF16),
        gcrops=((nb, rows, half), BF16),
    )
    pair = (2,)
    pairs = (nb, 2)
    sems = dict(
        sem_sw=pair, sem_sp=pairs, sem_ss=pairs, sem_sa=pairs, sem_ms=pairs, sem_ma=pairs,
        sem_ew=pair, sem_es=pairs, sem_ep=pairs, sem_hs=pairs, sem_he=pairs, sem_hg=pairs,
        sem_hx=pairs, sem_hh=(3, 2), sem_pa=(3, 2), sem_pq=pair, sem_hp=pair, sem_eb=pairs, sem_mg=pairs, sem_gx=pair,
        sem_mb=pairs, sem_ag=pairs, sem_sb=pairs, sem_sd=pairs, sem_gs=pair,
    )
    phases = [
        stem_forward, middle_forward, expand_forward, hidden_forward, whiten, hidden_backward,
        expand_backward, middle_backward, stem_backward, crops_backward,
    ]
    block = n == 16
    final = set(GRADS) | {"loss", "gcrops", "ghid", "gemb"}
    final |= set(NORMS)
    shared = {}
    if block:
        shared = dict(
            xd="epre", mgs="ss", ags="ss", agr="sr", mgf="mg", ag="mg", sgf="mg", sd="mo",
            sdp="mp", gcrops="sg", sown="mg", gxs="wep", ghid="wh",
        )
        groups = [phases + [whole_step]]
        final -= set(GRADS) | set(NORMS) | {"ghid"}
        whole = dict(
            gexp_t=((mid, 2 * half), BF16), gmid_t=((18 * mid, mid), BF16),
            gstem_t=((2 * half, mid), BF16), ghid_t=((2 * half, hid), BF16),
            norms=((8, half), F32),
        )
        final |= set(whole)
        table.update(whole)
        for name in GRADS:
            tall, cols = table[name][0]
            table[name + "_1"] = ((2, tall // 4, cols), BF16)
            table[name + "_2"] = ((2, tall // 8, cols), BF16)
            table[name + "_3"] = ((2, 3, tall // 32, cols), BF16)
            sems["sem_" + name] = (2, 7, 2)
        for name in ("gstem_1", "gstem_2", "gstem_3"):
            (streams, *several, tall, cols), kind = table[name]
            table[name] = ((2, streams, *several, tall // 2, cols), kind)
        sems["sem_gstem"] = (2, 2, 7, 2)
        sems.update(sem_in=(4 + nb,))
        for name in ("x", "ws", "wm", "we", "wh"):
            env[name + "_in"] = env.pop(name)
            table[name] = (env[name + "_in"].shape, BF16)
    else:
        groups = [[phase] for phase in phases]

    vmem = pl.BlockSpec(memory_space=pltpu.VMEM)
    smem = pl.BlockSpec(memory_space=pltpu.SMEM)
    hbm = pl.BlockSpec(memory_space=pl.ANY)
    used = [names_of(group + [norm_slopes, norm_terms]) for group in groups]
    for number, group in enumerate(groups):
        later = final.union(*used[number + 1 :])
        here = used[number]
        reads = [name for name in env if name in here]
        made = [name for name in table if name in here and name not in env]
        sem_names = [name for name in sems if name in here]
        own = [name for name in made if name not in shared]
        bases = {shared[name] for name in made if name in shared and name in later}
        outs = [name for name in own if name in later or name in bases]
        scratch = [name for name in own if name not in outs]
        names = reads + outs + scratch + sem_names
        remote = bool(sem_names)

        def kernel(*refs, group=group, names=names, remote=remote):
            c = Ctx(n, remote, remote)
            g = types.SimpleNamespace(**dict(zip(names, refs)))
            for name, base in shared.items():
                setattr(g, name, getattr(g, base))
            if block:
                whole_step(g, c)
            else:
                group[0](g, c).alone(nb)

        params = dict(vmem_limit_bytes=62 * 2**20)
        if remote:
            params.update(collective_id=number, has_side_effects=True)
        results = pl.pallas_call(
            kernel,
            out_shape=[jax.ShapeDtypeStruct(*table[name]) for name in outs],
            in_specs=[
                smem if name == "sizes" else hbm if name[-3:] == "_in" else vmem for name in reads
            ],
            out_specs=[hbm if name[-2:] == "_t" else vmem for name in outs],
            scratch_shapes=[pltpu.VMEM(*table[name]) for name in scratch]
            + [DMA(sems[name]) for name in sem_names],
            compiler_params=pltpu.CompilerParams(**params),
            name=group[-1].__name__,
        )(*[env[name] for name in reads])
        env.update(zip(outs, results))

    for name, base in shared.items():
        if name in final:
            env[name] = env[base]
    if block:
        widths = [table[name][0][1] for name in NORMS]
        arrays = [env[name] for name in ("gcrops", "gmid_t", "ghid_t", "gexp_t", "gstem_t")]
        (env["gcrops"], gmid, ghid, gexp, gstem), rows_out = widen(arrays, env["norms"], widths)
        env.update(zip(NORMS, rows_out))
    else:
        gexp, *gmid, gstem = lax.psum([env[name] for name in GRADS], "dp")
        gexp = gexp.reshape(2, mid, half).transpose(1, 0, 2).reshape(mid, 2 * half)
        gmid = jnp.concatenate(gmid, axis=0)
        ghid = env["ghid"]
    field = env["gcrops"].astype(F32).reshape(nb, area, crops, half).transpose(0, 2, 1, 3)
    return (
        env["loss"][0, 0],
        field,
        gstem.astype(F32),
        gmid.astype(F32).reshape(9, 2 * mid, mid),
        gexp.astype(F32),
        env["sgain"][0],
        env["sbias"][0],
        env["mgain"][0],
        env["mbias"][0],
        env["egain"][0],
        env["ebias"][0],
        ghid.astype(F32),
        env["hgain"][0],
        env["hbias"][0],
        env["gemb"],
    )


def solution(mesh):
    return jax.shard_map(
        body,
        mesh=mesh,
        in_specs=(
            P(None, "dp", None, "chan"),
            P(None, "chan"),
            P(None, None, "chan"),
            P("chan", None),
            P("chan"),
            P("chan"),
            P("chan"),
            P("chan"),
            P("chan"),
            P("chan"),
            P(None, "chan"),
            P("chan"),
            P("chan"),
            P("chan", None),
            P(),
            P(),
            P(),
        ),
        out_specs=(
            P(),
            P(None, "dp", None, "chan"),
            P(None, "chan"),
            P(None, None, "chan"),
            P("chan", None),
            P("chan"),
            P("chan"),
            P("chan"),
            P("chan"),
            P("chan"),
            P("chan"),
            P(None, "chan"),
            P("chan"),
            P("chan"),
            P("chan", None),
        ),
        check_vma=False,
    )
```

```python
import types

import jax
import jax.numpy as jnp
from jax import lax
from jax.experimental import pallas as pl
from jax.experimental.pallas import tpu as pltpu
from jax.sharding import PartitionSpec as P

SIDE = 7
AREA = SIDE * SIDE
WIDE = SIDE + 1
EPS_NORM = 1e-05
RIDGE = 0.5
LOSS_SCALE = 8192.0
HIGH = lax.Precision.HIGHEST
MESH = pl.DeviceIdType.MESH
F32 = jnp.float32
BF16 = jnp.bfloat16
DMA = pltpu.SemaphoreType.DMA


def nn(left, right):
    return jnp.dot(left, right, preferred_element_type=F32)


def nt(left, right, precision=None):
    return lax.dot_general(
        left, right, (((1,), (1,)), ((), ())), precision=precision, preferred_element_type=F32
    )


def tn(left, right, precision=None):
    return lax.dot_general(
        left, right, (((0,), (0,)), ((), ())), precision=precision, preferred_element_type=F32
    )


def sigmoid(values):
    return 0.5 * jnp.tanh(0.5 * values) + 0.5


def silu(values):
    return values * sigmoid(values)


def slope(values):
    part = sigmoid(values)
    return part * (1.0 + values * (1.0 - part))


def rows_at(start, size):
    return pl.ds(pl.multiple_of(start, size if size % 16 else 16), size)


class Ctx:
    def __init__(self, devices, partner, peers):
        self.n = devices
        self.p = lax.axis_index("dp")
        self.h = lax.axis_index("chan")
        self.o = 1 - self.h
        self.waits = 0
        self.loads = {}
        if partner or peers:
            barrier = pltpu.get_barrier_semaphore()
            if partner:
                pl.semaphore_signal(barrier, inc=1, device_id=(self.p, self.o), device_id_type=MESH)
                self.waits += 1
            if peers:

                def greet(d, carry):
                    pl.semaphore_signal(
                        barrier,
                        inc=1,
                        device_id=(lax.rem(self.p + d, self.n), self.h),
                        device_id_type=MESH,
                    )
                    return carry

                lax.fori_loop(1, self.n, greet, 0)
                self.waits += self.n - 1

    def ready(self):
        if self.waits:
            pl.semaphore_wait(pltpu.get_barrier_semaphore(), self.waits)
            self.waits = 0

    def load(self, name, index, src, dst, sem):
        self.loads[name, index] = pltpu.make_async_copy(src, dst, sem)
        self.loads[name, index].start()

    def loaded(self, name, index=0):
        copy = self.loads.pop((name, index), None)
        if copy is not None:
            copy.wait()

    def half(self, which, size):
        return pl.ds(pl.multiple_of(which * size, size), size)

    def partner(self, src, dst, sems):
        return pltpu.make_async_remote_copy(
            src_ref=src,
            dst_ref=dst,
            send_sem=sems.at[0],
            recv_sem=sems.at[1],
            device_id=(self.p, self.o),
            device_id_type=MESH,
        )

    def spread(self, src, dst, sems):
        def one(d, carry):
            pltpu.make_async_remote_copy(
                src_ref=src,
                dst_ref=dst,
                send_sem=sems.at[0],
                recv_sem=sems.at[1],
                device_id=(lax.rem(self.p + d, self.n), self.h),
                device_id_type=MESH,
            ).start()
            return carry

        lax.fori_loop(1, self.n, one, 0)

    def relay(self, ref, sems, stage):
        q, z = self.p % 4, self.p // 4
        x, y = q % 2, q // 2
        if stage == 0:
            blocks = [(ref.at[q, z], self.p + 4 * ((z + d) % 4 - z)) for d in range(1, 4)]
        else:
            near_x, near_y = self.p + 1 - 2 * x, self.p + 2 - 4 * y
            cols = ref.shape[-1] // 2
            one, two = pl.ds(0, cols), pl.ds(cols, cols)
            if stage == 1:
                blocks = [(ref.at[q, :, :, :, one], near_x), (ref.at[q, :, :, :, two], near_y)]
            else:
                blocks = [(ref.at[pl.ds(2 * y, 2), :, :, :, one], near_y)]
                blocks += [(ref.at[x + 2 * i, :, :, :, two], near_x) for i in range(2)]
        return [
            pltpu.make_async_remote_copy(
                src_ref=block,
                dst_ref=block,
                send_sem=sems.at[stage, 0],
                recv_sem=sems.at[stage, 1],
                device_id=(device, self.h),
                device_id_type=MESH,
            )
            for block, device in blocks
        ]

    def relay_wait(self, ref, sems, stage, which):
        blocks = (ref.at[0, pl.ds(0, 3)], ref.at[0], ref.at[pl.ds(0, 2)])[stage]
        self.take(blocks, sems.at[stage], which)

    def take(self, blocks, sems, which):
        pltpu.make_async_copy(blocks, blocks, sems.at[which]).wait()


class Phase:
    def __init__(self, pre, post, begin=None, arrive=None, end=None, **more):
        nothing = lambda *_: None
        self.pre, self.post = pre, post
        self.begin, self.arrive, self.end = begin or nothing, arrive or nothing, end or nothing
        self.__dict__.update(more)

    def alone(self, nb):
        self.begin()
        for step in (self.pre, self.post, self.arrive):
            for mb in range(nb):
                step(mb)
        self.end()


def each(count, body):
    lax.fori_loop(0, count, lambda i, c: (body(i), c)[1], 0)


def local_moments(ref, mb, rows, chunk, cols, out):
    lanes = 256
    for lo in range(0, cols, lanes):
        at = pl.ds(lo, lanes)

        def add(i, total):
            part = ref[mb, rows_at(i * chunk, chunk), at]
            return total + jnp.sum(part.reshape(-1, 8, lanes), axis=0)

        total = lax.fori_loop(0, rows // chunk, add, jnp.zeros((8, lanes), F32))
        mean = jnp.sum(total, axis=0, keepdims=True) * (1.0 / rows)

        def square(i, total):
            part = ref[mb, rows_at(i * chunk, chunk), at] - mean
            return total + jnp.sum((part * part).reshape(-1, 8, lanes), axis=0)

        total = lax.fori_loop(0, rows // chunk, square, jnp.zeros((8, lanes), F32))
        out[mb, 0:1, at] = mean
        out[mb, 1:2, at] = jnp.sum(total, axis=0, keepdims=True)


def joint_moments(parts, rows):
    n = parts.shape[0]
    mean = jnp.sum(parts, axis=0)[0:1] * (1.0 / n)
    apart = parts[:, 0:1, :] - mean[None]
    squares = jnp.sum(parts, axis=0)[1:2] + rows * jnp.sum(apart * apart, axis=0)
    return mean, lax.rsqrt(squares * (1.0 / (n * rows)) + EPS_NORM)


def stem_forward(g, c):
    nb, rows, half = g.x.shape
    crops = rows // AREA
    mid = g.ws.shape[1]

    def swap():
        return c.partner(g.ws.at[c.half(c.o, half)], g.wsp, g.sem_sw)

    def give(mb):
        return c.partner(g.ss.at[mb], g.sr.at[mb], g.sem_sp.at[mb])

    def act(mb):
        return c.partner(g.ao.at[mb], g.ap.at[mb], g.sem_sa.at[mb])

    def begin():
        g.ao[...] = jnp.zeros(g.ao.shape, BF16)
        c.loaded("ws")
        for mb in range(nb):
            if mb == nb - 1:
                c.ready()
                swap().start()
            c.loaded("x", mb)
            g.sown[mb] = nn(g.x[mb], g.ws[c.half(c.h, half), :])
        swap().wait_recv()
        for mb in range(nb):
            g.ss[mb] = nn(g.x[mb], g.wsp[...]).astype(BF16)
            give(mb).start()

    def pre(mb):
        give(mb).wait_recv()
        g.ef[0] = g.sown[mb] + g.sr[mb].astype(F32)
        local_moments(g.ef, 0, rows, 7 * crops, mid, g.em)
        g.spre[mb] = g.ef[0].astype(BF16)
        g.sm[mb] = g.em[0]
        g.sbuf[mb, c.p] = g.sm[mb]
        c.spread(g.sm.at[mb], g.sbuf.at[mb, c.p], g.sem_ss.at[mb])

    def post(mb):
        c.take(g.sbuf.at[mb, pl.ds(0, c.n - 1)], g.sem_ss.at[mb], 1)
        mean, scale = joint_moments(g.sbuf[mb], float(rows))
        g.sst[mb, 0:1] = mean
        g.sst[mb, 1:2] = scale
        gain = scale * g.stem_gain[...]
        bias = g.stem_bias[...] - mean * gain
        for i in range(SIDE):
            post = g.spre[mb, pl.ds(i * SIDE * crops, SIDE * crops)].astype(F32) * gain + bias
            g.ao[mb, pl.ds((WIDE + 1 + WIDE * i) * crops, SIDE * crops)] = silu(post).astype(BF16)
        act(mb).start()

    def end():
        swap().wait_send()
        for mb in range(nb):
            give(mb).wait_send()
            act(mb).wait_send()
            c.take(g.sbuf.at[mb, pl.ds(0, c.n - 1)], g.sem_ss.at[mb], 0)

    return Phase(pre, post, begin, lambda mb: act(mb).wait_recv(), end)


def conv_rows(crops):
    return SIDE * WIDE * crops


def middle_forward(g, c):
    nb, rows, mid = g.mpre.shape
    crops = rows // AREA
    long = conv_rows(crops)

    def act(mb):
        return c.partner(g.mo.at[mb], g.mp.at[mb], g.sem_ma.at[mb])

    def pre(mb):
        if mb == 0:
            c.loaded("wm")
        total = None
        for tap in range(9):
            at = pl.ds((WIDE * (tap // 3) + tap % 3) * crops, long)
            part = nn(g.ao[mb, at], g.wm[tap, c.half(c.h, mid), :])
            total = part if total is None else total + part
            total = total + nn(g.ap[mb, at], g.wm[tap, c.half(c.o, mid), :])
        for i in range(SIDE):
            g.ef[0, pl.ds(i * SIDE * crops, SIDE * crops)] = total[
                i * WIDE * crops : (i * WIDE + SIDE) * crops
            ]
        local_moments(g.ef, 0, rows, 7 * crops, mid, g.em)
        g.mpre[mb] = g.ef[0].astype(BF16)
        g.mm[mb] = g.em[0]
        g.mbuf[mb, c.p] = g.mm[mb]
        c.spread(g.mm.at[mb], g.mbuf.at[mb, c.p], g.sem_ms.at[mb])

    def post(mb):
        c.take(g.mbuf.at[mb, pl.ds(0, c.n - 1)], g.sem_ms.at[mb], 1)
        mean, scale = joint_moments(g.mbuf[mb], float(rows))
        g.mst[mb, 0:1] = mean
        g.mst[mb, 1:2] = scale
        gain = scale * g.middle_gain[...]
        bias = g.middle_bias[...] - mean * gain
        for i in range(SIDE):
            at = pl.ds(i * SIDE * crops, SIDE * crops)
            g.mo[mb, at] = silu(g.mpre[mb, at].astype(F32) * gain + bias).astype(BF16)
        act(mb).start()

    def end():
        for mb in range(nb):
            act(mb).wait_send()
            c.take(g.mbuf.at[mb, pl.ds(0, c.n - 1)], g.sem_ms.at[mb], 0)

    return Phase(pre, post, c.ready, lambda mb: act(mb).wait_recv(), end)


def expand_forward(g, c):
    nb, rows, half = g.x.shape
    crops = rows // AREA
    lanes = 256

    def swap():
        return c.partner(g.we.at[:, c.half(c.o, half)], g.wep, g.sem_ew)

    def pool(mb):
        return c.partner(g.po.at[mb], g.pp.at[mb], g.sem_ep.at[mb])

    def early():
        c.loaded("we")
        c.ready()
        swap().start()

    def begin():
        early()
        swap().wait_recv()

    def pre(mb):
        for k in range(half // lanes):
            cols = pl.ds(k * lanes, lanes)
            own = g.we[:, pl.ds(pl.multiple_of(c.h * half + k * lanes, lanes), lanes)]
            g.ef[0] = nn(g.mo[mb], own) + nn(g.mp[mb], g.wep[:, cols])
            local_moments(g.ef, 0, rows, 7 * crops, lanes, g.em)
            g.epre[mb, :, cols] = g.ef[0].astype(BF16)
            g.esend[mb, :, cols] = g.em[0]
        g.ebuf[mb, c.p] = g.esend[mb]
        c.spread(g.esend.at[mb], g.ebuf.at[mb, c.p], g.sem_es.at[mb])

    def post(mb):
        c.take(g.ebuf.at[mb, pl.ds(0, c.n - 1)], g.sem_es.at[mb], 1)
        mean, scale = joint_moments(g.ebuf[mb], float(rows))
        g.est[mb, 0:1] = mean
        g.est[mb, 1:2] = scale
        for lo in range(0, half, lanes):
            cols = pl.ds(lo, lanes)
            gain = g.est[mb, 1:2, cols] * g.expand_gain[:, cols]
            bias = g.expand_bias[:, cols] - g.est[mb, 0:1, cols] * gain

            def pixels(i, total):
                for j in range(SIDE):
                    at = rows_at((i * SIDE + j) * crops, crops)
                    summed = g.epre[mb, at, cols].astype(F32) * gain + bias
                    summed = summed + g.x[mb, at, cols].astype(F32)
                    gate = sigmoid(summed)
                    total = total + summed * gate
                    g.slo[mb, at, cols] = (gate * (1.0 + summed * (1.0 - gate))).astype(BF16)
                return total

            total = lax.fori_loop(0, SIDE, pixels, jnp.zeros((crops, lanes), F32))
            g.po[mb, :, cols] = (total * (1.0 / AREA)).astype(BF16)
        pool(mb).start()

    def end():
        swap().wait_send()
        for mb in range(nb):
            pool(mb).wait_send()
            c.take(g.ebuf.at[mb, pl.ds(0, c.n - 1)], g.sem_es.at[mb], 0)

    return Phase(
        pre, post, begin, lambda mb: pool(mb).wait_recv(), end, early=early,
        weights=lambda: swap().wait_recv(),
    )


def hidden_forward(g, c):
    nb, crops, half = g.po.shape
    part = crops // 2

    def trade(mb):
        return c.partner(g.pe.at[mb], g.pr.at[mb], g.sem_he.at[mb])

    def swap(mb):
        where = g.gath.at[mb, :, c.h]
        return c.partner(where, where, g.sem_hx.at[mb])

    def others(mb):
        return g.gath.at[mb, pl.ds(0, c.n - 1), c.h]

    def pre(mb):
        if mb == 0:
            c.loaded("wh")
        value = nn(g.po[mb], g.wh[c.half(c.h, half), :]) + nn(g.pp[mb], g.wh[c.half(c.o, half), :])
        g.hall[c.p % 4, c.p // 4, mb] = value.astype(BF16)
        mean = jnp.mean(value, axis=0, keepdims=True)
        g.hm[mb, 0:1] = mean
        g.hm[mb, 1:2] = jnp.sum((value - mean) * (value - mean), axis=0, keepdims=True)
        g.hbuf[mb, c.p] = g.hm[mb]
        c.spread(g.hm.at[mb], g.hbuf.at[mb, c.p], g.sem_hs.at[mb])

    def post(mb):
        c.take(g.hbuf.at[mb, pl.ds(0, c.n - 1)], g.sem_hs.at[mb], 1)
        mean, scale = joint_moments(g.hbuf[mb], float(crops))
        g.hst[mb, 0:1] = mean
        g.hst[mb, 1:2] = scale
        gain = scale * g.hidden_gain[...]
        bias = g.hidden_bias[...] - mean * gain
        act = silu(g.hall[c.p % 4, c.p // 4, mb].astype(F32) * gain + bias).astype(BF16)
        g.pe[mb] = nn(act, g.w2[...])
        trade(mb).start()

    def embed(mb):
        trade(mb).wait_recv()
        g.em2[mb] = (g.pe[mb] + g.pr[mb]).reshape(2, part, -1)
        g.gath[mb, c.p, c.h] = g.em2[mb, c.h]
        c.spread(g.em2.at[mb, c.h], g.gath.at[mb, c.p, c.h], g.sem_hg.at[mb])

    def mirror(mb):
        c.take(others(mb), g.sem_hg.at[mb], 1)
        swap(mb).start()

    def arrive(mb):
        swap(mb).wait_recv()

    def relay(name, stage):
        ref, sems = (g.hall, g.sem_hh) if name == "h" else (g.pall, g.sem_pa)
        if stage == 0 and name == "p":
            g.pall[c.p % 4, c.p // 4] = g.po[...]
        if stage > 0:
            c.relay_wait(ref, sems, stage - 1, 1)
        if stage < 3:
            for copy in c.relay(ref, sems, stage):
                copy.start()

    def direct(ref, sems):
        own = ref.at[c.p % 4, c.p // 4]
        c.spread(own, own, sems.at[0])
        for which in (1, 0):
            c.take(ref.at[pl.ds(0, 3)], sems.at[0], which)
            c.take(ref.at[0, pl.ds(0, c.n // 4 - 1)], sems.at[0], which)

    def pooled_swap():
        return c.partner(g.pall, g.qall, g.sem_pq)

    def end():
        pooled_swap().wait_send()
        for mb in range(nb):
            trade(mb).wait_send()
            swap(mb).wait_send()
            c.take(g.hbuf.at[mb, pl.ds(0, c.n - 1)], g.sem_hs.at[mb], 0)
            c.take(others(mb), g.sem_hg.at[mb], 0)

    def end_relay():
        for ref, sems in ((g.hall, g.sem_hh), (g.pall, g.sem_pa)):
            for stage in range(3):
                c.relay_wait(ref, sems, stage, 0)

    def all_arrive(mb):
        if mb == 0:
            for step in (embed, mirror, arrive):
                for k in range(nb):
                    step(k)
            g.pall[c.p % 4, c.p // 4] = g.po[...]
            direct(g.hall, g.sem_hh)
            direct(g.pall, g.sem_pa)
            pooled_swap().start()
            pooled_swap().wait_recv()

    return Phase(
        pre, post, c.ready, all_arrive, end, embed=embed, mirror=mirror, landed=arrive,
        relay=relay, pooled_swap=pooled_swap, end_relay=end_relay,
    )


def panel_steps(panel, start, lane, level):
    shape = panel.shape
    scaled = jnp.zeros(shape, F32)

    def wide(part):
        return jnp.broadcast_to(part, shape)

    for i in range(0, 8, 2):
        j = start + i
        one, two = lane == j, lane == j + 1
        c1, c2 = wide(panel[:, :, j : j + 1]), wide(panel[:, :, j + 1 : j + 2])
        r1, r2 = wide(panel[:, i : i + 1, :]), wide(panel[:, i + 1 : i + 2, :])
        a, b, d = wide(c1[:, i : i + 1]), wide(c1[:, i + 1 : i + 2]), wide(c2[:, i + 1 : i + 2])
        first = 1.0 / a
        second = a / (a * d - b * b)
        ratio = b * first
        r2 = r2 - ratio * r1
        m1 = jnp.where(one, 1.0, jnp.where(two, 0.0, r1))
        m2 = jnp.where(one, -ratio, jnp.where(two, 1.0, r2))
        l1 = c1 * first
        l2 = (c2 - l1 * b) * second
        cleared = jnp.where(jnp.logical_or(one, two), 0.0, panel)
        new = jnp.where(one, -ratio, r2)
        scaled = jnp.where(level == i, panel * first, jnp.where(level == i + 1, new * second, scaled))
        below = cleared - l1 * m1 - l2 * m2
        panel = jnp.where(level > i + 1, below, jnp.where(level == i + 1, new, panel))
    return panel, scaled


def eliminate(cov, between):
    total, width = cov.shape[0], cov.shape[1]
    pack = 8 * total
    side = -(-pack // width) * width
    lane = lax.broadcasted_iota(jnp.int32, (1, 1, width), 2)
    level = lax.broadcasted_iota(jnp.int32, (1, 8, width), 1)
    which = lax.broadcasted_iota(jnp.int32, (1, side), 1) // 8

    def product(left, right):
        return jnp.dot(left, right, precision=HIGH, preferred_element_type=F32)

    panel = cov[:, 0:8, :]
    for start in range(0, width, 8):
        between(start)
        panel, scaled = panel_steps(panel, start, lane, level)
        cov[:, start : start + 8, :] = panel
        after = start + 8
        if after == width:
            break
        inside = lane - start
        unit = jnp.where(inside == level, 1.0, 0.0)
        rows = jnp.where(jnp.logical_and(inside >= level, inside < 8), unit, panel)
        rows = rows.reshape(pack, width)
        scaled = scaled.reshape(pack, width)
        if side > pack:
            blank = jnp.zeros((side - pack, width), F32)
            rows = jnp.concatenate([rows, blank], axis=0)
            scaled = jnp.concatenate([scaled, blank], axis=0)
        flipped = scaled.T
        kept = jnp.logical_or(lane[0] < start, lane[0] >= after)
        near = flipped[after : after + 8]
        near = jnp.concatenate([jnp.where(which == k, near, 0.0) for k in range(total)], axis=0)
        change = product(near, rows).reshape(total, 8, width)
        panel = jnp.where(kept[None], cov[:, after : after + 8, :], 0.0) - change
        if after + 8 == width:
            continue
        far = flipped[after + 8 :]
        for k in range(total):
            change = product(jnp.where(which == k, far, 0.0), rows)
            cov[k, after + 8 :, :] = jnp.where(kept, cov[k, after + 8 :, :], 0.0) - change


def split(values):
    high = values.astype(BF16)
    return high, (values - high.astype(F32)).astype(BF16)


def fine(product, left, right):
    (a, b), (p, q) = split(left), split(right)
    return product(a, p) + (product(a, q) + product(b, p))


def whiten(g, c):
    nb, count = g.order.shape
    subs = g.sizes.shape[1]
    width = g.gath.shape[-1]
    pairs = g.pairs.shape[2]
    shape = (width, width)
    eye = lax.broadcasted_iota(jnp.int32, shape, 0) == lax.broadcasted_iota(jnp.int32, shape, 1)
    eye = eye.astype(F32)
    lower = lax.broadcasted_iota(jnp.int32, shape, 0) >= lax.broadcasted_iota(jnp.int32, shape, 1)
    lower = lower.astype(F32)
    strict = lower - eye
    crop_id = lax.broadcasted_iota(jnp.int32, (count, 1), 0)
    place = lax.broadcasted_iota(jnp.int32, (1, count), 1)

    def masks(mb):
        member = g.member[mb]
        return [(member == float(k)).astype(F32) for k in range(subs)]

    def apart(values, inside):
        return jnp.concatenate([values * mask for mask in inside], axis=1)

    def prepare(mb):
        end = jnp.int32(0)
        segment = jnp.zeros((1, count), F32)
        for k in range(subs - 1):
            end = end + g.sizes[mb, k]
            segment = segment + (place >= end).astype(F32)
        order = g.order[mb : mb + 1, :]
        member = jnp.sum(jnp.where(order == crop_id, segment, 0.0), axis=1, keepdims=True)
        g.member[mb] = jnp.broadcast_to(member, (count, width))
        embed = g.gath[mb].reshape(count, width)
        centred = jnp.zeros((count, width), F32)
        inside = masks(mb)
        for k in range(subs):
            centre = jnp.sum(embed * inside[k], axis=0, keepdims=True) / g.sizes[mb, k].astype(F32)
            centred = centred + (embed - centre) * inside[k]
        both = fine(tn, apart(centred, inside), centred)
        for k in range(subs):
            part = both[k * width : (k + 1) * width] / g.sizes[mb, k].astype(F32)
            g.cov[mb * subs + k] = part + RIDGE * eye
        g.cent[mb] = centred

    def factor_all(between):
        eliminate(g.cov, between)
        for k in range(nb * subs):
            inverse = g.cov[k]
            power = jnp.sum(inverse * eye, axis=1, keepdims=True)
            g.cov[k] = lax.rsqrt(power) * (inverse * strict + eye)
        g.loss[...] = jnp.zeros(g.loss.shape, F32)

    def rest(mb):
        inside = masks(mb)
        inverses = [g.cov[mb * subs + k] for k in range(subs)]
        white = fine(nt, apart(g.cent[mb], inside), jnp.concatenate(inverses, axis=1))
        power = jnp.sum(white * white, axis=1, keepdims=True)
        factor = lax.rsqrt(power + EPS_NORM)
        normed = white * factor
        first, second = g.pairs[mb, 0:1] == crop_id, g.pairs[mb, 1:2] == crop_id
        choose = (first.astype(F32) - second.astype(F32)).astype(BF16)
        high, rest_of = split(normed)
        differ = tn(choose, high) + tn(choose, rest_of)
        g.loss[...] = g.loss[...] + jnp.sum(differ * differ) * (1.0 / (pairs * nb))
        high, rest_of = split(differ)
        grad = (nn(choose, high) + nn(choose, rest_of)) * (2.0 * LOSS_SCALE / (nb * pairs))
        inner = jnp.sum(grad * white, axis=1, keepdims=True)
        grad = grad * factor - white * (factor * factor * factor * inner)
        low = tn(apart(grad, inside).astype(BF16), white.astype(BF16))
        sides, shift, shares = [], jnp.zeros((count, width), F32), []
        for k in range(subs):
            size = g.sizes[mb, k].astype(F32)
            part = low[k * width : (k + 1) * width]
            sides.append((part * lower + (part * strict).T).astype(BF16))
            shares.append(inside[k] / size)
            shift = shift + shares[k] * jnp.sum(grad * inside[k], axis=0, keepdims=True)
        shift = shift + nn(apart(white, shares).astype(BF16), jnp.concatenate(sides, axis=0))
        inverses = jnp.concatenate(inverses, axis=0).astype(BF16)
        delta = nn(apart(grad - shift, inside).astype(BF16), inverses)
        g.ed[mb] = delta.astype(BF16)

    def post(mb):
        if mb == 0:
            factor_all(lambda start: None)
        rest(mb)

    return Phase(prepare, post, factor_all=factor_all, rest=rest)


def hidden_backward(g, c):
    nb, crops, half = g.pg.shape
    count, hid = c.n * crops, g.hall.shape[4]
    chunk = 256

    def give():
        return c.partner(g.pgs, g.pgr, g.sem_hp)

    def rows_of(ref, mb, lo, size, cols):
        parts = []
        for z in range(lo // (4 * crops), (lo + size) // (4 * crops)):
            parts.append(ref[:, z, mb, :, cols].reshape(4 * crops, -1))
        return jnp.concatenate(parts, axis=0)

    def run():
        totals = jnp.zeros((2, hid), F32)
        emb = jnp.zeros(g.gemb.shape, F32)
        for mb in range(nb):
            mean, scale = g.hst[mb, 0:1], g.hst[mb, 1:2]
            shift = -mean * scale
            one = two = jnp.zeros((1, hid), F32)
            for lo in range(0, count, chunk):
                at = pl.ds(lo, chunk)
                part = rows_of(g.hall, mb, lo, chunk, slice(None))
                normal = part.astype(F32) * scale + shift
                value = normal * g.hidden_gain[...] + g.hidden_bias[...]
                gate = sigmoid(value)
                delta = g.ed[mb, at]
                emb = emb + tn((value * gate).astype(BF16), delta)
                grad = nt(delta, g.w2[...]) * (gate * (1.0 + value * (1.0 - gate)))
                one = one + jnp.sum(grad, axis=0, keepdims=True)
                two = two + jnp.sum(grad * normal, axis=0, keepdims=True)
                g.hgf[at] = grad
            sums = jnp.concatenate([one, two], axis=0)
            totals = totals + sums
            a, b, k = norm_terms(g.hst, mb, g.hidden_gain[...], sums, float(count))
            for lo in range(0, count, chunk):
                at = pl.ds(lo, chunk)
                part = rows_of(g.hall, mb, lo, chunk, slice(None))
                g.hd[mb, at] = (g.hgf[at] * a + part.astype(F32) * b + k).astype(BF16)
        g.hbias[...] = totals[0:1]
        g.hgain[...] = totals[1:2]
        g.gemb[...] = emb
        c.ready()
        for mb in range(nb):
            own = g.hd[mb, rows_at(c.p * crops, crops)]
            g.pgs[mb] = nt(own, g.wh[c.half(c.o, half), :]).astype(BF16)
        give().start()

    def finish():
        for mb in range(nb):
            own = g.hd[mb, rows_at(c.p * crops, crops)]
            g.pg[mb] = nt(own, g.wh[c.half(c.h, half), :])
        give().wait_recv()
        g.pg[...] = (g.pg[...] + g.pgr[...].astype(F32)) * (1.0 / AREA)

    def weights():
        hd = g.hd[...].reshape(nb * count, hid)
        lanes = 256
        for which, rows in ((c.h, g.pall), (c.o, g.qall)):
            for lo in range(0, half, lanes):
                part = [rows_of(rows, mb, 0, count, slice(lo, lo + lanes)) for mb in range(nb)]
                part = jnp.concatenate(part, axis=0)
                g.ghid[rows_at(which * half + lo, lanes), :] = tn(part, hd).astype(BF16)

    def end():
        give().wait_send()

    def pre(mb):
        if mb == 0:
            for step in (run, finish, weights):
                step()

    return Phase(pre, lambda mb: None, None, None, end, run=run, weights=weights, finish=finish)


def expand_backward(g, c):
    nb, rows, half = g.epre.shape
    crops = rows // AREA
    mid = g.we.shape[0]
    lanes = 256
    total_rows = float(rows) * c.n

    def pre(mb):
        if mb == 0:
            g.egain[...] = jnp.zeros(g.egain.shape, F32)
            g.ebias[...] = jnp.zeros(g.ebias.shape, F32)
        for lo in range(0, half, lanes):
            cols = pl.ds(lo, lanes)
            scale = g.est[mb, 1:2, cols]
            shift = -g.est[mb, 0:1, cols] * scale
            grad = g.pg[mb, :, cols]

            def pixels(i, carry):
                one, two = carry
                for j in range(SIDE):
                    at = rows_at((i * SIDE + j) * crops, crops)
                    normal = g.epre[mb, at, cols].astype(F32) * scale + shift
                    part = grad * g.slo[mb, at, cols].astype(F32)
                    g.sg[mb, at, cols] = part.astype(BF16)
                    one = one + part
                    two = two + part * normal
                return one, two

            zero = jnp.zeros((crops, lanes), F32)
            one, two = lax.fori_loop(0, SIDE, pixels, (zero, zero))
            g.ebm[mb, 0:1, cols] = jnp.sum(one, axis=0, keepdims=True)
            g.ebm[mb, 1:2, cols] = jnp.sum(two, axis=0, keepdims=True)
        g.ebb[mb, c.p] = g.ebm[mb]
        c.spread(g.ebm.at[mb], g.ebb.at[mb, c.p], g.sem_eb.at[mb])

    def give(mb):
        return c.partner(g.mgs.at[mb], g.mgr.at[mb], g.sem_mg.at[mb])

    def swap():
        return c.partner(g.gxs, g.gexp.at[c.half(c.h, mid)], g.sem_gx)

    def delta(mb):
        c.take(g.ebb.at[mb, pl.ds(0, c.n - 1)], g.sem_eb.at[mb], 1)
        g.ebt[...] = jnp.sum(g.ebb[mb], axis=0)
        g.ebias[...] = g.ebias[...] + g.ebt[0:1]
        g.egain[...] = g.egain[...] + g.ebt[1:2]
        for lo in range(0, half, lanes):
            cols = pl.ds(lo, lanes)
            scale = g.est[mb, 1:2, cols]
            gain = g.expand_gain[:, cols] * scale
            slant = gain * g.ebt[1:2, cols] * (-1.0 / total_rows)
            base = gain * g.ebt[0:1, cols] * (-1.0 / total_rows)
            base = base - slant * scale * g.est[mb, 0:1, cols]
            slant = slant * scale

            def pixels(i, carry):
                for j in range(SIDE):
                    at = rows_at((i * SIDE + j) * crops, crops)
                    part = g.sg[mb, at, cols].astype(F32) * gain + base
                    part = part + g.epre[mb, at, cols].astype(F32) * slant
                    g.xd[mb, at, cols] = part.astype(BF16)
                return carry

            lax.fori_loop(0, SIDE, pixels, 0)

    def middle(mb):
        g.mgs[mb] = nt(g.xd[mb], g.wep[...]).astype(BF16)
        give(mb).start()
        g.mg[mb] = nt(g.xd[mb], g.we[:, c.half(c.h, half)])

    def post(mb):
        delta(mb)
        middle(mb)

    def weights():
        xd = g.xd[...].reshape(nb * rows, half)
        g.gxs[...] = tn(g.mp[...].reshape(nb * rows, mid), xd).astype(BF16)
        swap().start()
        g.gexp[c.half(c.h, mid), :] = tn(g.mo[...].reshape(nb * rows, mid), xd).astype(BF16)

    def arrive(mb):
        give(mb).wait()
        g.mg[mb] = g.mg[mb] + g.mgr[mb].astype(F32)

    def weights_in():
        swap().wait_recv()

    def end():
        swap().wait_send()
        for mb in range(nb):
            c.take(g.ebb.at[mb, pl.ds(0, c.n - 1)], g.sem_eb.at[mb], 0)

    def end_alone():
        weights()
        weights_in()
        end()

    return Phase(
        pre, post, c.ready, arrive, end_alone, weights=weights, weights_in=weights_in, close=end,
        delta=delta, middle=middle,
    )


def norm_slopes(c, mb, grad, pre, stats, gain, bias, sums, buf, sem, out):
    rows, mid = pre.shape[1:]
    scale = stats[mb, 1:2]
    shift = -stats[mb, 0:1] * scale
    chunk = rows // SIDE

    def image_row(i, carry):
        one, two = carry
        at = rows_at(i * chunk, chunk)
        normal = pre[mb, at].astype(F32) * scale + shift
        part = grad[mb, at] * slope(normal * gain[...] + bias[...])
        out[mb, at] = part
        one = one + jnp.sum(part.reshape(-1, 8, mid), axis=0)
        two = two + jnp.sum((part * normal).reshape(-1, 8, mid), axis=0)
        return one, two

    zero = jnp.zeros((8, mid), F32)
    one, two = lax.fori_loop(0, SIDE, image_row, (zero, zero))
    sums[mb, 0:1] = jnp.sum(one, axis=0, keepdims=True)
    sums[mb, 1:2] = jnp.sum(two, axis=0, keepdims=True)
    buf[mb, c.p] = sums[mb]
    c.spread(sums.at[mb], buf.at[mb, c.p], sem.at[mb])


def norm_terms(stats, mb, gain, sums, count):
    scale = stats[mb, 1:2]
    a = gain * scale
    slant = a * sums[1:2] * (-1.0 / count)
    k = a * sums[0:1] * (-1.0 / count) - slant * scale * stats[mb, 0:1]
    return a, slant * scale, k


def middle_backward(g, c):
    nb, rows, mid = g.mpre.shape
    crops = rows // AREA
    long = conv_rows(crops)
    count = float(rows) * c.n

    def begin():
        c.ready()
        g.mdg[...] = jnp.zeros(g.mdg.shape, BF16)
        g.mgain[...] = jnp.zeros(g.mgain.shape, F32)
        g.mbias[...] = jnp.zeros(g.mbias.shape, F32)

    def pre(mb):
        norm_slopes(
            c, mb, g.mg, g.mpre, g.mst, g.middle_gain, g.middle_bias, g.mbm, g.mbb,
            g.sem_mb, g.mgf,
        )

    def give(mb):
        return c.partner(g.ags.at[mb], g.agr.at[mb], g.sem_ag.at[mb])

    def delta(mb):
        c.take(g.mbb.at[mb, pl.ds(0, c.n - 1)], g.sem_mb.at[mb], 1)
        sums = jnp.sum(g.mbb[mb], axis=0)
        g.mbias[...] = g.mbias[...] + sums[0:1]
        g.mgain[...] = g.mgain[...] + sums[1:2]
        a, b, k = norm_terms(g.mst, mb, g.middle_gain[...], sums, count)
        for i in range(SIDE):
            at = pl.ds(i * SIDE * crops, SIDE * crops)
            part = g.mgf[mb, at] * a + g.mpre[mb, at].astype(F32) * b + k
            g.mdg[mb, pl.ds((WIDE + 1 + WIDE * i) * crops, SIDE * crops)] = part.astype(BF16)
        g.mdt[:, mb * long : (mb + 1) * long] = g.mdg[mb, pl.ds((WIDE + 1) * crops, long)].T

    def spread(mb):
        for which, place in ((c.o, 0), (c.h, 1)):
            total = None
            for tap in range(9):
                at = pl.ds((WIDE * (2 - tap // 3) + 2 - tap % 3) * crops, long)
                part = nt(g.mdg[mb, at], g.wm[tap, c.half(which, mid), :])
                total = part if total is None else total + part
            for i in range(SIDE):
                at = pl.ds(i * SIDE * crops, SIDE * crops)
                part = total[i * WIDE * crops : (i * WIDE + SIDE) * crops]
                if place == 0:
                    g.ags[mb, at] = part.astype(BF16)
                else:
                    g.ag[mb, at] = part
            if place == 0:
                give(mb).start()

    def weights(out, first, taps):
        def one(i):
            tap = first + i
            at = pl.ds(pl.multiple_of((WIDE * (tap // 3) + tap % 3) * crops, crops), long)
            for act, which in ((g.ao, c.h), (g.ap, c.o)):
                field = jnp.concatenate([act[mb, at] for mb in range(nb)], axis=0)
                part = nn(g.mdt[...], field)
                out[c.half(2 * i + which, mid), :] = part.T.astype(BF16)

        each(taps, one)

    def arrive(mb):
        give(mb).wait()
        g.ag[mb] = g.ag[mb] + g.agr[mb].astype(F32)

    def end():
        for mb in range(nb):
            c.take(g.mbb.at[mb, pl.ds(0, c.n - 1)], g.sem_mb.at[mb], 0)

    def post(mb):
        delta(mb)
        spread(mb)

    def all_weights():
        weights(g.gmida, 0, 3)
        weights(g.gmidb, 3, 3)
        weights(g.gmidc, 6, 3)

    def end_alone():
        all_weights()
        end()

    return Phase(
        pre, post, begin, arrive, end_alone, delta=delta, spread=spread, weights=weights, close=end
    )


def stem_backward(g, c):
    nb, rows, mid = g.spre.shape
    half = g.x.shape[2]
    crops = rows // AREA
    count = float(rows) * c.n

    def begin():
        c.ready()
        g.sgain[...] = jnp.zeros(g.sgain.shape, F32)
        g.sbias[...] = jnp.zeros(g.sbias.shape, F32)

    def pre(mb):
        norm_slopes(
            c, mb, g.ag, g.spre, g.sst, g.stem_gain, g.stem_bias, g.sbm, g.sbb,
            g.sem_sb, g.sgf,
        )

    def give(mb):
        return c.partner(g.sd.at[mb], g.sdp.at[mb], g.sem_sd.at[mb])

    def swap():
        return c.partner(g.gss, g.gstem.at[c.half(c.h, half)], g.sem_gs)

    def post(mb):
        c.take(g.sbb.at[mb, pl.ds(0, c.n - 1)], g.sem_sb.at[mb], 1)
        sums = jnp.sum(g.sbb[mb], axis=0)
        g.sbias[...] = g.sbias[...] + sums[0:1]
        g.sgain[...] = g.sgain[...] + sums[1:2]
        a, b, k = norm_terms(g.sst, mb, g.stem_gain[...], sums, count)
        for i in range(SIDE):
            at = pl.ds(i * SIDE * crops, SIDE * crops)
            g.sd[mb, at] = (g.sgf[mb, at] * a + g.spre[mb, at].astype(F32) * b + k).astype(BF16)
        give(mb).start()

    def weights():
        lanes = 256
        sd = g.sd[...].reshape(nb * rows, mid)
        sdp = g.sdp[...].reshape(nb * rows, mid)
        for lo in range(0, half, lanes):
            field = g.x[:, :, lo : lo + lanes].reshape(nb * rows, lanes)
            g.gss[lo : lo + lanes] = tn(field, sdp).astype(BF16)
            own = rows_at(c.h * half + lo, lanes)
            g.gstem[own, :] = tn(field, sd).astype(BF16)
        swap().start()

    def weights_in():
        swap().wait_recv()

    def end():
        swap().wait_send()
        for mb in range(nb):
            give(mb).wait_send()
            c.take(g.sbb.at[mb, pl.ds(0, c.n - 1)], g.sem_sb.at[mb], 0)

    def end_alone():
        weights()
        weights_in()
        end()

    return Phase(
        pre, post, begin, lambda mb: give(mb).wait_recv(), end_alone, weights=weights,
        weights_in=weights_in, close=end,
    )


def crops_backward(g, c):
    half = g.wsp.shape[0]

    def pre(mb):
        part = nt(g.sd[mb], g.ws[c.half(c.h, half), :]) + nt(g.sdp[mb], g.wsp[...])
        g.gcrops[mb] = (part + g.sg[mb].astype(F32)).astype(BF16)

    return Phase(pre, lambda mb: None)


class Total:
    def __init__(self, c, local, place, one, two, three, sems):
        self.done = 0
        self.c, self.local, self.place, self.sems = c, local, place, sems
        self.one, self.two, self.three = one, two, three
        self.long = local.shape[0] // 2
        x, y, self.z = c.p % 2, (c.p // 2) % 2, c.p // 4
        step_x, step_y = c.p + 1 - 2 * x, c.p + 2 - 4 * y
        self.ways = ((x, step_x, y, step_y), (y, step_y, x, step_x))
        self.half, self.quarter, self.piece = self.long // 2, self.long // 4, self.long // 16

    def copy(self, stream, step, src, dst, device):
        return pltpu.make_async_remote_copy(
            src_ref=src,
            dst_ref=dst,
            send_sem=self.sems.at[stream, step, 0],
            recv_sem=self.sems.at[stream, step, 1],
            device_id=(device, self.c.h),
            device_id_type=MESH,
        )

    def at(self, start, size):
        return pl.ds(pl.multiple_of(start, 16), size)

    def start(self, step):
        for stream in range(2):
            b1, d1, b2, d2 = self.ways[stream]
            base = stream * self.long
            kept = base + b1 * self.half
            core = kept + b2 * self.quarter
            if step == 0:
                src = self.local.at[self.at(base + (1 - b1) * self.half, self.half)]
                self.copy(stream, step, src, self.one.at[stream], d1).start()
            elif step == 1:
                src = self.one.at[stream, self.at((1 - b2) * self.quarter, self.quarter)]
                self.copy(stream, step, src, self.two.at[stream], d2).start()
            elif step == 4:
                self.keep(stream, core).wait()
                src = self.place(stream, core, self.quarter)
                self.copy(stream, step, src, src, d2).start()
            elif step == 5:
                src = self.place(stream, kept, self.half)
                self.copy(stream, step, src, src, d1).start()
            else:
                if step == 3:
                    self.keep(stream, core).start()
                for d in range(1, 4):
                    other = (self.z + d) % 4
                    device = self.c.p + 4 * (other - self.z)
                    if step == 2:
                        src = self.two.at[stream, self.at(other * self.piece, self.piece)]
                        dst = self.three.at[stream, 3 - d]
                    else:
                        src = self.two.at[stream, self.at(self.z * self.piece, self.piece)]
                        dst = self.place(stream, core + self.z * self.piece, self.piece)
                    self.copy(stream, step, src, dst, device).start()

    def keep(self, stream, core):
        piece = self.at(self.z * self.piece, self.piece)
        place = self.place(stream, core + self.z * self.piece, self.piece)
        return pltpu.make_async_copy(self.two.at[stream, piece], place, self.sems.at[stream, 6, 0])

    def wait(self, stream, step, which):
        blocks = {0: self.one, 1: self.two, 2: self.three, 3: self.three, 4: self.two, 5: self.one}
        self.c.take(blocks[step].at[stream], self.sems.at[stream, step], which)

    def take(self, step):
        for stream in range(2):
            self.wait(stream, step, 1)
            b1, d1, b2, d2 = self.ways[stream]
            kept = stream * self.long + b1 * self.half
            core = kept + b2 * self.quarter
            one, two, three = self.one.at[stream], self.two.at[stream], self.three.at[stream]
            if step == 0:
                self.add(one, 0, [(one, 0), (self.local, kept)], self.half)
            elif step == 1:
                self.add(two, 0, [(two, 0), (one, b2 * self.quarter)], self.quarter)
            elif step == 2:
                terms = [(two, self.z * self.piece)] + [(three.at[d], 0) for d in range(3)]
                self.add(two, self.z * self.piece, terms, self.piece)

    def add(self, out, start, terms, size):
        fits = 2**14 // self.local.shape[1]
        chunk = max(k for k in range(16, fits + 1, 16) if size % k == 0)

        def one(i):
            total = None
            for ref, begin in terms:
                value = ref[pl.ds(pl.multiple_of(begin + i * chunk, 16), chunk), :].astype(F32)
                total = value if total is None else total + value
            out[pl.ds(pl.multiple_of(start + i * chunk, 16), chunk), :] = total.astype(BF16)

        each(size // chunk, one)

    def step(self):
        self.take(self.done)
        self.done += 1
        if self.done < 6:
            self.start(self.done)

    def close(self):
        for stream in range(2):
            for step in range(6):
                self.wait(stream, step, 0)


def whole_step(g, c):
    nb, half = g.x.shape[0], g.x.shape[2]
    mid = g.ws.shape[1]
    c.load("ws", 0, g.ws_in, g.ws, g.sem_in.at[0])
    for mb in range(nb):
        c.load("x", mb, g.x_in.at[mb], g.x.at[mb], g.sem_in.at[4 + mb])
    c.load("we", 0, g.we_in, g.we, g.sem_in.at[1])
    c.load("wm", 0, g.wm_in, g.wm, g.sem_in.at[2])
    c.load("wh", 0, g.wh_in, g.wh, g.sem_in.at[3])
    stem, middle, expand = stem_forward(g, c), middle_forward(g, c), expand_forward(g, c)
    hidden, white, hback = hidden_forward(g, c), whiten(g, c), hidden_backward(g, c)
    eback, mback, sback = expand_backward(g, c), middle_backward(g, c), stem_backward(g, c)
    field = crops_backward(g, c)

    def chain(first, second):
        first.post(0)
        for mb in range(1, nb):
            first.post(mb)
            first.arrive(mb - 1)
            second.pre(mb - 1)
        first.arrive(nb - 1)
        second.pre(nb - 1)

    stem.begin()
    expand.early()
    for mb in range(nb):
        stem.pre(mb)
    chain(stem, middle)
    expand.weights()
    chain(middle, expand)
    chain(expand, hidden)
    for step in (hidden.post, hidden.embed, hidden.mirror):
        for mb in range(nb):
            step(mb)
    hidden.relay("h", 0)
    hidden.relay("p", 0)
    for mb in range(nb):
        hidden.landed(mb)
        white.pre(mb)

    def between(start):
        if start == 40:
            hidden.relay("h", 1)
        if start == 72:
            hidden.relay("h", 2)
        if start == 104:
            hidden.relay("p", 1)

    white.factor_all(between)
    for mb in range(nb):
        white.rest(mb)
    hidden.relay("p", 2)
    for phase in (stem, middle, expand):
        phase.end()

    def rows_of(out, first):
        return lambda stream, start, size: out.at[pl.ds(pl.multiple_of(first + start, 16), size)]

    def halves_of(out):
        def place(stream, start, size):
            at = pl.ds(pl.multiple_of(start - stream * mid, 16), size)
            return out.at[at, pl.ds(stream * half, half)]

        return place

    third = g.gmida.shape[0]
    exp = Total(c, g.gexp, halves_of(g.gexp_t), g.gexp_1, g.gexp_2, g.gexp_3, g.sem_gexp)
    place = [rows_of(g.gmid_t, i * third) for i in range(3)]
    one = Total(c, g.gmida, place[0], g.gmida_1, g.gmida_2, g.gmida_3, g.sem_gmida)
    two = Total(c, g.gmidb, place[1], g.gmidb_1, g.gmidb_2, g.gmidb_3, g.sem_gmidb)
    three = Total(c, g.gmidc, place[2], g.gmidc_1, g.gmidc_2, g.gmidc_3, g.sem_gmidc)
    last, rest = (
        Total(
            c, g.gstem.at[pl.ds(i * half, half)], rows_of(g.gstem_t, i * half), g.gstem_1.at[i],
            g.gstem_2.at[i], g.gstem_3.at[i], g.sem_gstem.at[i],
        )
        for i in range(2)
    )
    keep = pltpu.make_async_copy(g.ghid, g.ghid_t, g.sem_in.at[0])

    hidden.relay("h", 3)
    hback.run()
    hback.finish()
    for mb in range(nb):
        eback.pre(mb)
    mback.begin()
    sback.begin()
    eback.delta(0)
    eback.delta(1)
    eback.delta(2)
    eback.weights()
    eback.middle(0)
    eback.weights_in()
    exp.start(0)
    eback.middle(1)
    eback.arrive(0)
    mback.pre(0)
    eback.middle(2)
    eback.arrive(1)
    mback.pre(1)
    eback.arrive(2)
    mback.pre(2)
    hidden.relay("p", 3)
    hidden.pooled_swap().start()
    mback.delta(0)
    exp.step()
    mback.delta(1)
    mback.delta(2)
    mback.weights(g.gmida, 0, 3)
    exp.step()
    one.start(0)
    mback.weights(g.gmidb, 3, 3)
    two.start(0)
    mback.weights(g.gmidc, 6, 3)
    three.start(0)
    mback.spread(0)
    exp.step()
    one.step()
    mback.spread(1)
    two.step()
    mback.arrive(0)
    sback.pre(0)
    mback.spread(2)
    exp.step()
    one.step()
    three.step()
    mback.arrive(1)
    sback.pre(1)
    mback.arrive(2)
    sback.pre(2)
    two.step()
    sback.post(0)
    sback.post(1)
    exp.step()
    one.step()
    three.step()
    sback.post(2)
    for mb in range(nb):
        sback.arrive(mb)
    sback.weights()
    two.step()
    sback.weights_in()
    exp.step()
    one.step()
    last.start(0)
    rest.start(0)
    field.pre(0)
    field.pre(1)
    field.pre(2)
    one.step()
    three.step()
    hidden.pooled_swap().wait_recv()
    hback.weights()
    keep.start()
    last.step()
    two.step()
    rest.step()
    three.step()
    one.step()
    last.step()
    two.step()
    rest.step()
    last.step()
    three.step()
    rest.step()
    two.step()
    last.step()
    rest.step()
    three.step()
    last.step()
    rest.step()
    last.step()
    rest.step()
    gains = (g.sgain, g.sbias, g.mgain, g.mbias, g.egain, g.ebias, g.hgain, g.hbias)
    for row, value in enumerate(gains):
        g.norms[row : row + 1, : value.shape[1]] = value[...]
    hidden.end()
    hidden.end_relay()
    hback.end()
    for phase in (eback, mback, sback):
        phase.close()
    for total in (exp, one, two, three, last, rest):
        total.close()
    keep.wait()


def widen(arrays, norms, widths):
    whole = [(array.shape, 2 if array.size > 2**20 else 1) for array in arrays]
    parts = []
    for number, (shape, cuts) in enumerate(whole):
        if len(shape) == 3:
            cut = -(-shape[1] // 32) * 16
            parts += [
                (number, (i, pl.ds(start, size)), (size, shape[2]))
                for i in range(shape[0])
                for start, size in ((0, cut), (cut, shape[1] - cut))
            ]
        else:
            size = shape[0] // cuts
            parts += [(number, (pl.ds(i * size, size),), (size, shape[1])) for i in range(cuts)]
    count, many = len(arrays), len(parts)

    def kernel(*refs):
        sources, lines = refs[:count], refs[count]
        results = refs[count + 1 : 2 * count + 1]
        rows = refs[2 * count + 1 : 2 * count + 1 + len(widths)]
        narrow = refs[2 * count + 1 + len(widths) : 2 * count + 1 + len(widths) + many]
        wide = refs[2 * count + 1 + len(widths) + many : -2]
        sem_a, sem_b = refs[-2:]
        ins, outs = [], []
        for i, (number, where, _) in enumerate(parts):
            ins.append(pltpu.make_async_copy(sources[number].at[where], narrow[i], sem_a.at[i]))
            outs.append(pltpu.make_async_copy(wide[i], results[number].at[where], sem_b.at[i]))
            ins[i].start()
        for row, width in enumerate(widths):
            rows[row][...] = lines[row : row + 1, :width]
        for i, (_, _, (tall, _)) in enumerate(parts):
            ins[i].wait()

            def cast(j, i=i):
                at = rows_at(j * 16, 16)
                wide[i][at, :] = narrow[i][at, :].astype(F32)

            each(tall // 16, cast)
            outs[i].start()
        for copy in outs:
            copy.wait()

    hbm, vmem = pl.BlockSpec(memory_space=pl.ANY), pl.BlockSpec(memory_space=pltpu.VMEM)
    results = pl.pallas_call(
        kernel,
        out_shape=[jax.ShapeDtypeStruct(array.shape, F32) for array in arrays]
        + [jax.ShapeDtypeStruct((1, width), F32) for width in widths],
        in_specs=[hbm] * count + [vmem],
        out_specs=[hbm] * count + [vmem] * len(widths),
        scratch_shapes=[pltpu.VMEM(size, BF16) for _, _, size in parts]
        + [pltpu.VMEM(size, F32) for _, _, size in parts]
        + [DMA((many,)), DMA((many,))],
        compiler_params=pltpu.CompilerParams(vmem_limit_bytes=60 * 2**20),
        name="widen",
    )(*arrays, norms)
    return results[:count], results[count:]


NORMS = ("sgain", "sbias", "mgain", "mbias", "egain", "ebias", "hgain", "hbias")
GRADS = ("gexp", "gmida", "gmidb", "gmidc", "gstem")


def names_of(functions):
    found, codes = set(), [function.__code__ for function in functions]
    while codes:
        code = codes.pop()
        found |= set(code.co_names)
        codes += [value for value in code.co_consts if isinstance(value, types.CodeType)]
    return found


def body(
    crops_in, stem_weight, middle_weight, expand_weight, stem_gain, stem_bias, middle_gain,
    middle_bias, expand_gain, expand_bias, hidden_weight, hidden_gain, hidden_bias, embed_weight,
    sub_sizes, crop_order, pair_index,
):
    nb, crops, area, half = crops_in.shape
    n = lax.axis_size("dp")
    rows = crops * area
    mid = stem_weight.shape[1]
    hid = hidden_weight.shape[1]
    width = embed_weight.shape[1]
    count = crop_order.shape[1]
    subs = sub_sizes.shape[1]
    long = conv_rows(crops)
    tall = long + 2 * (WIDE + 1) * crops

    def line(v):
        return v.reshape(1, -1)

    env = dict(
        x=crops_in.transpose(0, 2, 1, 3).reshape(nb, rows, half),
        ws=stem_weight,
        wm=middle_weight,
        we=expand_weight,
        wh=hidden_weight,
        w2=embed_weight,
        stem_gain=line(stem_gain),
        stem_bias=line(stem_bias),
        middle_gain=line(middle_gain),
        middle_bias=line(middle_bias),
        expand_gain=line(expand_gain),
        expand_bias=line(expand_bias),
        hidden_gain=line(hidden_gain),
        hidden_bias=line(hidden_bias),
        sizes=sub_sizes,
        order=crop_order,
        pairs=pair_index.transpose(0, 2, 1),
    )
    table = dict(
        wsp=((half, mid), BF16),
        spre=((nb, rows, mid), BF16),
        sst=((nb, 2, mid), F32),
        ao=((nb, tall, mid), BF16),
        ap=((nb, tall, mid), BF16),
        ss=((nb, rows, mid), BF16),
        sr=((nb, rows, mid), BF16),
        sm=((nb, 2, mid), F32),
        sbuf=((nb, n, 2, mid), F32),
        mpre=((nb, rows, mid), BF16),
        mst=((nb, 2, mid), F32),
        mo=((nb, rows, mid), BF16),
        mp=((nb, rows, mid), BF16),
        mm=((nb, 2, mid), F32),
        mbuf=((nb, n, 2, mid), F32),
        wep=((mid, half), BF16),
        ef=((1, rows, 256), F32),
        em=((1, 2, 256), F32),
        esend=((nb, 2, half), F32),
        ebuf=((nb, n, 2, half), F32),
        epre=((nb, rows, half), BF16),
        est=((nb, 2, half), F32),
        po=((nb, crops, half), BF16),
        pp=((nb, crops, half), BF16),
        hall=((4, n // 4, nb, crops, hid), BF16),
        pall=((4, n // 4, nb, crops, half), BF16),
        qall=((4, n // 4, nb, crops, half), BF16),
        sown=((nb, rows, mid), F32),
        hm=((nb, 2, hid), F32),
        hbuf=((nb, n, 2, hid), F32),
        hst=((nb, 2, hid), F32),
        pe=((nb, crops, width), F32),
        pr=((nb, crops, width), F32),
        em2=((nb, 2, crops // 2, width), F32),
        gath=((nb, n, 2, crops // 2, width), F32),
        member=((nb, count, width), F32),
        cent=((nb, count, width), F32),
        cov=((nb * subs, width, width), F32),
        loss=((1, width), F32),
        ed=((nb, count, width), BF16),
        gemb=((hid, width), F32),
        hgf=((count, hid), F32),
        hgain=((1, hid), F32),
        hbias=((1, hid), F32),
        hd=((nb, count, hid), BF16),
        pgs=((nb, crops, half), BF16),
        pgr=((nb, crops, half), BF16),
        ghid=((2 * half, hid), BF16),
        pg=((nb, crops, half), F32),
        slo=((nb, rows, half), BF16),
        sg=((nb, rows, half), BF16),
        ebm=((nb, 2, half), F32),
        ebt=((2, half), F32),
        ebb=((nb, n, 2, half), F32),
        egain=((1, half), F32),
        ebias=((1, half), F32),
        xd=((nb, rows, half), BF16),
        mgs=((nb, rows, mid), BF16),
        mgr=((nb, rows, mid), BF16),
        mg=((nb, rows, mid), F32),
        gxs=((mid, half), BF16),
        gexp=((2 * mid, half), BF16),
        mdg=((nb, tall, mid), BF16),
        mdt=((mid, nb * long), BF16),
        mgf=((nb, rows, mid), F32),
        mbm=((nb, 2, mid), F32),
        mbb=((nb, n, 2, mid), F32),
        mgain=((1, mid), F32),
        mbias=((1, mid), F32),
        ags=((nb, rows, mid), BF16),
        agr=((nb, rows, mid), BF16),
        ag=((nb, rows, mid), F32),
        gmida=((6 * mid, mid), BF16),
        gmidb=((6 * mid, mid), BF16),
        gmidc=((6 * mid, mid), BF16),
        sgf=((nb, rows, mid), F32),
        sbm=((nb, 2, mid), F32),
        sbb=((nb, n, 2, mid), F32),
        sgain=((1, mid), F32),
        sbias=((1, mid), F32),
        sd=((nb, rows, mid), BF16),
        sdp=((nb, rows, mid), BF16),
        gss=((half, mid), BF16),
        gstem=((2 * half, mid), BF16),
        gcrops=((nb, rows, half), BF16),
    )
    pair = (2,)
    pairs = (nb, 2)
    sems = dict(
        sem_sw=pair, sem_sp=pairs, sem_ss=pairs, sem_sa=pairs, sem_ms=pairs, sem_ma=pairs,
        sem_ew=pair, sem_es=pairs, sem_ep=pairs, sem_hs=pairs, sem_he=pairs, sem_hg=pairs,
        sem_hx=pairs, sem_hh=(3, 2), sem_pa=(3, 2), sem_pq=pair, sem_hp=pair, sem_eb=pairs, sem_mg=pairs, sem_gx=pair,
        sem_mb=pairs, sem_ag=pairs, sem_sb=pairs, sem_sd=pairs, sem_gs=pair,
    )
    phases = [
        stem_forward, middle_forward, expand_forward, hidden_forward, whiten, hidden_backward,
        expand_backward, middle_backward, stem_backward, crops_backward,
    ]
    block = n == 16
    final = set(GRADS) | {"loss", "gcrops", "ghid", "gemb"}
    final |= set(NORMS)
    shared = {}
    if block:
        shared = dict(
            xd="epre", mgs="ss", ags="ss", agr="sr", mgf="mg", ag="mg", sgf="mg", sd="mo",
            sdp="mp", gcrops="sg", slo="sg", sown="mg", ghid="wh",
        )
        groups = [phases + [whole_step]]
        final -= set(GRADS) | set(NORMS) | {"ghid"}
        whole = dict(
            gexp_t=((mid, 2 * half), BF16), gmid_t=((18 * mid, mid), BF16),
            gstem_t=((2 * half, mid), BF16), ghid_t=((2 * half, hid), BF16),
            norms=((8, half), F32),
        )
        final |= set(whole)
        table.update(whole)
        for name in GRADS:
            tall, cols = table[name][0]
            table[name + "_1"] = ((2, tall // 4, cols), BF16)
            table[name + "_2"] = ((2, tall // 8, cols), BF16)
            table[name + "_3"] = ((2, 3, tall // 32, cols), BF16)
            sems["sem_" + name] = (2, 7, 2)
        for name in ("gstem_1", "gstem_2", "gstem_3"):
            (streams, *several, tall, cols), kind = table[name]
            table[name] = ((2, streams, *several, tall // 2, cols), kind)
        sems["sem_gstem"] = (2, 2, 7, 2)
        sems.update(sem_in=(4 + nb,))
        for name in ("x", "ws", "wm", "we", "wh"):
            env[name + "_in"] = env.pop(name)
            table[name] = (env[name + "_in"].shape, BF16)
    else:
        groups = [[phase] for phase in phases]

    vmem = pl.BlockSpec(memory_space=pltpu.VMEM)
    smem = pl.BlockSpec(memory_space=pltpu.SMEM)
    hbm = pl.BlockSpec(memory_space=pl.ANY)
    used = [names_of(group + [norm_slopes, norm_terms]) for group in groups]
    for number, group in enumerate(groups):
        later = final.union(*used[number + 1 :])
        here = used[number]
        reads = [name for name in env if name in here]
        made = [name for name in table if name in here and name not in env]
        sem_names = [name for name in sems if name in here]
        own = [name for name in made if name not in shared]
        bases = {shared[name] for name in made if name in shared and name in later}
        outs = [name for name in own if name in later or name in bases]
        scratch = [name for name in own if name not in outs]
        names = reads + outs + scratch + sem_names
        remote = bool(sem_names)

        def kernel(*refs, group=group, names=names, remote=remote):
            c = Ctx(n, remote, remote)
            g = types.SimpleNamespace(**dict(zip(names, refs)))
            for name, base in shared.items():
                setattr(g, name, getattr(g, base))
            if block:
                whole_step(g, c)
            else:
                group[0](g, c).alone(nb)

        params = dict(vmem_limit_bytes=63 * 2**20)
        if remote:
            params.update(collective_id=number, has_side_effects=True)
        results = pl.pallas_call(
            kernel,
            out_shape=[jax.ShapeDtypeStruct(*table[name]) for name in outs],
            in_specs=[
                smem if name == "sizes" else hbm if name[-3:] == "_in" else vmem for name in reads
            ],
            out_specs=[hbm if name[-2:] == "_t" else vmem for name in outs],
            scratch_shapes=[pltpu.VMEM(*table[name]) for name in scratch]
            + [DMA(sems[name]) for name in sem_names],
            compiler_params=pltpu.CompilerParams(**params),
            name=group[-1].__name__,
        )(*[env[name] for name in reads])
        env.update(zip(outs, results))

    for name, base in shared.items():
        if name in final:
            env[name] = env[base]
    if block:
        widths = [table[name][0][1] for name in NORMS]
        arrays = [env[name] for name in ("gcrops", "gmid_t", "ghid_t", "gexp_t", "gstem_t")]
        (env["gcrops"], gmid, ghid, gexp, gstem), rows_out = widen(arrays, env["norms"], widths)
        env.update(zip(NORMS, rows_out))
    else:
        gexp, *gmid, gstem = lax.psum([env[name] for name in GRADS], "dp")
        gexp = gexp.reshape(2, mid, half).transpose(1, 0, 2).reshape(mid, 2 * half)
        gmid = jnp.concatenate(gmid, axis=0)
        ghid = env["ghid"]
    field = env["gcrops"].astype(F32).reshape(nb, area, crops, half).transpose(0, 2, 1, 3)
    return (
        env["loss"][0, 0],
        field,
        gstem.astype(F32),
        gmid.astype(F32).reshape(9, 2 * mid, mid),
        gexp.astype(F32),
        env["sgain"][0],
        env["sbias"][0],
        env["mgain"][0],
        env["mbias"][0],
        env["egain"][0],
        env["ebias"][0],
        ghid.astype(F32),
        env["hgain"][0],
        env["hbias"][0],
        env["gemb"],
    )


def solution(mesh):
    return jax.shard_map(
        body,
        mesh=mesh,
        in_specs=(
            P(None, "dp", None, "chan"),
            P(None, "chan"),
            P(None, None, "chan"),
            P("chan", None),
            P("chan"),
            P("chan"),
            P("chan"),
            P("chan"),
            P("chan"),
            P("chan"),
            P(None, "chan"),
            P("chan"),
            P("chan"),
            P("chan", None),
            P(),
            P(),
            P(),
        ),
        out_specs=(
            P(),
            P(None, "dp", None, "chan"),
            P(None, "chan"),
            P(None, None, "chan"),
            P("chan", None),
            P("chan"),
            P("chan"),
            P("chan"),
            P("chan"),
            P("chan"),
            P("chan"),
            P(None, "chan"),
            P("chan"),
            P("chan"),
            P("chan", None),
        ),
        check_vma=False,
    )
```

```python
import types

import jax
import jax.numpy as jnp
from jax import lax
from jax.experimental import pallas as pl
from jax.experimental.pallas import tpu as pltpu
from jax.sharding import PartitionSpec as P

SIDE = 7
AREA = SIDE * SIDE
WIDE = SIDE + 1
EPS_NORM = 1e-05
RIDGE = 0.5
LOSS_SCALE = 8192.0
HIGH = lax.Precision.HIGHEST
MESH = pl.DeviceIdType.MESH
F32 = jnp.float32
BF16 = jnp.bfloat16
DMA = pltpu.SemaphoreType.DMA


def nn(left, right):
    return jnp.dot(left, right, preferred_element_type=F32)


def nt(left, right, precision=None):
    return lax.dot_general(
        left, right, (((1,), (1,)), ((), ())), precision=precision, preferred_element_type=F32
    )


def tn(left, right, precision=None):
    return lax.dot_general(
        left, right, (((0,), (0,)), ((), ())), precision=precision, preferred_element_type=F32
    )


def sigmoid(values):
    return 0.5 * jnp.tanh(0.5 * values) + 0.5


def silu(values):
    return values * sigmoid(values)


def slope(values):
    part = sigmoid(values)
    return part * (1.0 + values * (1.0 - part))


def rows_at(start, size):
    return pl.ds(pl.multiple_of(start, size if size % 16 else 16), size)


class Ctx:
    def __init__(self, devices, partner, peers):
        self.n = devices
        self.p = lax.axis_index("dp")
        self.h = lax.axis_index("chan")
        self.o = 1 - self.h
        self.waits = 0
        self.loads = {}
        if partner or peers:
            barrier = pltpu.get_barrier_semaphore()
            if partner:
                pl.semaphore_signal(barrier, inc=1, device_id=(self.p, self.o), device_id_type=MESH)
                self.waits += 1
            if peers:

                def greet(d, carry):
                    pl.semaphore_signal(
                        barrier,
                        inc=1,
                        device_id=(lax.rem(self.p + d, self.n), self.h),
                        device_id_type=MESH,
                    )
                    return carry

                lax.fori_loop(1, self.n, greet, 0)
                self.waits += self.n - 1

    def ready(self):
        if self.waits:
            pl.semaphore_wait(pltpu.get_barrier_semaphore(), self.waits)
            self.waits = 0

    def load(self, name, index, src, dst, sem):
        self.loads[name, index] = pltpu.make_async_copy(src, dst, sem)
        self.loads[name, index].start()

    def loaded(self, name, index=0):
        copy = self.loads.pop((name, index), None)
        if copy is not None:
            copy.wait()

    def half(self, which, size):
        return pl.ds(pl.multiple_of(which * size, size), size)

    def partner(self, src, dst, sems):
        return pltpu.make_async_remote_copy(
            src_ref=src,
            dst_ref=dst,
            send_sem=sems.at[0],
            recv_sem=sems.at[1],
            device_id=(self.p, self.o),
            device_id_type=MESH,
        )

    def spread(self, src, dst, sems):
        def one(d, carry):
            pltpu.make_async_remote_copy(
                src_ref=src,
                dst_ref=dst,
                send_sem=sems.at[0],
                recv_sem=sems.at[1],
                device_id=(lax.rem(self.p + d, self.n), self.h),
                device_id_type=MESH,
            ).start()
            return carry

        lax.fori_loop(1, self.n, one, 0)

    def relay(self, ref, sems, stage):
        q, z = self.p % 4, self.p // 4
        x, y = q % 2, q // 2
        if stage == 0:
            blocks = [(ref.at[q, z], self.p + 4 * ((z + d) % 4 - z)) for d in range(1, 4)]
        else:
            near_x, near_y = self.p + 1 - 2 * x, self.p + 2 - 4 * y
            cols = ref.shape[-1] // 2
            one, two = pl.ds(0, cols), pl.ds(cols, cols)
            if stage == 1:
                blocks = [(ref.at[q, :, :, :, one], near_x), (ref.at[q, :, :, :, two], near_y)]
            else:
                blocks = [(ref.at[pl.ds(2 * y, 2), :, :, :, one], near_y)]
                blocks += [(ref.at[x + 2 * i, :, :, :, two], near_x) for i in range(2)]
        return [
            pltpu.make_async_remote_copy(
                src_ref=block,
                dst_ref=block,
                send_sem=sems.at[stage, 0],
                recv_sem=sems.at[stage, 1],
                device_id=(device, self.h),
                device_id_type=MESH,
            )
            for block, device in blocks
        ]

    def relay_wait(self, ref, sems, stage, which):
        blocks = (ref.at[0, pl.ds(0, 3)], ref.at[0], ref.at[pl.ds(0, 2)])[stage]
        self.take(blocks, sems.at[stage], which)

    def take(self, blocks, sems, which):
        pltpu.make_async_copy(blocks, blocks, sems.at[which]).wait()


class Phase:
    def __init__(self, pre, post, begin=None, arrive=None, end=None, **more):
        nothing = lambda *_: None
        self.pre, self.post = pre, post
        self.begin, self.arrive, self.end = begin or nothing, arrive or nothing, end or nothing
        self.__dict__.update(more)

    def alone(self, nb):
        self.begin()
        for step in (self.pre, self.post, self.arrive):
            for mb in range(nb):
                step(mb)
        self.end()


def each(count, body):
    lax.fori_loop(0, count, lambda i, c: (body(i), c)[1], 0)


def local_moments(ref, mb, rows, chunk, cols, out):
    lanes = 256
    for lo in range(0, cols, lanes):
        at = pl.ds(lo, lanes)

        def add(i, total):
            part = ref[mb, rows_at(i * chunk, chunk), at]
            return total + jnp.sum(part.reshape(-1, 8, lanes), axis=0)

        total = lax.fori_loop(0, rows // chunk, add, jnp.zeros((8, lanes), F32))
        mean = jnp.sum(total, axis=0, keepdims=True) * (1.0 / rows)

        def square(i, total):
            part = ref[mb, rows_at(i * chunk, chunk), at] - mean
            return total + jnp.sum((part * part).reshape(-1, 8, lanes), axis=0)

        total = lax.fori_loop(0, rows // chunk, square, jnp.zeros((8, lanes), F32))
        out[mb, 0:1, at] = mean
        out[mb, 1:2, at] = jnp.sum(total, axis=0, keepdims=True)


def joint_moments(parts, rows):
    n = parts.shape[0]
    mean = jnp.sum(parts, axis=0)[0:1] * (1.0 / n)
    apart = parts[:, 0:1, :] - mean[None]
    squares = jnp.sum(parts, axis=0)[1:2] + rows * jnp.sum(apart * apart, axis=0)
    return mean, lax.rsqrt(squares * (1.0 / (n * rows)) + EPS_NORM)


def stem_forward(g, c):
    nb, rows, half = g.x.shape
    crops = rows // AREA
    mid = g.ws.shape[1]

    def swap():
        return c.partner(g.ws.at[c.half(c.o, half)], g.wsp, g.sem_sw)

    def give(mb):
        return c.partner(g.ss.at[mb], g.sr.at[mb], g.sem_sp.at[mb])

    def act(mb):
        return c.partner(g.ao.at[mb], g.ap.at[mb], g.sem_sa.at[mb])

    def begin():
        g.ao[...] = jnp.zeros(g.ao.shape, BF16)
        c.loaded("ws")
        for mb in range(nb):
            if mb == nb - 1:
                c.ready()
                swap().start()
            c.loaded("x", mb)
            g.sown[mb] = nn(g.x[mb], g.ws[c.half(c.h, half), :])
        swap().wait_recv()
        for mb in range(nb):
            g.ss[mb] = nn(g.x[mb], g.wsp[...]).astype(BF16)
            give(mb).start()

    def pre(mb):
        give(mb).wait_recv()
        g.ef[0] = g.sown[mb] + g.sr[mb].astype(F32)
        local_moments(g.ef, 0, rows, 7 * crops, mid, g.em)
        g.spre[mb] = g.ef[0].astype(BF16)
        g.sm[mb] = g.em[0]
        g.sbuf[mb, c.p] = g.sm[mb]
        c.spread(g.sm.at[mb], g.sbuf.at[mb, c.p], g.sem_ss.at[mb])

    def post(mb):
        c.take(g.sbuf.at[mb, pl.ds(0, c.n - 1)], g.sem_ss.at[mb], 1)
        mean, scale = joint_moments(g.sbuf[mb], float(rows))
        g.sst[mb, 0:1] = mean
        g.sst[mb, 1:2] = scale
        gain = scale * g.stem_gain[...]
        bias = g.stem_bias[...] - mean * gain
        for i in range(SIDE):
            post = g.spre[mb, pl.ds(i * SIDE * crops, SIDE * crops)].astype(F32) * gain + bias
            g.ao[mb, pl.ds((WIDE + 1 + WIDE * i) * crops, SIDE * crops)] = silu(post).astype(BF16)
        act(mb).start()

    def end():
        swap().wait_send()
        for mb in range(nb):
            give(mb).wait_send()
            act(mb).wait_send()
            c.take(g.sbuf.at[mb, pl.ds(0, c.n - 1)], g.sem_ss.at[mb], 0)

    return Phase(pre, post, begin, lambda mb: act(mb).wait_recv(), end)


def conv_rows(crops):
    return SIDE * WIDE * crops


def middle_forward(g, c):
    nb, rows, mid = g.mpre.shape
    crops = rows // AREA
    long = conv_rows(crops)

    def act(mb):
        return c.partner(g.mo.at[mb], g.mp.at[mb], g.sem_ma.at[mb])

    def pre(mb):
        if mb == 0:
            c.loaded("wm")
        total = None
        for tap in range(9):
            at = pl.ds((WIDE * (tap // 3) + tap % 3) * crops, long)
            part = nn(g.ao[mb, at], g.wm[tap, c.half(c.h, mid), :])
            total = part if total is None else total + part
            total = total + nn(g.ap[mb, at], g.wm[tap, c.half(c.o, mid), :])
        for i in range(SIDE):
            g.ef[0, pl.ds(i * SIDE * crops, SIDE * crops)] = total[
                i * WIDE * crops : (i * WIDE + SIDE) * crops
            ]
        local_moments(g.ef, 0, rows, 7 * crops, mid, g.em)
        g.mpre[mb] = g.ef[0].astype(BF16)
        g.mm[mb] = g.em[0]
        g.mbuf[mb, c.p] = g.mm[mb]
        c.spread(g.mm.at[mb], g.mbuf.at[mb, c.p], g.sem_ms.at[mb])

    def post(mb):
        c.take(g.mbuf.at[mb, pl.ds(0, c.n - 1)], g.sem_ms.at[mb], 1)
        mean, scale = joint_moments(g.mbuf[mb], float(rows))
        g.mst[mb, 0:1] = mean
        g.mst[mb, 1:2] = scale
        gain = scale * g.middle_gain[...]
        bias = g.middle_bias[...] - mean * gain
        for i in range(SIDE):
            at = pl.ds(i * SIDE * crops, SIDE * crops)
            g.mo[mb, at] = silu(g.mpre[mb, at].astype(F32) * gain + bias).astype(BF16)
        act(mb).start()

    def end():
        for mb in range(nb):
            act(mb).wait_send()
            c.take(g.mbuf.at[mb, pl.ds(0, c.n - 1)], g.sem_ms.at[mb], 0)

    return Phase(pre, post, c.ready, lambda mb: act(mb).wait_recv(), end)


def expand_forward(g, c):
    nb, rows, half = g.x.shape
    crops = rows // AREA
    lanes = 256

    def swap():
        return c.partner(g.we.at[:, c.half(c.o, half)], g.wep, g.sem_ew)

    def pool(mb):
        return c.partner(g.po.at[mb], g.pp.at[mb], g.sem_ep.at[mb])

    def early():
        c.loaded("we")
        c.ready()
        swap().start()

    def begin():
        early()
        swap().wait_recv()

    def pre(mb):
        for k in range(half // lanes):
            cols = pl.ds(k * lanes, lanes)
            own = g.we[:, pl.ds(pl.multiple_of(c.h * half + k * lanes, lanes), lanes)]
            g.ef[0] = nn(g.mo[mb], own) + nn(g.mp[mb], g.wep[:, cols])
            local_moments(g.ef, 0, rows, 7 * crops, lanes, g.em)
            g.epre[mb, :, cols] = g.ef[0].astype(BF16)
            g.esend[mb, :, cols] = g.em[0]
        g.ebuf[mb, c.p] = g.esend[mb]
        c.spread(g.esend.at[mb], g.ebuf.at[mb, c.p], g.sem_es.at[mb])

    def post(mb):
        c.take(g.ebuf.at[mb, pl.ds(0, c.n - 1)], g.sem_es.at[mb], 1)
        mean, scale = joint_moments(g.ebuf[mb], float(rows))
        g.est[mb, 0:1] = mean
        g.est[mb, 1:2] = scale
        for lo in range(0, half, lanes):
            cols = pl.ds(lo, lanes)
            gain = g.est[mb, 1:2, cols] * g.expand_gain[:, cols]
            bias = g.expand_bias[:, cols] - g.est[mb, 0:1, cols] * gain

            def pixels(i, total):
                for j in range(SIDE):
                    at = rows_at((i * SIDE + j) * crops, crops)
                    summed = g.epre[mb, at, cols].astype(F32) * gain + bias
                    summed = summed + g.x[mb, at, cols].astype(F32)
                    gate = sigmoid(summed)
                    total = total + summed * gate
                    g.slo[mb, at, cols] = (gate * (1.0 + summed * (1.0 - gate))).astype(BF16)
                return total

            total = lax.fori_loop(0, SIDE, pixels, jnp.zeros((crops, lanes), F32))
            g.po[mb, :, cols] = (total * (1.0 / AREA)).astype(BF16)
        pool(mb).start()

    def end():
        swap().wait_send()
        for mb in range(nb):
            pool(mb).wait_send()
            c.take(g.ebuf.at[mb, pl.ds(0, c.n - 1)], g.sem_es.at[mb], 0)

    return Phase(
        pre, post, begin, lambda mb: pool(mb).wait_recv(), end, early=early,
        weights=lambda: swap().wait_recv(),
    )


def hidden_forward(g, c):
    nb, crops, half = g.po.shape
    part = crops // 2

    def trade(mb):
        return c.partner(g.pe.at[mb], g.pr.at[mb], g.sem_he.at[mb])

    def swap(mb):
        where = g.gath.at[mb, :, c.h]
        return c.partner(where, where, g.sem_hx.at[mb])

    def others(mb):
        return g.gath.at[mb, pl.ds(0, c.n - 1), c.h]

    def pre(mb):
        if mb == 0:
            c.loaded("wh")
        value = nn(g.po[mb], g.wh[c.half(c.h, half), :]) + nn(g.pp[mb], g.wh[c.half(c.o, half), :])
        g.hall[c.p % 4, c.p // 4, mb] = value.astype(BF16)
        mean = jnp.mean(value, axis=0, keepdims=True)
        g.hm[mb, 0:1] = mean
        g.hm[mb, 1:2] = jnp.sum((value - mean) * (value - mean), axis=0, keepdims=True)
        g.hbuf[mb, c.p] = g.hm[mb]
        c.spread(g.hm.at[mb], g.hbuf.at[mb, c.p], g.sem_hs.at[mb])

    def post(mb):
        c.take(g.hbuf.at[mb, pl.ds(0, c.n - 1)], g.sem_hs.at[mb], 1)
        mean, scale = joint_moments(g.hbuf[mb], float(crops))
        g.hst[mb, 0:1] = mean
        g.hst[mb, 1:2] = scale
        gain = scale * g.hidden_gain[...]
        bias = g.hidden_bias[...] - mean * gain
        act = silu(g.hall[c.p % 4, c.p // 4, mb].astype(F32) * gain + bias).astype(BF16)
        g.pe[mb] = nn(act, g.w2[...])
        trade(mb).start()

    def embed(mb):
        trade(mb).wait_recv()
        g.em2[mb] = (g.pe[mb] + g.pr[mb]).reshape(2, part, -1)
        g.gath[mb, c.p, c.h] = g.em2[mb, c.h]
        c.spread(g.em2.at[mb, c.h], g.gath.at[mb, c.p, c.h], g.sem_hg.at[mb])

    def mirror(mb):
        c.take(others(mb), g.sem_hg.at[mb], 1)
        swap(mb).start()

    def arrive(mb):
        swap(mb).wait_recv()

    def relay(name, stage):
        ref, sems = (g.hall, g.sem_hh) if name == "h" else (g.pall, g.sem_pa)
        if stage == 0 and name == "p":
            g.pall[c.p % 4, c.p // 4] = g.po[...]
        if stage > 0:
            c.relay_wait(ref, sems, stage - 1, 1)
        if stage < 3:
            for copy in c.relay(ref, sems, stage):
                copy.start()

    def direct(ref, sems):
        own = ref.at[c.p % 4, c.p // 4]
        c.spread(own, own, sems.at[0])
        for which in (1, 0):
            c.take(ref.at[pl.ds(0, 3)], sems.at[0], which)
            c.take(ref.at[0, pl.ds(0, c.n // 4 - 1)], sems.at[0], which)

    def pooled_swap():
        return c.partner(g.pall, g.qall, g.sem_pq)

    def end():
        pooled_swap().wait_send()
        for mb in range(nb):
            trade(mb).wait_send()
            swap(mb).wait_send()
            c.take(g.hbuf.at[mb, pl.ds(0, c.n - 1)], g.sem_hs.at[mb], 0)
            c.take(others(mb), g.sem_hg.at[mb], 0)

    def end_relay():
        for ref, sems in ((g.hall, g.sem_hh), (g.pall, g.sem_pa)):
            for stage in range(3):
                c.relay_wait(ref, sems, stage, 0)

    def all_arrive(mb):
        if mb == 0:
            for step in (embed, mirror, arrive):
                for k in range(nb):
                    step(k)
            g.pall[c.p % 4, c.p // 4] = g.po[...]
            direct(g.hall, g.sem_hh)
            direct(g.pall, g.sem_pa)
            pooled_swap().start()
            pooled_swap().wait_recv()

    return Phase(
        pre, post, c.ready, all_arrive, end, embed=embed, mirror=mirror, landed=arrive,
        relay=relay, pooled_swap=pooled_swap, end_relay=end_relay,
    )


def panel_steps(panel, start, lane, level):
    shape = panel.shape
    scaled = jnp.zeros(shape, F32)

    def wide(part):
        return jnp.broadcast_to(part, shape)

    for i in range(0, 8, 2):
        j = start + i
        one, two = lane == j, lane == j + 1
        c1, c2 = wide(panel[:, :, j : j + 1]), wide(panel[:, :, j + 1 : j + 2])
        r1, r2 = wide(panel[:, i : i + 1, :]), wide(panel[:, i + 1 : i + 2, :])
        a, b, d = wide(c1[:, i : i + 1]), wide(c1[:, i + 1 : i + 2]), wide(c2[:, i + 1 : i + 2])
        first = 1.0 / a
        second = a / (a * d - b * b)
        ratio = b * first
        r2 = r2 - ratio * r1
        m1 = jnp.where(one, 1.0, jnp.where(two, 0.0, r1))
        m2 = jnp.where(one, -ratio, jnp.where(two, 1.0, r2))
        l1 = c1 * first
        l2 = (c2 - l1 * b) * second
        cleared = jnp.where(jnp.logical_or(one, two), 0.0, panel)
        new = jnp.where(one, -ratio, r2)
        scaled = jnp.where(level == i, panel * first, jnp.where(level == i + 1, new * second, scaled))
        below = cleared - l1 * m1 - l2 * m2
        panel = jnp.where(level > i + 1, below, jnp.where(level == i + 1, new, panel))
    return panel, scaled


def eliminate(cov, between):
    total, width = cov.shape[0], cov.shape[1]
    pack = 8 * total
    side = -(-pack // width) * width
    lane = lax.broadcasted_iota(jnp.int32, (1, 1, width), 2)
    level = lax.broadcasted_iota(jnp.int32, (1, 8, width), 1)
    which = lax.broadcasted_iota(jnp.int32, (1, side), 1) // 8

    def product(left, right):
        return jnp.dot(left, right, precision=HIGH, preferred_element_type=F32)

    panel = cov[:, 0:8, :]
    for start in range(0, width, 8):
        between(start)
        panel, scaled = panel_steps(panel, start, lane, level)
        cov[:, start : start + 8, :] = panel
        after = start + 8
        if after == width:
            break
        inside = lane - start
        unit = jnp.where(inside == level, 1.0, 0.0)
        rows = jnp.where(jnp.logical_and(inside >= level, inside < 8), unit, panel)
        rows = rows.reshape(pack, width)
        scaled = scaled.reshape(pack, width)
        if side > pack:
            blank = jnp.zeros((side - pack, width), F32)
            rows = jnp.concatenate([rows, blank], axis=0)
            scaled = jnp.concatenate([scaled, blank], axis=0)
        flipped = scaled.T
        kept = jnp.logical_or(lane[0] < start, lane[0] >= after)
        near = flipped[after : after + 8]
        near = jnp.concatenate([jnp.where(which == k, near, 0.0) for k in range(total)], axis=0)
        change = product(near, rows).reshape(total, 8, width)
        panel = jnp.where(kept[None], cov[:, after : after + 8, :], 0.0) - change
        if after + 8 == width:
            continue
        far = flipped[after + 8 :]
        for k in range(total):
            change = product(jnp.where(which == k, far, 0.0), rows)
            cov[k, after + 8 :, :] = jnp.where(kept, cov[k, after + 8 :, :], 0.0) - change


def split(values):
    high = values.astype(BF16)
    return high, (values - high.astype(F32)).astype(BF16)


def fine(product, left, right):
    (a, b), (p, q) = split(left), split(right)
    return product(a, p) + (product(a, q) + product(b, p))


def whiten(g, c):
    nb, count = g.order.shape
    subs = g.sizes.shape[1]
    width = g.gath.shape[-1]
    pairs = g.pairs.shape[2]
    shape = (width, width)
    eye = lax.broadcasted_iota(jnp.int32, shape, 0) == lax.broadcasted_iota(jnp.int32, shape, 1)
    eye = eye.astype(F32)
    lower = lax.broadcasted_iota(jnp.int32, shape, 0) >= lax.broadcasted_iota(jnp.int32, shape, 1)
    lower = lower.astype(F32)
    strict = lower - eye
    crop_id = lax.broadcasted_iota(jnp.int32, (count, 1), 0)
    place = lax.broadcasted_iota(jnp.int32, (1, count), 1)

    def masks(mb):
        member = g.member[mb]
        return [(member == float(k)).astype(F32) for k in range(subs)]

    def apart(values, inside):
        return jnp.concatenate([values * mask for mask in inside], axis=1)

    def prepare(mb):
        end = jnp.int32(0)
        segment = jnp.zeros((1, count), F32)
        for k in range(subs - 1):
            end = end + g.sizes[mb, k]
            segment = segment + (place >= end).astype(F32)
        order = g.order[mb : mb + 1, :]
        member = jnp.sum(jnp.where(order == crop_id, segment, 0.0), axis=1, keepdims=True)
        g.member[mb] = jnp.broadcast_to(member, (count, width))
        embed = g.gath[mb].reshape(count, width)
        centred = jnp.zeros((count, width), F32)
        inside = masks(mb)
        for k in range(subs):
            centre = jnp.sum(embed * inside[k], axis=0, keepdims=True) / g.sizes[mb, k].astype(F32)
            centred = centred + (embed - centre) * inside[k]
        both = fine(tn, apart(centred, inside), centred)
        for k in range(subs):
            part = both[k * width : (k + 1) * width] / g.sizes[mb, k].astype(F32)
            g.cov[mb * subs + k] = part + RIDGE * eye
        g.cent[mb] = centred

    def factor_all(between):
        eliminate(g.cov, between)
        for k in range(nb * subs):
            inverse = g.cov[k]
            power = jnp.sum(inverse * eye, axis=1, keepdims=True)
            g.cov[k] = lax.rsqrt(power) * (inverse * strict + eye)
        g.loss[...] = jnp.zeros(g.loss.shape, F32)

    def rest(mb):
        inside = masks(mb)
        inverses = [g.cov[mb * subs + k] for k in range(subs)]
        white = fine(nt, apart(g.cent[mb], inside), jnp.concatenate(inverses, axis=1))
        power = jnp.sum(white * white, axis=1, keepdims=True)
        factor = lax.rsqrt(power + EPS_NORM)
        normed = white * factor
        first, second = g.pairs[mb, 0:1] == crop_id, g.pairs[mb, 1:2] == crop_id
        choose = (first.astype(F32) - second.astype(F32)).astype(BF16)
        high, rest_of = split(normed)
        differ = tn(choose, high) + tn(choose, rest_of)
        g.loss[...] = g.loss[...] + jnp.sum(differ * differ) * (1.0 / (pairs * nb))
        high, rest_of = split(differ)
        grad = (nn(choose, high) + nn(choose, rest_of)) * (2.0 * LOSS_SCALE / (nb * pairs))
        inner = jnp.sum(grad * white, axis=1, keepdims=True)
        grad = grad * factor - white * (factor * factor * factor * inner)
        low = tn(apart(grad, inside).astype(BF16), white.astype(BF16))
        sides, shift, shares = [], jnp.zeros((count, width), F32), []
        for k in range(subs):
            size = g.sizes[mb, k].astype(F32)
            part = low[k * width : (k + 1) * width]
            sides.append((part * lower + (part * strict).T).astype(BF16))
            shares.append(inside[k] / size)
            shift = shift + shares[k] * jnp.sum(grad * inside[k], axis=0, keepdims=True)
        shift = shift + nn(apart(white, shares).astype(BF16), jnp.concatenate(sides, axis=0))
        inverses = jnp.concatenate(inverses, axis=0).astype(BF16)
        delta = nn(apart(grad - shift, inside).astype(BF16), inverses)
        g.ed[mb] = delta.astype(BF16)

    def post(mb):
        if mb == 0:
            factor_all(lambda start: None)
        rest(mb)

    return Phase(prepare, post, factor_all=factor_all, rest=rest)


def hidden_backward(g, c):
    nb, crops, half = g.pg.shape
    count, hid = c.n * crops, g.hall.shape[4]
    chunk = 256

    def give():
        return c.partner(g.pgs, g.pgr, g.sem_hp)

    def rows_of(ref, mb, lo, size, cols):
        parts = []
        for z in range(lo // (4 * crops), (lo + size) // (4 * crops)):
            parts.append(ref[:, z, mb, :, cols].reshape(4 * crops, -1))
        return jnp.concatenate(parts, axis=0)

    def run():
        totals = jnp.zeros((2, hid), F32)
        emb = jnp.zeros(g.gemb.shape, F32)
        for mb in range(nb):
            mean, scale = g.hst[mb, 0:1], g.hst[mb, 1:2]
            shift = -mean * scale
            one = two = jnp.zeros((1, hid), F32)
            for lo in range(0, count, chunk):
                at = pl.ds(lo, chunk)
                part = rows_of(g.hall, mb, lo, chunk, slice(None))
                normal = part.astype(F32) * scale + shift
                value = normal * g.hidden_gain[...] + g.hidden_bias[...]
                gate = sigmoid(value)
                delta = g.ed[mb, at]
                emb = emb + tn((value * gate).astype(BF16), delta)
                grad = nt(delta, g.w2[...]) * (gate * (1.0 + value * (1.0 - gate)))
                one = one + jnp.sum(grad, axis=0, keepdims=True)
                two = two + jnp.sum(grad * normal, axis=0, keepdims=True)
                g.hgf[at] = grad
            sums = jnp.concatenate([one, two], axis=0)
            totals = totals + sums
            a, b, k = norm_terms(g.hst, mb, g.hidden_gain[...], sums, float(count))
            for lo in range(0, count, chunk):
                at = pl.ds(lo, chunk)
                part = rows_of(g.hall, mb, lo, chunk, slice(None))
                g.hd[mb, at] = (g.hgf[at] * a + part.astype(F32) * b + k).astype(BF16)
        g.hbias[...] = totals[0:1]
        g.hgain[...] = totals[1:2]
        g.gemb[...] = emb
        c.ready()
        for mb in range(nb):
            own = g.hd[mb, rows_at(c.p * crops, crops)]
            g.pgs[mb] = nt(own, g.wh[c.half(c.o, half), :]).astype(BF16)
        give().start()

    def finish():
        for mb in range(nb):
            own = g.hd[mb, rows_at(c.p * crops, crops)]
            g.pg[mb] = nt(own, g.wh[c.half(c.h, half), :])
        give().wait_recv()
        g.pg[...] = (g.pg[...] + g.pgr[...].astype(F32)) * (1.0 / AREA)

    def weights():
        hd = g.hd[...].reshape(nb * count, hid)
        lanes = 256
        for which, rows in ((c.h, g.pall), (c.o, g.qall)):
            for lo in range(0, half, lanes):
                part = [rows_of(rows, mb, 0, count, slice(lo, lo + lanes)) for mb in range(nb)]
                part = jnp.concatenate(part, axis=0)
                g.ghid[rows_at(which * half + lo, lanes), :] = tn(part, hd).astype(BF16)

    def end():
        give().wait_send()

    def pre(mb):
        if mb == 0:
            for step in (run, finish, weights):
                step()

    return Phase(pre, lambda mb: None, None, None, end, run=run, weights=weights, finish=finish)


def expand_backward(g, c):
    nb, rows, half = g.epre.shape
    crops = rows // AREA
    mid = g.we.shape[0]
    lanes = 256
    total_rows = float(rows) * c.n

    def pre(mb):
        if mb == 0:
            g.egain[...] = jnp.zeros(g.egain.shape, F32)
            g.ebias[...] = jnp.zeros(g.ebias.shape, F32)
        for lo in range(0, half, lanes):
            cols = pl.ds(lo, lanes)
            scale = g.est[mb, 1:2, cols]
            shift = -g.est[mb, 0:1, cols] * scale
            grad = g.pg[mb, :, cols]

            def pixels(i, carry):
                one, two = carry
                for j in range(SIDE):
                    at = rows_at((i * SIDE + j) * crops, crops)
                    normal = g.epre[mb, at, cols].astype(F32) * scale + shift
                    part = grad * g.slo[mb, at, cols].astype(F32)
                    g.sg[mb, at, cols] = part.astype(BF16)
                    one = one + part
                    two = two + part * normal
                return one, two

            zero = jnp.zeros((crops, lanes), F32)
            one, two = lax.fori_loop(0, SIDE, pixels, (zero, zero))
            g.ebm[mb, 0:1, cols] = jnp.sum(one, axis=0, keepdims=True)
            g.ebm[mb, 1:2, cols] = jnp.sum(two, axis=0, keepdims=True)
        g.ebb[mb, c.p] = g.ebm[mb]
        c.spread(g.ebm.at[mb], g.ebb.at[mb, c.p], g.sem_eb.at[mb])

    def give(mb):
        return c.partner(g.mgs.at[mb], g.mgr.at[mb], g.sem_mg.at[mb])

    def swap():
        return c.partner(g.gxs, g.gexp.at[c.half(c.h, mid)], g.sem_gx)

    def delta(mb):
        c.take(g.ebb.at[mb, pl.ds(0, c.n - 1)], g.sem_eb.at[mb], 1)
        g.ebt[...] = jnp.sum(g.ebb[mb], axis=0)
        g.ebias[...] = g.ebias[...] + g.ebt[0:1]
        g.egain[...] = g.egain[...] + g.ebt[1:2]
        for lo in range(0, half, lanes):
            cols = pl.ds(lo, lanes)
            scale = g.est[mb, 1:2, cols]
            gain = g.expand_gain[:, cols] * scale
            slant = gain * g.ebt[1:2, cols] * (-1.0 / total_rows)
            base = gain * g.ebt[0:1, cols] * (-1.0 / total_rows)
            base = base - slant * scale * g.est[mb, 0:1, cols]
            slant = slant * scale

            def pixels(i, carry):
                for j in range(SIDE):
                    at = rows_at((i * SIDE + j) * crops, crops)
                    part = g.sg[mb, at, cols].astype(F32) * gain + base
                    part = part + g.epre[mb, at, cols].astype(F32) * slant
                    g.xd[mb, at, cols] = part.astype(BF16)
                return carry

            lax.fori_loop(0, SIDE, pixels, 0)

    def middle(mb):
        g.mgs[mb] = nt(g.xd[mb], g.wep[...]).astype(BF16)
        give(mb).start()
        g.mg[mb] = nt(g.xd[mb], g.we[:, c.half(c.h, half)])

    def post(mb):
        delta(mb)
        middle(mb)

    def weights():
        xd = g.xd[...].reshape(nb * rows, half)
        g.gxs[...] = tn(g.mp[...].reshape(nb * rows, mid), xd).astype(BF16)
        swap().start()
        g.gexp[c.half(c.h, mid), :] = tn(g.mo[...].reshape(nb * rows, mid), xd).astype(BF16)

    def arrive(mb):
        give(mb).wait()
        g.mg[mb] = g.mg[mb] + g.mgr[mb].astype(F32)

    def weights_in():
        swap().wait_recv()

    def end():
        swap().wait_send()
        for mb in range(nb):
            c.take(g.ebb.at[mb, pl.ds(0, c.n - 1)], g.sem_eb.at[mb], 0)

    def end_alone():
        weights()
        weights_in()
        end()

    return Phase(
        pre, post, c.ready, arrive, end_alone, weights=weights, weights_in=weights_in, close=end,
        delta=delta, middle=middle,
    )


def norm_slopes(c, mb, grad, pre, stats, gain, bias, sums, buf, sem, out):
    rows, mid = pre.shape[1:]
    scale = stats[mb, 1:2]
    shift = -stats[mb, 0:1] * scale
    chunk = rows // SIDE

    def image_row(i, carry):
        one, two = carry
        at = rows_at(i * chunk, chunk)
        normal = pre[mb, at].astype(F32) * scale + shift
        part = grad[mb, at] * slope(normal * gain[...] + bias[...])
        out[mb, at] = part
        one = one + jnp.sum(part.reshape(-1, 8, mid), axis=0)
        two = two + jnp.sum((part * normal).reshape(-1, 8, mid), axis=0)
        return one, two

    zero = jnp.zeros((8, mid), F32)
    one, two = lax.fori_loop(0, SIDE, image_row, (zero, zero))
    sums[mb, 0:1] = jnp.sum(one, axis=0, keepdims=True)
    sums[mb, 1:2] = jnp.sum(two, axis=0, keepdims=True)
    buf[mb, c.p] = sums[mb]
    c.spread(sums.at[mb], buf.at[mb, c.p], sem.at[mb])


def norm_terms(stats, mb, gain, sums, count):
    scale = stats[mb, 1:2]
    a = gain * scale
    slant = a * sums[1:2] * (-1.0 / count)
    k = a * sums[0:1] * (-1.0 / count) - slant * scale * stats[mb, 0:1]
    return a, slant * scale, k


def middle_backward(g, c):
    nb, rows, mid = g.mpre.shape
    crops = rows // AREA
    long = conv_rows(crops)
    count = float(rows) * c.n

    def begin():
        c.ready()
        g.mdg[...] = jnp.zeros(g.mdg.shape, BF16)
        g.mgain[...] = jnp.zeros(g.mgain.shape, F32)
        g.mbias[...] = jnp.zeros(g.mbias.shape, F32)

    def pre(mb):
        norm_slopes(
            c, mb, g.mg, g.mpre, g.mst, g.middle_gain, g.middle_bias, g.mbm, g.mbb,
            g.sem_mb, g.mgf,
        )

    def give(mb):
        return c.partner(g.ags.at[mb], g.agr.at[mb], g.sem_ag.at[mb])

    def delta(mb):
        c.take(g.mbb.at[mb, pl.ds(0, c.n - 1)], g.sem_mb.at[mb], 1)
        sums = jnp.sum(g.mbb[mb], axis=0)
        g.mbias[...] = g.mbias[...] + sums[0:1]
        g.mgain[...] = g.mgain[...] + sums[1:2]
        a, b, k = norm_terms(g.mst, mb, g.middle_gain[...], sums, count)
        for i in range(SIDE):
            at = pl.ds(i * SIDE * crops, SIDE * crops)
            part = g.mgf[mb, at] * a + g.mpre[mb, at].astype(F32) * b + k
            g.mdg[mb, pl.ds((WIDE + 1 + WIDE * i) * crops, SIDE * crops)] = part.astype(BF16)
        g.mdt[:, mb * long : (mb + 1) * long] = g.mdg[mb, pl.ds((WIDE + 1) * crops, long)].T

    def spread(mb):
        for which, place in ((c.o, 0), (c.h, 1)):
            total = None
            for tap in range(9):
                at = pl.ds((WIDE * (2 - tap // 3) + 2 - tap % 3) * crops, long)
                part = nt(g.mdg[mb, at], g.wm[tap, c.half(which, mid), :])
                total = part if total is None else total + part
            for i in range(SIDE):
                at = pl.ds(i * SIDE * crops, SIDE * crops)
                part = total[i * WIDE * crops : (i * WIDE + SIDE) * crops]
                if place == 0:
                    g.ags[mb, at] = part.astype(BF16)
                else:
                    g.ag[mb, at] = part
            if place == 0:
                give(mb).start()

    def weights(out, first, taps):
        def one(i):
            tap = first + i
            at = pl.ds(pl.multiple_of((WIDE * (tap // 3) + tap % 3) * crops, crops), long)
            for act, which in ((g.ao, c.h), (g.ap, c.o)):
                field = jnp.concatenate([act[mb, at] for mb in range(nb)], axis=0)
                part = nn(g.mdt[...], field)
                out[c.half(2 * i + which, mid), :] = part.T.astype(BF16)

        each(taps, one)

    def arrive(mb):
        give(mb).wait()
        g.ag[mb] = g.ag[mb] + g.agr[mb].astype(F32)

    def end():
        for mb in range(nb):
            c.take(g.mbb.at[mb, pl.ds(0, c.n - 1)], g.sem_mb.at[mb], 0)

    def post(mb):
        delta(mb)
        spread(mb)

    def all_weights():
        weights(g.gmida, 0, 3)
        weights(g.gmidb, 3, 3)
        weights(g.gmidc, 6, 3)

    def end_alone():
        all_weights()
        end()

    return Phase(
        pre, post, begin, arrive, end_alone, delta=delta, spread=spread, weights=weights, close=end
    )


def stem_backward(g, c):
    nb, rows, mid = g.spre.shape
    half = g.x.shape[2]
    crops = rows // AREA
    count = float(rows) * c.n

    def begin():
        c.ready()
        g.sgain[...] = jnp.zeros(g.sgain.shape, F32)
        g.sbias[...] = jnp.zeros(g.sbias.shape, F32)

    def pre(mb):
        norm_slopes(
            c, mb, g.ag, g.spre, g.sst, g.stem_gain, g.stem_bias, g.sbm, g.sbb,
            g.sem_sb, g.sgf,
        )

    def give(mb):
        return c.partner(g.sd.at[mb], g.sdp.at[mb], g.sem_sd.at[mb])

    def swap():
        return c.partner(g.gss, g.gstem.at[c.half(c.h, half)], g.sem_gs)

    def post(mb):
        c.take(g.sbb.at[mb, pl.ds(0, c.n - 1)], g.sem_sb.at[mb], 1)
        sums = jnp.sum(g.sbb[mb], axis=0)
        g.sbias[...] = g.sbias[...] + sums[0:1]
        g.sgain[...] = g.sgain[...] + sums[1:2]
        a, b, k = norm_terms(g.sst, mb, g.stem_gain[...], sums, count)
        for i in range(SIDE):
            at = pl.ds(i * SIDE * crops, SIDE * crops)
            g.sd[mb, at] = (g.sgf[mb, at] * a + g.spre[mb, at].astype(F32) * b + k).astype(BF16)
        give(mb).start()

    def weights():
        lanes = 256
        sd = g.sd[...].reshape(nb * rows, mid)
        sdp = g.sdp[...].reshape(nb * rows, mid)
        for lo in range(0, half, lanes):
            field = g.x[:, :, lo : lo + lanes].reshape(nb * rows, lanes)
            g.gss[lo : lo + lanes] = tn(field, sdp).astype(BF16)
            own = rows_at(c.h * half + lo, lanes)
            g.gstem[own, :] = tn(field, sd).astype(BF16)
        swap().start()

    def weights_in():
        swap().wait_recv()

    def end():
        swap().wait_send()
        for mb in range(nb):
            give(mb).wait_send()
            c.take(g.sbb.at[mb, pl.ds(0, c.n - 1)], g.sem_sb.at[mb], 0)

    def end_alone():
        weights()
        weights_in()
        end()

    return Phase(
        pre, post, begin, lambda mb: give(mb).wait_recv(), end_alone, weights=weights,
        weights_in=weights_in, close=end,
    )


def crops_backward(g, c):
    half = g.wsp.shape[0]

    def pre(mb):
        part = nt(g.sd[mb], g.ws[c.half(c.h, half), :]) + nt(g.sdp[mb], g.wsp[...])
        g.gcrops[mb] = (part + g.sg[mb].astype(F32)).astype(BF16)

    return Phase(pre, lambda mb: None)


class Total:
    def __init__(self, c, local, place, one, two, three, sems):
        self.done = 0
        self.c, self.local, self.place, self.sems = c, local, place, sems
        self.one, self.two, self.three = one, two, three
        self.long = local.shape[0] // 2
        x, y, self.z = c.p % 2, (c.p // 2) % 2, c.p // 4
        step_x, step_y = c.p + 1 - 2 * x, c.p + 2 - 4 * y
        self.ways = ((x, step_x, y, step_y), (y, step_y, x, step_x))
        self.half, self.quarter, self.piece = self.long // 2, self.long // 4, self.long // 16

    def copy(self, stream, step, src, dst, device):
        return pltpu.make_async_remote_copy(
            src_ref=src,
            dst_ref=dst,
            send_sem=self.sems.at[stream, step, 0],
            recv_sem=self.sems.at[stream, step, 1],
            device_id=(device, self.c.h),
            device_id_type=MESH,
        )

    def at(self, start, size):
        return pl.ds(pl.multiple_of(start, 16), size)

    def start(self, step):
        for stream in range(2):
            b1, d1, b2, d2 = self.ways[stream]
            base = stream * self.long
            kept = base + b1 * self.half
            core = kept + b2 * self.quarter
            if step == 0:
                src = self.local.at[self.at(base + (1 - b1) * self.half, self.half)]
                self.copy(stream, step, src, self.one.at[stream], d1).start()
            elif step == 1:
                src = self.one.at[stream, self.at((1 - b2) * self.quarter, self.quarter)]
                self.copy(stream, step, src, self.two.at[stream], d2).start()
            elif step == 4:
                self.keep(stream, core).wait()
                src = self.place(stream, core, self.quarter)
                self.copy(stream, step, src, src, d2).start()
            elif step == 5:
                src = self.place(stream, kept, self.half)
                self.copy(stream, step, src, src, d1).start()
            else:
                if step == 3:
                    self.keep(stream, core).start()
                for d in range(1, 4):
                    other = (self.z + d) % 4
                    device = self.c.p + 4 * (other - self.z)
                    if step == 2:
                        src = self.two.at[stream, self.at(other * self.piece, self.piece)]
                        dst = self.three.at[stream, 3 - d]
                    else:
                        src = self.two.at[stream, self.at(self.z * self.piece, self.piece)]
                        dst = self.place(stream, core + self.z * self.piece, self.piece)
                    self.copy(stream, step, src, dst, device).start()

    def keep(self, stream, core):
        piece = self.at(self.z * self.piece, self.piece)
        place = self.place(stream, core + self.z * self.piece, self.piece)
        return pltpu.make_async_copy(self.two.at[stream, piece], place, self.sems.at[stream, 6, 0])

    def wait(self, stream, step, which):
        blocks = {0: self.one, 1: self.two, 2: self.three, 3: self.three, 4: self.two, 5: self.one}
        self.c.take(blocks[step].at[stream], self.sems.at[stream, step], which)

    def take(self, step):
        for stream in range(2):
            self.wait(stream, step, 1)
            b1, d1, b2, d2 = self.ways[stream]
            kept = stream * self.long + b1 * self.half
            core = kept + b2 * self.quarter
            one, two, three = self.one.at[stream], self.two.at[stream], self.three.at[stream]
            if step == 0:
                self.add(one, 0, [(one, 0), (self.local, kept)], self.half)
            elif step == 1:
                self.add(two, 0, [(two, 0), (one, b2 * self.quarter)], self.quarter)
            elif step == 2:
                terms = [(two, self.z * self.piece)] + [(three.at[d], 0) for d in range(3)]
                self.add(two, self.z * self.piece, terms, self.piece)

    def add(self, out, start, terms, size):
        fits = 2**14 // self.local.shape[1]
        chunk = max(k for k in range(16, fits + 1, 16) if size % k == 0)

        def one(i):
            total = None
            for ref, begin in terms:
                value = ref[pl.ds(pl.multiple_of(begin + i * chunk, 16), chunk), :].astype(F32)
                total = value if total is None else total + value
            out[pl.ds(pl.multiple_of(start + i * chunk, 16), chunk), :] = total.astype(BF16)

        each(size // chunk, one)

    def step(self):
        self.take(self.done)
        self.done += 1
        if self.done < 6:
            self.start(self.done)

    def close(self):
        for stream in range(2):
            for step in range(6):
                self.wait(stream, step, 0)


def whole_step(g, c):
    nb, half = g.x.shape[0], g.x.shape[2]
    mid = g.ws.shape[1]
    c.load("ws", 0, g.ws_in, g.ws, g.sem_in.at[0])
    for mb in range(nb):
        c.load("x", mb, g.x_in.at[mb], g.x.at[mb], g.sem_in.at[4 + mb])
    c.load("we", 0, g.we_in, g.we, g.sem_in.at[1])
    c.load("wm", 0, g.wm_in, g.wm, g.sem_in.at[2])
    c.load("wh", 0, g.wh_in, g.wh, g.sem_in.at[3])
    stem, middle, expand = stem_forward(g, c), middle_forward(g, c), expand_forward(g, c)
    hidden, white, hback = hidden_forward(g, c), whiten(g, c), hidden_backward(g, c)
    eback, mback, sback = expand_backward(g, c), middle_backward(g, c), stem_backward(g, c)
    field = crops_backward(g, c)

    def chain(first, second):
        first.post(0)
        for mb in range(1, nb):
            first.post(mb)
            first.arrive(mb - 1)
            second.pre(mb - 1)
        first.arrive(nb - 1)
        second.pre(nb - 1)

    stem.begin()
    expand.early()
    for mb in range(nb):
        stem.pre(mb)
    chain(stem, middle)
    expand.weights()
    chain(middle, expand)
    chain(expand, hidden)
    final = nb - 1
    for step in (hidden.post, hidden.embed):
        for mb in range(final):
            step(mb)
    hidden.post(final)
    hidden.embed(final)
    for mb in range(final):
        hidden.mirror(mb)
    for mb in range(final):
        hidden.landed(mb)
        white.pre(mb)
    hidden.mirror(final)
    hidden.relay("h", 0)
    hidden.relay("p", 0)
    hidden.landed(final)
    white.pre(final)

    def between(start):
        if start == 40:
            hidden.relay("h", 1)
        if start == 72:
            hidden.relay("h", 2)
        if start == 104:
            hidden.relay("p", 1)

    white.factor_all(between)
    for mb in range(nb):
        white.rest(mb)
    hidden.relay("p", 2)
    for phase in (stem, middle, expand):
        phase.end()

    def rows_of(out, first):
        return lambda stream, start, size: out.at[pl.ds(pl.multiple_of(first + start, 16), size)]

    def halves_of(out):
        def place(stream, start, size):
            at = pl.ds(pl.multiple_of(start - stream * mid, 16), size)
            return out.at[at, pl.ds(stream * half, half)]

        return place

    third = g.gmida.shape[0]
    exp = Total(c, g.gexp, halves_of(g.gexp_t), g.gexp_1, g.gexp_2, g.gexp_3, g.sem_gexp)
    place = [rows_of(g.gmid_t, i * third) for i in range(3)]
    one = Total(c, g.gmida, place[0], g.gmida_1, g.gmida_2, g.gmida_3, g.sem_gmida)
    two = Total(c, g.gmidb, place[1], g.gmidb_1, g.gmidb_2, g.gmidb_3, g.sem_gmidb)
    three = Total(c, g.gmidc, place[2], g.gmidc_1, g.gmidc_2, g.gmidc_3, g.sem_gmidc)
    last, rest = (
        Total(
            c, g.gstem.at[pl.ds(i * half, half)], rows_of(g.gstem_t, i * half), g.gstem_1.at[i],
            g.gstem_2.at[i], g.gstem_3.at[i], g.sem_gstem.at[i],
        )
        for i in range(2)
    )
    keep = pltpu.make_async_copy(g.ghid, g.ghid_t, g.sem_in.at[0])

    hidden.relay("h", 3)
    hback.run()
    hback.finish()
    for mb in range(nb):
        eback.pre(mb)
    mback.begin()
    sback.begin()
    eback.delta(0)
    eback.delta(1)
    eback.delta(2)
    eback.weights()
    eback.middle(0)
    eback.weights_in()
    exp.start(0)
    eback.middle(1)
    eback.arrive(0)
    mback.pre(0)
    eback.middle(2)
    eback.arrive(1)
    mback.pre(1)
    eback.arrive(2)
    mback.pre(2)
    hidden.relay("p", 3)
    hidden.pooled_swap().start()
    mback.delta(0)
    exp.step()
    mback.delta(1)
    mback.delta(2)
    mback.weights(g.gmida, 0, 3)
    exp.step()
    one.start(0)
    mback.weights(g.gmidb, 3, 3)
    two.start(0)
    mback.weights(g.gmidc, 6, 3)
    three.start(0)
    mback.spread(0)
    exp.step()
    one.step()
    mback.spread(1)
    two.step()
    mback.arrive(0)
    sback.pre(0)
    mback.spread(2)
    exp.step()
    one.step()
    three.step()
    mback.arrive(1)
    sback.pre(1)
    mback.arrive(2)
    sback.pre(2)
    two.step()
    sback.post(0)
    sback.post(1)
    exp.step()
    one.step()
    three.step()
    sback.post(2)
    for mb in range(nb):
        sback.arrive(mb)
    sback.weights()
    two.step()
    sback.weights_in()
    exp.step()
    one.step()
    last.start(0)
    rest.start(0)
    field.pre(0)
    field.pre(1)
    field.pre(2)
    one.step()
    three.step()
    hidden.pooled_swap().wait_recv()
    hback.weights()
    keep.start()
    last.step()
    two.step()
    rest.step()
    three.step()
    one.step()
    last.step()
    two.step()
    rest.step()
    last.step()
    three.step()
    rest.step()
    two.step()
    last.step()
    rest.step()
    three.step()
    last.step()
    rest.step()
    last.step()
    rest.step()
    gains = (g.sgain, g.sbias, g.mgain, g.mbias, g.egain, g.ebias, g.hgain, g.hbias)
    for row, value in enumerate(gains):
        g.norms[row : row + 1, : value.shape[1]] = value[...]
    hidden.end()
    hidden.end_relay()
    hback.end()
    for phase in (eback, mback, sback):
        phase.close()
    for total in (exp, one, two, three, last, rest):
        total.close()
    keep.wait()


def widen(arrays, norms, widths):
    whole = [(array.shape, 2 if array.size > 2**20 else 1) for array in arrays]
    parts = []
    for number, (shape, cuts) in enumerate(whole):
        if len(shape) == 3:
            cut = -(-shape[1] // 32) * 16
            parts += [
                (number, (i, pl.ds(start, size)), (size, shape[2]))
                for i in range(shape[0])
                for start, size in ((0, cut), (cut, shape[1] - cut))
            ]
        else:
            size = shape[0] // cuts
            parts += [(number, (pl.ds(i * size, size),), (size, shape[1])) for i in range(cuts)]
    count, many = len(arrays), len(parts)

    def kernel(*refs):
        sources, lines = refs[:count], refs[count]
        results = refs[count + 1 : 2 * count + 1]
        rows = refs[2 * count + 1 : 2 * count + 1 + len(widths)]
        narrow = refs[2 * count + 1 + len(widths) : 2 * count + 1 + len(widths) + many]
        wide = refs[2 * count + 1 + len(widths) + many : -2]
        sem_a, sem_b = refs[-2:]
        ins, outs = [], []
        for i, (number, where, _) in enumerate(parts):
            ins.append(pltpu.make_async_copy(sources[number].at[where], narrow[i], sem_a.at[i]))
            outs.append(pltpu.make_async_copy(wide[i], results[number].at[where], sem_b.at[i]))
            ins[i].start()
        for row, width in enumerate(widths):
            rows[row][...] = lines[row : row + 1, :width]
        for i, (_, _, (tall, _)) in enumerate(parts):
            ins[i].wait()

            def cast(j, i=i):
                at = rows_at(j * 16, 16)
                wide[i][at, :] = narrow[i][at, :].astype(F32)

            each(tall // 16, cast)
            outs[i].start()
        for copy in outs:
            copy.wait()

    hbm, vmem = pl.BlockSpec(memory_space=pl.ANY), pl.BlockSpec(memory_space=pltpu.VMEM)
    results = pl.pallas_call(
        kernel,
        out_shape=[jax.ShapeDtypeStruct(array.shape, F32) for array in arrays]
        + [jax.ShapeDtypeStruct((1, width), F32) for width in widths],
        in_specs=[hbm] * count + [vmem],
        out_specs=[hbm] * count + [vmem] * len(widths),
        scratch_shapes=[pltpu.VMEM(size, BF16) for _, _, size in parts]
        + [pltpu.VMEM(size, F32) for _, _, size in parts]
        + [DMA((many,)), DMA((many,))],
        compiler_params=pltpu.CompilerParams(vmem_limit_bytes=60 * 2**20),
        name="widen",
    )(*arrays, norms)
    return results[:count], results[count:]


NORMS = ("sgain", "sbias", "mgain", "mbias", "egain", "ebias", "hgain", "hbias")
GRADS = ("gexp", "gmida", "gmidb", "gmidc", "gstem")


def names_of(functions):
    found, codes = set(), [function.__code__ for function in functions]
    while codes:
        code = codes.pop()
        found |= set(code.co_names)
        codes += [value for value in code.co_consts if isinstance(value, types.CodeType)]
    return found


def body(
    crops_in, stem_weight, middle_weight, expand_weight, stem_gain, stem_bias, middle_gain,
    middle_bias, expand_gain, expand_bias, hidden_weight, hidden_gain, hidden_bias, embed_weight,
    sub_sizes, crop_order, pair_index,
):
    nb, crops, area, half = crops_in.shape
    n = lax.axis_size("dp")
    rows = crops * area
    mid = stem_weight.shape[1]
    hid = hidden_weight.shape[1]
    width = embed_weight.shape[1]
    count = crop_order.shape[1]
    subs = sub_sizes.shape[1]
    long = conv_rows(crops)
    tall = long + 2 * (WIDE + 1) * crops

    def line(v):
        return v.reshape(1, -1)

    env = dict(
        x=crops_in.transpose(0, 2, 1, 3).reshape(nb, rows, half),
        ws=stem_weight,
        wm=middle_weight,
        we=expand_weight,
        wh=hidden_weight,
        w2=embed_weight,
        stem_gain=line(stem_gain),
        stem_bias=line(stem_bias),
        middle_gain=line(middle_gain),
        middle_bias=line(middle_bias),
        expand_gain=line(expand_gain),
        expand_bias=line(expand_bias),
        hidden_gain=line(hidden_gain),
        hidden_bias=line(hidden_bias),
        sizes=sub_sizes,
        order=crop_order,
        pairs=pair_index.transpose(0, 2, 1),
    )
    table = dict(
        wsp=((half, mid), BF16),
        spre=((nb, rows, mid), BF16),
        sst=((nb, 2, mid), F32),
        ao=((nb, tall, mid), BF16),
        ap=((nb, tall, mid), BF16),
        ss=((nb, rows, mid), BF16),
        sr=((nb, rows, mid), BF16),
        sm=((nb, 2, mid), F32),
        sbuf=((nb, n, 2, mid), F32),
        mpre=((nb, rows, mid), BF16),
        mst=((nb, 2, mid), F32),
        mo=((nb, rows, mid), BF16),
        mp=((nb, rows, mid), BF16),
        mm=((nb, 2, mid), F32),
        mbuf=((nb, n, 2, mid), F32),
        wep=((mid, half), BF16),
        ef=((1, rows, 256), F32),
        em=((1, 2, 256), F32),
        esend=((nb, 2, half), F32),
        ebuf=((nb, n, 2, half), F32),
        epre=((nb, rows, half), BF16),
        est=((nb, 2, half), F32),
        po=((nb, crops, half), BF16),
        pp=((nb, crops, half), BF16),
        hall=((4, n // 4, nb, crops, hid), BF16),
        pall=((4, n // 4, nb, crops, half), BF16),
        qall=((4, n // 4, nb, crops, half), BF16),
        sown=((nb, rows, mid), F32),
        hm=((nb, 2, hid), F32),
        hbuf=((nb, n, 2, hid), F32),
        hst=((nb, 2, hid), F32),
        pe=((nb, crops, width), F32),
        pr=((nb, crops, width), F32),
        em2=((nb, 2, crops // 2, width), F32),
        gath=((nb, n, 2, crops // 2, width), F32),
        member=((nb, count, width), F32),
        cent=((nb, count, width), F32),
        cov=((nb * subs, width, width), F32),
        loss=((1, width), F32),
        ed=((nb, count, width), BF16),
        gemb=((hid, width), F32),
        hgf=((count, hid), F32),
        hgain=((1, hid), F32),
        hbias=((1, hid), F32),
        hd=((nb, count, hid), BF16),
        pgs=((nb, crops, half), BF16),
        pgr=((nb, crops, half), BF16),
        ghid=((2 * half, hid), BF16),
        pg=((nb, crops, half), F32),
        slo=((nb, rows, half), BF16),
        sg=((nb, rows, half), BF16),
        ebm=((nb, 2, half), F32),
        ebt=((2, half), F32),
        ebb=((nb, n, 2, half), F32),
        egain=((1, half), F32),
        ebias=((1, half), F32),
        xd=((nb, rows, half), BF16),
        mgs=((nb, rows, mid), BF16),
        mgr=((nb, rows, mid), BF16),
        mg=((nb, rows, mid), F32),
        gxs=((mid, half), BF16),
        gexp=((2 * mid, half), BF16),
        mdg=((nb, tall, mid), BF16),
        mdt=((mid, nb * long), BF16),
        mgf=((nb, rows, mid), F32),
        mbm=((nb, 2, mid), F32),
        mbb=((nb, n, 2, mid), F32),
        mgain=((1, mid), F32),
        mbias=((1, mid), F32),
        ags=((nb, rows, mid), BF16),
        agr=((nb, rows, mid), BF16),
        ag=((nb, rows, mid), F32),
        gmida=((6 * mid, mid), BF16),
        gmidb=((6 * mid, mid), BF16),
        gmidc=((6 * mid, mid), BF16),
        sgf=((nb, rows, mid), F32),
        sbm=((nb, 2, mid), F32),
        sbb=((nb, n, 2, mid), F32),
        sgain=((1, mid), F32),
        sbias=((1, mid), F32),
        sd=((nb, rows, mid), BF16),
        sdp=((nb, rows, mid), BF16),
        gss=((half, mid), BF16),
        gstem=((2 * half, mid), BF16),
        gcrops=((nb, rows, half), BF16),
    )
    pair = (2,)
    pairs = (nb, 2)
    sems = dict(
        sem_sw=pair, sem_sp=pairs, sem_ss=pairs, sem_sa=pairs, sem_ms=pairs, sem_ma=pairs,
        sem_ew=pair, sem_es=pairs, sem_ep=pairs, sem_hs=pairs, sem_he=pairs, sem_hg=pairs,
        sem_hx=pairs, sem_hh=(3, 2), sem_pa=(3, 2), sem_pq=pair, sem_hp=pair, sem_eb=pairs, sem_mg=pairs, sem_gx=pair,
        sem_mb=pairs, sem_ag=pairs, sem_sb=pairs, sem_sd=pairs, sem_gs=pair,
    )
    phases = [
        stem_forward, middle_forward, expand_forward, hidden_forward, whiten, hidden_backward,
        expand_backward, middle_backward, stem_backward, crops_backward,
    ]
    block = n == 16
    final = set(GRADS) | {"loss", "gcrops", "ghid", "gemb"}
    final |= set(NORMS)
    shared = {}
    if block:
        shared = dict(
            xd="epre", mgs="ss", ags="ss", agr="sr", mgf="mg", ag="mg", sgf="mg", sd="mo",
            sdp="mp", gcrops="sg", slo="sg", sown="mg", ghid="wh",
        )
        groups = [phases + [whole_step]]
        final -= set(GRADS) | set(NORMS) | {"ghid"}
        whole = dict(
            gexp_t=((mid, 2 * half), BF16), gmid_t=((18 * mid, mid), BF16),
            gstem_t=((2 * half, mid), BF16), ghid_t=((2 * half, hid), BF16),
            norms=((8, half), F32),
        )
        final |= set(whole)
        table.update(whole)
        for name in GRADS:
            tall, cols = table[name][0]
            table[name + "_1"] = ((2, tall // 4, cols), BF16)
            table[name + "_2"] = ((2, tall // 8, cols), BF16)
            table[name + "_3"] = ((2, 3, tall // 32, cols), BF16)
            sems["sem_" + name] = (2, 7, 2)
        for name in ("gstem_1", "gstem_2", "gstem_3"):
            (streams, *several, tall, cols), kind = table[name]
            table[name] = ((2, streams, *several, tall // 2, cols), kind)
        sems["sem_gstem"] = (2, 2, 7, 2)
        sems.update(sem_in=(4 + nb,))
        for name in ("x", "ws", "wm", "we", "wh"):
            env[name + "_in"] = env.pop(name)
            table[name] = (env[name + "_in"].shape, BF16)
    else:
        groups = [[phase] for phase in phases]

    vmem = pl.BlockSpec(memory_space=pltpu.VMEM)
    smem = pl.BlockSpec(memory_space=pltpu.SMEM)
    hbm = pl.BlockSpec(memory_space=pl.ANY)
    used = [names_of(group + [norm_slopes, norm_terms]) for group in groups]
    for number, group in enumerate(groups):
        later = final.union(*used[number + 1 :])
        here = used[number]
        reads = [name for name in env if name in here]
        made = [name for name in table if name in here and name not in env]
        sem_names = [name for name in sems if name in here]
        own = [name for name in made if name not in shared]
        bases = {shared[name] for name in made if name in shared and name in later}
        outs = [name for name in own if name in later or name in bases]
        scratch = [name for name in own if name not in outs]
        names = reads + outs + scratch + sem_names
        remote = bool(sem_names)

        def kernel(*refs, group=group, names=names, remote=remote):
            c = Ctx(n, remote, remote)
            g = types.SimpleNamespace(**dict(zip(names, refs)))
            for name, base in shared.items():
                setattr(g, name, getattr(g, base))
            if block:
                whole_step(g, c)
            else:
                group[0](g, c).alone(nb)

        params = dict(vmem_limit_bytes=63 * 2**20)
        if remote:
            params.update(collective_id=number, has_side_effects=True)
        results = pl.pallas_call(
            kernel,
            out_shape=[jax.ShapeDtypeStruct(*table[name]) for name in outs],
            in_specs=[
                smem if name == "sizes" else hbm if name[-3:] == "_in" else vmem for name in reads
            ],
            out_specs=[hbm if name[-2:] == "_t" else vmem for name in outs],
            scratch_shapes=[pltpu.VMEM(*table[name]) for name in scratch]
            + [DMA(sems[name]) for name in sem_names],
            compiler_params=pltpu.CompilerParams(**params),
            name=group[-1].__name__,
        )(*[env[name] for name in reads])
        env.update(zip(outs, results))

    for name, base in shared.items():
        if name in final:
            env[name] = env[base]
    if block:
        widths = [table[name][0][1] for name in NORMS]
        arrays = [env[name] for name in ("gcrops", "gmid_t", "ghid_t", "gexp_t", "gstem_t")]
        (env["gcrops"], gmid, ghid, gexp, gstem), rows_out = widen(arrays, env["norms"], widths)
        env.update(zip(NORMS, rows_out))
    else:
        gexp, *gmid, gstem = lax.psum([env[name] for name in GRADS], "dp")
        gexp = gexp.reshape(2, mid, half).transpose(1, 0, 2).reshape(mid, 2 * half)
        gmid = jnp.concatenate(gmid, axis=0)
        ghid = env["ghid"]
    field = env["gcrops"].astype(F32).reshape(nb, area, crops, half).transpose(0, 2, 1, 3)
    return (
        env["loss"][0, 0],
        field,
        gstem.astype(F32),
        gmid.astype(F32).reshape(9, 2 * mid, mid),
        gexp.astype(F32),
        env["sgain"][0],
        env["sbias"][0],
        env["mgain"][0],
        env["mbias"][0],
        env["egain"][0],
        env["ebias"][0],
        ghid.astype(F32),
        env["hgain"][0],
        env["hbias"][0],
        env["gemb"],
    )


def solution(mesh):
    return jax.shard_map(
        body,
        mesh=mesh,
        in_specs=(
            P(None, "dp", None, "chan"),
            P(None, "chan"),
            P(None, None, "chan"),
            P("chan", None),
            P("chan"),
            P("chan"),
            P("chan"),
            P("chan"),
            P("chan"),
            P("chan"),
            P(None, "chan"),
            P("chan"),
            P("chan"),
            P("chan", None),
            P(),
            P(),
            P(),
        ),
        out_specs=(
            P(),
            P(None, "dp", None, "chan"),
            P(None, "chan"),
            P(None, None, "chan"),
            P("chan", None),
            P("chan"),
            P("chan"),
            P("chan"),
            P("chan"),
            P("chan"),
            P("chan"),
            P(None, "chan"),
            P("chan"),
            P("chan"),
            P("chan", None),
        ),
        check_vma=False,
    )
```
